32 devices in a mesh: expert: 2 (over x), dp: 16 (over z, y, core).
Axes of the slice: x: 2, y: 2, z: 4, core: 2. Of those that a mesh axis runs over, the one named last changes fastest.
Arguments:
- tokens: bfloat16 [16, 4, 2048], P('dp', 'expert'), may hold values from -6 to 6
- out_grad: bfloat16 [16, 4, 2048], P('dp', 'expert'), may hold values from -6 to 6
- expert_ids: int32 [16, 4, 2], P('dp'), may hold values from 0 to 1, as said below
- gate_scores: bfloat16 [16, 4, 2], P('dp'), may hold values from 0.25 to 1
- w_gate: bfloat16 [2, 2048, 8192], P('expert', None, 'dp'), may hold values from -0.125 to 0.125
- w_up: bfloat16 [2, 2048, 8192], P('expert', None, 'dp'), may hold values from -0.125 to 0.125
- w_down: bfloat16 [2, 8192, 2048], P('expert', 'dp'), may hold values from -0.0625 to 0.0625
Outputs:
- token_grad: bfloat16 [16, 4, 2048], P('dp', 'expert')
- grad_gate: bfloat16 [2, 2048, 8192], P('expert', None, 'dp')
- grad_up: bfloat16 [2, 2048, 8192], P('expert', None, 'dp')
- grad_down: bfloat16 [2, 8192, 2048], P('expert', 'dp')
The draws below stay inside these ranges and needn't reach their ends.
Inputs may be any that keep to these rules, and one draw needn't show every extreme that they name: `expert_ids`: each token names two different experts; within a group no expert is named by more than 4 tokens, and in every group some expert is named by exactly 4 tokens.
All inputs are finite; a program needn't handle non-finite values.
Results may differ from the reference program's by a relative error of at most 0.0058.
Values may be sent and summed in bfloat16 or wider, within the bound.
No kernel may reach another device: no remote copies, remote signals or barrier semaphores. Data moves between devices by JAX's collectives and lax.ppermute only.
A program may use at most 64 MiB of HBM per device.

```python
import jax
import jax.numpy as jnp
from jax import lax

D = 2048
FF = 8192
EXPERTS = 2
GROUPS = 16
GROUP_TOK = 4
CAP = 4


def draw_expert_ids(key, part):
    base = jax.random.fold_in(key, 11)
    lead_key, score_key = jax.random.split(base, 2)
    leader = jax.random.randint(lead_key, (GROUPS,), 0, EXPERTS)
    noise = jax.random.randint(score_key, (GROUP_TOK, GROUPS, EXPERTS), 0, 64)
    expert_range = jnp.arange(EXPERTS, dtype=jnp.int32)

    def assign(loads, noise_row):
        score = noise_row + jnp.where(expert_range[None, :] == leader[:, None], 4096, 0)
        score = jnp.where(loads >= CAP, -100000, score)
        score = score * 16 + expert_range[None, :]
        picked = jnp.argsort(-score, axis=-1, stable=True)[:, :2].astype(jnp.int32)
        onehot = (picked[:, :, None] == expert_range[None, None, :]).astype(jnp.int32)
        return (loads + jnp.sum(onehot, axis=1), picked)
    start_loads = jnp.zeros((GROUPS, EXPERTS), jnp.int32)
    final_loads, picks = lax.scan(assign, start_loads, noise)
    return jnp.transpose(picks, (1, 0, 2))


def block_levels(key, shape, shards, smallest, largest):
    loudness = 1.0
    for position, shards_of in shards:
        steps = jax.random.uniform(jax.random.fold_in(jax.random.fold_in(key, 6), position), (shards_of,), jnp.float32, smallest / len(shards), largest / len(shards))
        loudness = loudness * jnp.repeat(jnp.exp(steps), shape[position] // shards_of).reshape((-1,) + (1,) * (len(shape) - 1 - position))
    return loudness


def bell_draw(own_key, dims, deviation, reach, shards=(), kind=jnp.bfloat16):
    array = jax.random.normal(own_key, dims, jnp.float32) * deviation
    if len(shards) > 0:
        array = block_levels(own_key, dims, shards, -0.22, 0.18) * array
    return jnp.clip(array, min=-reach, max=reach).astype(kind)


def setup_inputs(seed: int = 0) -> dict:
    seeds = jax.random.split(jax.random.key(seed), 8)
    tokens = bell_draw(seeds[0], (GROUPS, GROUP_TOK, D), 1.0, 6.0, ((0, 16), (1, 2)))
    out_grad = bell_draw(seeds[1], (GROUPS, GROUP_TOK, D), 1.0, 6.0, ((0, 16), (1, 2)))
    expert_ids = draw_expert_ids(jax.random.fold_in(seeds[7], 71), 0)
    gate_scores = jnp.clip(0.25 + 0.75 * jax.random.uniform(seeds[3], (GROUPS, GROUP_TOK, 2), jnp.float32) ** block_levels(seeds[3], (GROUPS, GROUP_TOK, 2), ((0, 16),), -0.2, 0.2), 0.25, 1.0).astype(jnp.bfloat16)
    w_gate = bell_draw(seeds[4], (EXPERTS, D, FF), D ** -0.5, 0.125, ((0, 2), (2, 16)))
    w_up = bell_draw(seeds[5], (EXPERTS, D, FF), D ** -0.5, 0.125, ((0, 2), (2, 16)))
    w_down = bell_draw(seeds[6], (EXPERTS, FF, D), FF ** -0.5, 0.0625, ((0, 2), (1, 16)))
    return dict(tokens=tokens, out_grad=out_grad, expert_ids=expert_ids, gate_scores=gate_scores, w_gate=w_gate, w_up=w_up, w_down=w_down)


def expert_pass(operands):
    input_rows, grad_rows, gate_mat, up_mat, down_mat = operands
    pre_gate = jnp.dot(input_rows, gate_mat, preferred_element_type=jnp.float32)
    pre_up = jnp.dot(input_rows, up_mat, preferred_element_type=jnp.float32)
    sigmoid_gate = jax.nn.sigmoid(pre_gate)
    activated = pre_gate * sigmoid_gate
    hidden = (activated * pre_up).astype(jnp.bfloat16)
    grad_down = jnp.dot(hidden.T, grad_rows, preferred_element_type=jnp.float32).astype(jnp.bfloat16)
    grad_hidden = jnp.dot(grad_rows, down_mat.T, preferred_element_type=jnp.float32)
    gate_delta = (grad_hidden * pre_up * sigmoid_gate * (1.0 + pre_gate * (1.0 - sigmoid_gate))).astype(jnp.bfloat16)
    up_delta = (grad_hidden * activated).astype(jnp.bfloat16)
    grad_gate = jnp.dot(input_rows.T, gate_delta, preferred_element_type=jnp.float32).astype(jnp.bfloat16)
    grad_up = jnp.dot(input_rows.T, up_delta, preferred_element_type=jnp.float32).astype(jnp.bfloat16)
    row_grad = jnp.dot(gate_delta, gate_mat.T, preferred_element_type=jnp.float32)
    row_grad = row_grad + jnp.dot(up_delta, up_mat.T, preferred_element_type=jnp.float32)
    return grad_gate, grad_up, grad_down, row_grad


def slot_table(expert_ids, experts):
    expert_range = jnp.arange(experts, dtype=jnp.int32)
    naming = jnp.sum((expert_ids[..., :, None] == expert_range).astype(jnp.int32), axis=-2).astype(jnp.int32)
    before = (jnp.cumsum(naming, axis=-2).astype(jnp.int32) - naming).astype(jnp.int32)
    return jnp.take_along_axis(before, expert_ids, axis=-1).astype(jnp.int32)


def reference(tokens, out_grad, expert_ids, gate_scores, w_gate, w_up, w_down):
    groups, group_tok, width = tokens.shape
    experts = w_gate.shape[0]
    slot_ids = slot_table(expert_ids, experts)
    expert_range = jnp.arange(experts, dtype=jnp.int32)
    slot_range = jnp.arange(CAP, dtype=jnp.int32)
    matches = (expert_ids[:, None, None, :, :] == expert_range[None, :, None, None, None]) & (slot_ids[:, None, None, :, :] == slot_range[None, None, :, None, None])
    placing = jnp.sum(matches.astype(jnp.float32), axis=-1)
    weighting = jnp.sum(matches.astype(jnp.float32) * gate_scores.astype(jnp.float32)[:, None, None, :, :], axis=-1)
    input_rows = jnp.einsum("gect,gtd->egcd", placing, tokens.astype(jnp.float32)).astype(jnp.bfloat16)
    grad_rows = jnp.einsum("gect,gtd->egcd", weighting, out_grad.astype(jnp.float32)).astype(jnp.bfloat16)
    input_rows = input_rows.reshape(experts, groups * CAP, width)
    grad_rows = grad_rows.reshape(experts, groups * CAP, width)
    grad_gate, grad_up, grad_down, row_grad = lax.map(expert_pass, (input_rows, grad_rows, w_gate, w_up, w_down))
    row_grad = row_grad.reshape(experts, groups, CAP, width)
    token_grad = jnp.einsum("gect,egcd->gtd", placing, row_grad, precision=lax.Precision.HIGHEST)
    return token_grad.astype(jnp.bfloat16), grad_gate, grad_up, grad_down
```

```python
import jax
import jax.numpy as jnp
from jax import lax
from jax.sharding import PartitionSpec as P

LANES = 128
BOTH = ("dp", "expert")


def pack(tokens, out_grad, expert_ids, gate_scores, experts, my_expert):
    tok_dev = tokens.shape[1]
    ids = lax.dynamic_slice_in_dim(expert_ids[0], my_expert * tok_dev, tok_dev, 0)
    scores = lax.dynamic_slice_in_dim(gate_scores[0], my_expert * tok_dev, tok_dev, 0)
    lane = lax.broadcasted_iota(jnp.int32, (tok_dev, LANES), 1)
    table = jnp.zeros((tok_dev, LANES), jnp.bfloat16)
    for k in range(ids.shape[1]):
        table = jnp.where(ids[:, k : k + 1] == lane, scores[:, k : k + 1], table)
    return jnp.concatenate([tokens[0], out_grad[0], table], axis=1)


def local(tokens, out_grad, expert_ids, gate_scores, w_gate, w_up, w_down):
    width = tokens.shape[2]
    tok_dev = tokens.shape[1]
    experts = lax.axis_size("expert")
    devices = experts * lax.axis_size("dp")
    my_expert = lax.axis_index("expert")
    payload = pack(tokens, out_grad, expert_ids, gate_scores, experts, my_expert)
    rows = lax.all_gather(payload, BOTH, axis=0, tiled=True)
    x = rows[:, :width]
    lane = lax.broadcasted_iota(jnp.int32, (rows.shape[0], LANES), 1)
    weight = jnp.sum(
        jnp.where(lane == my_expert, rows[:, 2 * width :].astype(jnp.float32), 0.0),
        axis=1,
        keepdims=True,
    )
    dy = (rows[:, width : 2 * width].astype(jnp.float32) * weight).astype(jnp.bfloat16)
    gate_slab, up_slab, down_slab = w_gate[0], w_up[0], w_down[0]
    pre_gate = jnp.dot(x, gate_slab, preferred_element_type=jnp.float32)
    pre_up = jnp.dot(x, up_slab, preferred_element_type=jnp.float32)
    sigmoid_gate = jax.nn.sigmoid(pre_gate)
    activated = pre_gate * sigmoid_gate
    hidden = (activated * pre_up).astype(jnp.bfloat16)
    grad_hidden = jnp.dot(dy, down_slab.T, preferred_element_type=jnp.float32)
    gate_delta = (
        grad_hidden * pre_up * sigmoid_gate * (1.0 + pre_gate * (1.0 - sigmoid_gate))
    ).astype(jnp.bfloat16)
    up_delta = (grad_hidden * activated).astype(jnp.bfloat16)
    total = jnp.dot(gate_delta, gate_slab.T, preferred_element_type=jnp.float32)
    total = total + jnp.dot(up_delta, up_slab.T, preferred_element_type=jnp.float32)
    shares = total.astype(jnp.bfloat16).reshape(devices, tok_dev, width)
    shares = lax.all_to_all(shares, BOTH, 0, 0, tiled=True)
    token_grad = jnp.sum(shares.astype(jnp.float32), axis=0)
    grad_down = jnp.dot(hidden.T, dy, preferred_element_type=jnp.float32)
    grad_gate = jnp.dot(x.T, gate_delta, preferred_element_type=jnp.float32)
    grad_up = jnp.dot(x.T, up_delta, preferred_element_type=jnp.float32)
    return tuple(g.astype(jnp.bfloat16)[None] for g in (token_grad, grad_gate, grad_up, grad_down))


def solution(mesh):
    return jax.shard_map(
        local,
        mesh=mesh,
        in_specs=(
            P("dp", "expert", None),
            P("dp", "expert", None),
            P("dp", None, None),
            P("dp", None, None),
            P("expert", None, "dp"),
            P("expert", None, "dp"),
            P("expert", "dp", None),
        ),
        out_specs=(
            P("dp", "expert", None),
            P("expert", None, "dp"),
            P("expert", None, "dp"),
            P("expert", "dp", None),
        ),
        check_vma=False,
    )
```

```python
import jax
import jax.numpy as jnp
from jax import lax
from jax.sharding import PartitionSpec as P

LANES = 128
BOTH = ("dp", "expert")


def pack(tokens, out_grad, expert_ids, gate_scores, experts, my_expert):
    tok_dev = tokens.shape[1]
    ids = lax.dynamic_slice_in_dim(expert_ids[0], my_expert * tok_dev, tok_dev, 0)
    scores = lax.dynamic_slice_in_dim(gate_scores[0], my_expert * tok_dev, tok_dev, 0)
    lane = lax.broadcasted_iota(jnp.int32, (tok_dev, LANES), 1)
    table = jnp.zeros((tok_dev, LANES), jnp.bfloat16)
    for k in range(ids.shape[1]):
        table = jnp.where(ids[:, k : k + 1] == lane, scores[:, k : k + 1], table)
    return jnp.concatenate([tokens[0], out_grad[0], table], axis=1)


def local(tokens, out_grad, expert_ids, gate_scores, w_gate, w_up, w_down):
    width = tokens.shape[2]
    tok_dev = tokens.shape[1]
    experts = lax.axis_size("expert")
    devices = experts * lax.axis_size("dp")
    my_expert = lax.axis_index("expert")
    payload = pack(tokens, out_grad, expert_ids, gate_scores, experts, my_expert)
    copies = jnp.broadcast_to(payload[None], (devices,) + payload.shape)
    rows = lax.all_to_all(copies, BOTH, 0, 0, tiled=True).reshape(devices * tok_dev, -1)
    x = rows[:, :width]
    lane = lax.broadcasted_iota(jnp.int32, (rows.shape[0], LANES), 1)
    weight = jnp.sum(
        jnp.where(lane == my_expert, rows[:, 2 * width :].astype(jnp.float32), 0.0),
        axis=1,
        keepdims=True,
    )
    dy = (rows[:, width : 2 * width].astype(jnp.float32) * weight).astype(jnp.bfloat16)
    gate_slab, up_slab, down_slab = w_gate[0], w_up[0], w_down[0]
    pre_gate = jnp.dot(x, gate_slab, preferred_element_type=jnp.float32)
    pre_up = jnp.dot(x, up_slab, preferred_element_type=jnp.float32)
    sigmoid_gate = jax.nn.sigmoid(pre_gate)
    activated = pre_gate * sigmoid_gate
    hidden = (activated * pre_up).astype(jnp.bfloat16)
    grad_hidden = jnp.dot(dy, down_slab.T, preferred_element_type=jnp.float32)
    gate_delta = (
        grad_hidden * pre_up * sigmoid_gate * (1.0 + pre_gate * (1.0 - sigmoid_gate))
    ).astype(jnp.bfloat16)
    up_delta = (grad_hidden * activated).astype(jnp.bfloat16)
    total = jnp.dot(gate_delta, gate_slab.T, preferred_element_type=jnp.float32)
    total = total + jnp.dot(up_delta, up_slab.T, preferred_element_type=jnp.float32)
    shares = total.astype(jnp.bfloat16).reshape(devices, tok_dev, width)
    shares = lax.all_to_all(shares, BOTH, 0, 0, tiled=True)
    token_grad = jnp.sum(shares.astype(jnp.float32), axis=0)
    grad_down = jnp.dot(hidden.T, dy, preferred_element_type=jnp.float32)
    grad_gate = jnp.dot(x.T, gate_delta, preferred_element_type=jnp.float32)
    grad_up = jnp.dot(x.T, up_delta, preferred_element_type=jnp.float32)
    return tuple(g.astype(jnp.bfloat16)[None] for g in (token_grad, grad_gate, grad_up, grad_down))


def solution(mesh):
    return jax.shard_map(
        local,
        mesh=mesh,
        in_specs=(
            P("dp", "expert", None),
            P("dp", "expert", None),
            P("dp", None, None),
            P("dp", None, None),
            P("expert", None, "dp"),
            P("expert", None, "dp"),
            P("expert", "dp", None),
        ),
        out_specs=(
            P("dp", "expert", None),
            P("expert", None, "dp"),
            P("expert", None, "dp"),
            P("expert", "dp", None),
        ),
        check_vma=False,
    )
```

```python
import jax
import jax.numpy as jnp
from jax import lax
from jax.sharding import PartitionSpec as P

LANES = 128
BOTH = ("expert", "dp")


def pack(tokens, out_grad, expert_ids, gate_scores, my_expert):
    tok_dev = tokens.shape[1]
    ids = lax.dynamic_slice_in_dim(expert_ids[0], my_expert * tok_dev, tok_dev, 0)
    scores = lax.dynamic_slice_in_dim(gate_scores[0], my_expert * tok_dev, tok_dev, 0)
    lane = lax.broadcasted_iota(jnp.int32, (tok_dev, LANES), 1)
    table = jnp.zeros((tok_dev, LANES), jnp.bfloat16)
    for k in range(ids.shape[1]):
        table = jnp.where(ids[:, k : k + 1] == lane, scores[:, k : k + 1], table)
    return jnp.concatenate([tokens[0], out_grad[0], table], axis=1)


class Grid:
    def __init__(self):
        dp = lax.axis_size("dp")
        ey = 1
        while (2 * ey) ** 2 <= dp // 2:
            ey *= 2
        self.sizes = (lax.axis_size("expert"), dp // 2 // ey, ey, 2)
        self.count = dp * lax.axis_size("expert")

    def coords(self, index):
        out = []
        for size in reversed(self.sizes):
            out.append(index % size)
            index = index // size
        return tuple(reversed(out))

    def index(self, coords):
        total = 0
        for size, c in zip(self.sizes, coords):
            total = total * size + c % size
        return total

    def shifted(self, index, shift):
        return self.index(tuple(c + s for c, s in zip(self.coords(index), shift)))

    def fetch(self, block, shift):
        perm = [(self.shifted(d, shift), d) for d in range(self.count)]
        return lax.ppermute(block, BOTH, perm)


def local(tokens, out_grad, expert_ids, gate_scores, w_gate, w_up, w_down):
    width = tokens.shape[2]
    tok_dev = tokens.shape[1]
    grid = Grid()
    ex, ez, ey, ec = grid.sizes
    devices = grid.count
    my_expert = lax.axis_index("expert")
    me = my_expert * lax.axis_size("dp") + lax.axis_index("dp")
    blocks = pack(tokens, out_grad, expert_ids, gate_scores, my_expert)[None]
    shifts = [(0, 0, 0, 0)]
    for phase in (
        [(0, z, 0, 0) for z in range(ez)],
        [(x, 0, y, 0) for y in range(ey) for x in range(ex)],
        [(0, 0, 0, c) for c in range(ec)],
    ):
        got = [blocks if not any(s) else grid.fetch(blocks, s) for s in phase]
        blocks = jnp.concatenate(got, axis=0)
        shifts = [tuple(a + b for a, b in zip(s, t)) for s in phase for t in shifts]
    rows = blocks.reshape(devices * tok_dev, -1)
    owners = jnp.stack([grid.shifted(me, s) for s in shifts])
    x = rows[:, :width]
    lane = lax.broadcasted_iota(jnp.int32, (rows.shape[0], LANES), 1)
    weight = jnp.sum(
        jnp.where(lane == my_expert, rows[:, 2 * width :].astype(jnp.float32), 0.0),
        axis=1,
        keepdims=True,
    )
    dy = (rows[:, width : 2 * width].astype(jnp.float32) * weight).astype(jnp.bfloat16)
    gate_slab, up_slab, down_slab = w_gate[0], w_up[0], w_down[0]
    pre_gate = jnp.dot(x, gate_slab, preferred_element_type=jnp.float32)
    pre_up = jnp.dot(x, up_slab, preferred_element_type=jnp.float32)
    sigmoid_gate = jax.nn.sigmoid(pre_gate)
    activated = pre_gate * sigmoid_gate
    hidden = (activated * pre_up).astype(jnp.bfloat16)
    grad_hidden = jnp.dot(dy, down_slab.T, preferred_element_type=jnp.float32)
    gate_delta = (
        grad_hidden * pre_up * sigmoid_gate * (1.0 + pre_gate * (1.0 - sigmoid_gate))
    ).astype(jnp.bfloat16)
    up_delta = (grad_hidden * activated).astype(jnp.bfloat16)
    place = jnp.arange(devices, dtype=jnp.int32)[:, None] == owners[None, :]
    place = jnp.repeat(jnp.repeat(place, tok_dev, axis=0), tok_dev, axis=1)
    token = jnp.arange(devices * tok_dev, dtype=jnp.int32) % tok_dev
    place = (place & (token[:, None] == token[None, :])).astype(jnp.bfloat16)
    gate_sent = jnp.dot(place, gate_delta, preferred_element_type=jnp.bfloat16)
    up_sent = jnp.dot(place, up_delta, preferred_element_type=jnp.bfloat16)
    total = jnp.dot(gate_sent, gate_slab.T, preferred_element_type=jnp.float32)
    total = total + jnp.dot(up_sent, up_slab.T, preferred_element_type=jnp.float32)
    shares = total.astype(jnp.bfloat16).reshape(devices, tok_dev, width)
    shares = lax.all_to_all(shares, BOTH, 0, 0, tiled=True)
    token_grad = jnp.sum(shares.astype(jnp.float32), axis=0)
    grad_down = jnp.dot(hidden.T, dy, preferred_element_type=jnp.float32)
    grad_gate = jnp.dot(x.T, gate_delta, preferred_element_type=jnp.float32)
    grad_up = jnp.dot(x.T, up_delta, preferred_element_type=jnp.float32)
    return tuple(g.astype(jnp.bfloat16)[None] for g in (token_grad, grad_gate, grad_up, grad_down))


def solution(mesh):
    return jax.shard_map(
        local,
        mesh=mesh,
        in_specs=(
            P("dp", "expert", None),
            P("dp", "expert", None),
            P("dp", None, None),
            P("dp", None, None),
            P("expert", None, "dp"),
            P("expert", None, "dp"),
            P("expert", "dp", None),
        ),
        out_specs=(
            P("dp", "expert", None),
            P("expert", None, "dp"),
            P("expert", None, "dp"),
            P("expert", "dp", None),
        ),
        check_vma=False,
    )
```

```python
import jax
import jax.numpy as jnp
from jax import lax
from jax.sharding import PartitionSpec as P

LANES = 128
BOTH = ("expert", "dp")
CORES = 2


def pack(tokens, out_grad, expert_ids, gate_scores, experts, my_expert):
    tok_dev = tokens.shape[1]
    ids = lax.dynamic_slice_in_dim(expert_ids[0], my_expert * tok_dev, tok_dev, 0)
    scores = lax.dynamic_slice_in_dim(gate_scores[0], my_expert * tok_dev, tok_dev, 0)
    lane = lax.broadcasted_iota(jnp.int32, (tok_dev, LANES), 1)
    table = jnp.zeros((tok_dev, LANES), jnp.bfloat16)
    for k in range(ids.shape[1]):
        table = jnp.where(ids[:, k : k + 1] == lane, scores[:, k : k + 1], table)
    return jnp.concatenate([tokens[0], out_grad[0], table], axis=1)


def local(tokens, out_grad, expert_ids, gate_scores, w_gate, w_up, w_down):
    width = tokens.shape[2]
    tok_dev = tokens.shape[1]
    experts = lax.axis_size("expert")
    devices = experts * lax.axis_size("dp")
    my_expert = lax.axis_index("expert")
    payload = pack(tokens, out_grad, expert_ids, gate_scores, experts, my_expert)
    chips = devices // CORES
    same_core = [[chip * CORES + core for chip in range(chips)] for core in range(CORES)]
    core_pairs = [(d, d ^ 1) for d in range(devices)]
    copies = jnp.broadcast_to(payload[None], (chips,) + payload.shape)
    mine = lax.all_to_all(copies, BOTH, 0, 0, axis_index_groups=same_core, tiled=True)
    rows = jnp.concatenate([mine, lax.ppermute(mine, BOTH, core_pairs)], axis=0)
    rows = rows.reshape(devices * tok_dev, -1)
    x = rows[:, :width]
    lane = lax.broadcasted_iota(jnp.int32, (rows.shape[0], LANES), 1)
    weight = jnp.sum(
        jnp.where(lane == my_expert, rows[:, 2 * width :].astype(jnp.float32), 0.0),
        axis=1,
        keepdims=True,
    )
    dy = (rows[:, width : 2 * width].astype(jnp.float32) * weight).astype(jnp.bfloat16)
    gate_slab, up_slab, down_slab = w_gate[0], w_up[0], w_down[0]
    pre_gate = jnp.dot(x, gate_slab, preferred_element_type=jnp.float32)
    pre_up = jnp.dot(x, up_slab, preferred_element_type=jnp.float32)
    sigmoid_gate = jax.nn.sigmoid(pre_gate)
    activated = pre_gate * sigmoid_gate
    hidden = (activated * pre_up).astype(jnp.bfloat16)
    grad_hidden = jnp.dot(dy, down_slab.T, preferred_element_type=jnp.float32)
    gate_delta = (
        grad_hidden * pre_up * sigmoid_gate * (1.0 + pre_gate * (1.0 - sigmoid_gate))
    ).astype(jnp.bfloat16)
    up_delta = (grad_hidden * activated).astype(jnp.bfloat16)
    total = jnp.dot(gate_delta, gate_slab.T, preferred_element_type=jnp.float32)
    total = total + jnp.dot(up_delta, up_slab.T, preferred_element_type=jnp.float32)
    half = chips * tok_dev
    other = lax.ppermute(total[half:].astype(jnp.bfloat16), BOTH, core_pairs)
    shares = (total[:half] + other.astype(jnp.float32)).astype(jnp.bfloat16)
    shares = shares.reshape(chips, tok_dev, width)
    shares = lax.all_to_all(shares, BOTH, 0, 0, axis_index_groups=same_core, tiled=True)
    token_grad = jnp.sum(shares.astype(jnp.float32), axis=0)
    grad_down = jnp.dot(hidden.T, dy, preferred_element_type=jnp.float32)
    grad_gate = jnp.dot(x.T, gate_delta, preferred_element_type=jnp.float32)
    grad_up = jnp.dot(x.T, up_delta, preferred_element_type=jnp.float32)
    return tuple(g.astype(jnp.bfloat16)[None] for g in (token_grad, grad_gate, grad_up, grad_down))


def solution(mesh):
    return jax.shard_map(
        local,
        mesh=mesh,
        in_specs=(
            P("dp", "expert", None),
            P("dp", "expert", None),
            P("dp", None, None),
            P("dp", None, None),
            P("expert", None, "dp"),
            P("expert", None, "dp"),
            P("expert", "dp", None),
        ),
        out_specs=(
            P("dp", "expert", None),
            P("expert", None, "dp"),
            P("expert", None, "dp"),
            P("expert", "dp", None),
        ),
        check_vma=False,
    )
```

```python
import functools

import jax
import jax.numpy as jnp
from jax import lax
from jax.experimental import pallas as pl
from jax.experimental.pallas import tpu as pltpu
from jax.sharding import PartitionSpec as P

LANES = 128
CORES = 2
BOTH = ("expert", "dp")
ROWS = 32
VMEM = pl.BlockSpec(memory_space=pltpu.VMEM)


def pack_kernel(tokens_ref, grad_ref, ids_ref, scores_ref, out_ref):
    chips, tok_dev, _ = out_ref.shape
    width = tokens_ref.shape[2]
    first = lax.axis_index("expert") * tok_dev
    ids = ids_ref[0]
    scores = scores_ref[0].astype(jnp.float32)
    token = lax.broadcasted_iota(jnp.int32, ids.shape, 1)
    lane = lax.broadcasted_iota(jnp.int32, (ids.shape[0], LANES), 1)
    row = lax.broadcasted_iota(jnp.int32, (tok_dev, LANES), 0)
    table = jnp.zeros((tok_dev, LANES), jnp.float32)
    for i in range(tok_dev):
        mine = token == first + i
        named = jnp.sum(jnp.where(mine, ids, 0), axis=1, keepdims=True)
        score = jnp.sum(jnp.where(mine, scores, 0.0), axis=1, keepdims=True)
        weights = jnp.sum(jnp.where(lane == named, score, 0.0), axis=0, keepdims=True)
        table = jnp.where(row == i, weights, table)
    table = table.astype(jnp.bfloat16)

    def write(chip, carry):
        out_ref[chip, :, :width] = tokens_ref[0]
        out_ref[chip, :, width : 2 * width] = grad_ref[0]
        out_ref[chip, :, 2 * width :] = table
        return carry

    lax.fori_loop(0, chips, write, 0, unroll=chips <= 16)


def pack(tokens, out_grad, expert_ids, gate_scores, chips):
    _, tok_dev, width = tokens.shape
    return pl.pallas_call(
        pack_kernel,
        out_shape=jax.ShapeDtypeStruct((chips, tok_dev, 2 * width + LANES), jnp.bfloat16),
        in_specs=[VMEM] * 4,
        out_specs=VMEM,
        compiler_params=pltpu.CompilerParams(vmem_limit_bytes=16 << 20),
    )(tokens, out_grad, jnp.swapaxes(expert_ids, 1, 2), jnp.swapaxes(gate_scores, 1, 2))


def rows_kernel(
    mine_ref, other_ref, gate_ref, up_ref, down_ref,
    shares_ref, x_ref, dy_ref, gate_delta_ref, up_delta_ref, hidden_ref,
):
    width = x_ref.shape[1]
    tok_dev = shares_ref.shape[1]
    my_expert = lax.axis_index("expert")
    my_core = lax.axis_index("dp") % CORES
    contract_last = (((1,), (1,)), ((), ()))
    devices = ROWS // tok_dev

    def step(block, carry):
        here = pl.ds(pl.multiple_of(block * ROWS, ROWS), ROWS)
        lane = lax.broadcasted_iota(jnp.int32, (ROWS, LANES), 1)
        x_parts, dy_parts = [], []
        for src in (mine_ref, other_ref):
            table = src[here, 2 * width :].astype(jnp.float32)
            weight = jnp.sum(jnp.where(lane == my_expert, table, 0.0), axis=1, keepdims=True)
            x_parts.append(src[here, :width])
            raw = src[here, width : 2 * width].astype(jnp.float32)
            dy_parts.append((raw * weight).astype(jnp.bfloat16))
        x = jnp.concatenate(x_parts, axis=0)
        dy = jnp.concatenate(dy_parts, axis=0)
        both = pl.ds(pl.multiple_of(block * 2 * ROWS, 2 * ROWS), 2 * ROWS)
        x_ref[both] = x
        dy_ref[both] = dy
        pre_gate = jnp.dot(x, gate_ref[0], preferred_element_type=jnp.float32)
        pre_up = jnp.dot(x, up_ref[0], preferred_element_type=jnp.float32)
        sigmoid_gate = jax.nn.sigmoid(pre_gate)
        activated = pre_gate * sigmoid_gate
        hidden_ref[both] = (activated * pre_up).astype(jnp.bfloat16)
        grad_hidden = lax.dot_general(
            dy, down_ref[0], contract_last, preferred_element_type=jnp.float32
        )
        gate_delta = (
            grad_hidden * pre_up * sigmoid_gate * (1.0 + pre_gate * (1.0 - sigmoid_gate))
        ).astype(jnp.bfloat16)
        up_delta = (grad_hidden * activated).astype(jnp.bfloat16)
        gate_delta_ref[both] = gate_delta
        up_delta_ref[both] = up_delta
        total = lax.dot_general(
            gate_delta, gate_ref[0], contract_last, preferred_element_type=jnp.float32
        )
        total = total + lax.dot_general(
            up_delta, up_ref[0], contract_last, preferred_element_type=jnp.float32
        )
        total = total.astype(jnp.bfloat16)
        for half, core in enumerate((my_core, 1 - my_core)):
            for j in range(devices):
                row = half * ROWS + j * tok_dev
                shares_ref[(block * devices + j) * CORES + core] = total[row : row + tok_dev]
        return carry

    blocks = mine_ref.shape[0] // ROWS
    if blocks == 1:
        step(0, 0)
    else:
        lax.fori_loop(0, blocks, step, 0)


def rows_pass(mine, other, w_gate, w_up, w_down, tok_dev):
    half, _ = mine.shape
    _, width, hidden = w_gate.shape
    rows = 2 * half
    bf16 = functools.partial(jax.ShapeDtypeStruct, dtype=jnp.bfloat16)
    weights = 3 * width * hidden * 2
    moved = weights + rows * (6 * width + 3 * hidden) * 2
    return pl.pallas_call(
        rows_kernel,
        out_shape=(
            bf16((rows // tok_dev, tok_dev, width)),
            bf16((rows, width)),
            bf16((rows, width)),
            bf16((rows, hidden)),
            bf16((rows, hidden)),
            bf16((rows, hidden)),
        ),
        in_specs=[VMEM] * 5,
        out_specs=(VMEM,) * 6,
        cost_estimate=pl.CostEstimate(
            flops=10 * rows * width * hidden, bytes_accessed=moved, transcendentals=rows * hidden
        ),
        compiler_params=pltpu.CompilerParams(vmem_limit_bytes=(12 << 20) + 2 * moved),
    )(mine, other, w_gate, w_up, w_down)


def local(tokens, out_grad, expert_ids, gate_scores, w_gate, w_up, w_down):
    tok_dev = tokens.shape[1]
    devices = lax.axis_size("expert") * lax.axis_size("dp")
    chips = devices // CORES
    same_core = [[chip * CORES + core for chip in range(chips)] for core in range(CORES)]
    core_pairs = [(d, d ^ 1) for d in range(devices)]
    copies = pack(tokens, out_grad, expert_ids, gate_scores, chips)
    mine = lax.all_to_all(copies, BOTH, 0, 0, axis_index_groups=same_core, tiled=True)
    other = lax.ppermute(mine, BOTH, core_pairs)
    half = chips * tok_dev
    shares, x, dy, gate_delta, up_delta, hidden = rows_pass(
        mine.reshape(half, -1), other.reshape(half, -1), w_gate, w_up, w_down, tok_dev
    )
    shares = lax.all_to_all(shares, BOTH, 0, 0, tiled=True)
    token_grad = jnp.sum(shares.astype(jnp.float32), axis=0)
    grad_down = jnp.dot(hidden.T, dy, preferred_element_type=jnp.float32)
    grad_gate = jnp.dot(x.T, gate_delta, preferred_element_type=jnp.float32)
    grad_up = jnp.dot(x.T, up_delta, preferred_element_type=jnp.float32)
    return tuple(g.astype(jnp.bfloat16)[None] for g in (token_grad, grad_gate, grad_up, grad_down))


def solution(mesh):
    return jax.shard_map(
        local,
        mesh=mesh,
        in_specs=(
            P("dp", "expert", None),
            P("dp", "expert", None),
            P("dp", None, None),
            P("dp", None, None),
            P("expert", None, "dp"),
            P("expert", None, "dp"),
            P("expert", "dp", None),
        ),
        out_specs=(
            P("dp", "expert", None),
            P("expert", None, "dp"),
            P("expert", None, "dp"),
            P("expert", "dp", None),
        ),
        check_vma=False,
    )
```

```python
import functools

import jax
import jax.numpy as jnp
from jax import lax
from jax.experimental import pallas as pl
from jax.experimental.pallas import tpu as pltpu
from jax.sharding import PartitionSpec as P

LANES = 128
CORES = 2
BOTH = ("expert", "dp")
ROWS = 32
PIECES = 4
VMEM = pl.BlockSpec(memory_space=pltpu.VMEM)
HBM = pl.BlockSpec(memory_space=pltpu.HBM)


def pack_kernel(
    tokens_hbm, grad_hbm, ids_hbm, scores_hbm, out_ref,
    tokens_ref, grad_ref, ids_ref, scores_ref, sems,
):
    copies = [
        pltpu.make_async_copy(src, dst, sems.at[i])
        for i, (src, dst) in enumerate((
            (ids_hbm, ids_ref),
            (scores_hbm, scores_ref),
            (tokens_hbm, tokens_ref),
            (grad_hbm, grad_ref),
        ))
    ]
    for copy in copies:
        copy.start()
    for copy in copies:
        copy.wait()
    chips, tok_dev, _ = out_ref.shape
    width = tokens_ref.shape[2]
    first = lax.axis_index("expert") * tok_dev
    ids = ids_ref[0]
    scores = scores_ref[0].astype(jnp.float32)
    token = lax.broadcasted_iota(jnp.int32, ids.shape, 1)
    lane = lax.broadcasted_iota(jnp.int32, (ids.shape[0], LANES), 1)
    row = lax.broadcasted_iota(jnp.int32, (tok_dev, LANES), 0)
    table = jnp.zeros((tok_dev, LANES), jnp.float32)
    for i in range(tok_dev):
        mine = token == first + i
        named = jnp.sum(jnp.where(mine, ids, 0), axis=1, keepdims=True)
        score = jnp.sum(jnp.where(mine, scores, 0.0), axis=1, keepdims=True)
        weights = jnp.sum(jnp.where(lane == named, score, 0.0), axis=0, keepdims=True)
        table = jnp.where(row == i, weights, table)
    table = table.astype(jnp.bfloat16)

    def write(chip, carry):
        out_ref[chip, :, :width] = tokens_ref[0]
        out_ref[chip, :, width : 2 * width] = grad_ref[0]
        out_ref[chip, :, 2 * width :] = table
        return carry

    lax.fori_loop(0, chips, write, 0, unroll=chips <= 16)


def pack(tokens, out_grad, expert_ids, gate_scores, chips):
    _, tok_dev, width = tokens.shape
    operands = [
        pltpu.with_memory_space_constraint(a, pltpu.HBM)
        for a in (
            tokens, out_grad, jnp.swapaxes(expert_ids, 1, 2), jnp.swapaxes(gate_scores, 1, 2)
        )
    ]
    return pl.pallas_call(
        pack_kernel,
        out_shape=jax.ShapeDtypeStruct((chips, tok_dev, 2 * width + LANES), jnp.bfloat16),
        in_specs=[HBM] * 4,
        out_specs=VMEM,
        scratch_shapes=[pltpu.VMEM(a.shape, a.dtype) for a in operands]
        + [pltpu.SemaphoreType.DMA((4,))],
        compiler_params=pltpu.CompilerParams(vmem_limit_bytes=16 << 20),
    )(*operands)


def fetch_kernel(gate_hbm, up_hbm, down_hbm, gate_ref, up_ref, down_ref, sems):
    copies = []
    for i, (src, dst) in enumerate(
        ((gate_hbm, gate_ref), (up_hbm, up_ref), (down_hbm, down_ref))
    ):
        rows = src.shape[1] // PIECES
        for piece in range(PIECES):
            part = pl.ds(piece * rows, rows)
            copies.append(
                pltpu.make_async_copy(src.at[0, part], dst.at[part], sems.at[i, piece])
            )
    for copy in copies:
        copy.start()
    for copy in copies:
        copy.wait()


def fetch(*weights):
    moved = sum(w.size * 2 for w in weights)
    weights = [pltpu.with_memory_space_constraint(w, pltpu.HBM) for w in weights]
    return pl.pallas_call(
        fetch_kernel,
        out_shape=tuple(pltpu.VMEM(w.shape[1:], w.dtype) for w in weights),
        in_specs=[HBM] * 3,
        out_specs=(VMEM,) * 3,
        scratch_shapes=[pltpu.SemaphoreType.DMA((3, PIECES))],
        cost_estimate=pl.CostEstimate(flops=0, bytes_accessed=2 * moved, transcendentals=0),
        compiler_params=pltpu.CompilerParams(vmem_limit_bytes=16 << 20),
    )(*weights)


def rows_kernel(
    mine_ref, other_ref, gate_ref, up_ref, down_ref,
    shares_ref, x_ref, dy_ref, gate_delta_ref, up_delta_ref, hidden_ref,
):
    width = x_ref.shape[1]
    tok_dev = shares_ref.shape[1]
    my_expert = lax.axis_index("expert")
    my_core = lax.axis_index("dp") % CORES
    contract_last = (((1,), (1,)), ((), ()))
    devices = ROWS // tok_dev

    def step(block, carry):
        here = pl.ds(pl.multiple_of(block * ROWS, ROWS), ROWS)
        lane = lax.broadcasted_iota(jnp.int32, (ROWS, LANES), 1)
        x_parts, dy_parts = [], []
        for src in (mine_ref, other_ref):
            table = src[here, 2 * width :].astype(jnp.float32)
            weight = jnp.sum(jnp.where(lane == my_expert, table, 0.0), axis=1, keepdims=True)
            x_parts.append(src[here, :width])
            raw = src[here, width : 2 * width].astype(jnp.float32)
            dy_parts.append((raw * weight).astype(jnp.bfloat16))
        x = jnp.concatenate(x_parts, axis=0)
        dy = jnp.concatenate(dy_parts, axis=0)
        both = pl.ds(pl.multiple_of(block * 2 * ROWS, 2 * ROWS), 2 * ROWS)
        x_ref[both] = x
        dy_ref[both] = dy
        pre_gate = jnp.dot(x, gate_ref[...], preferred_element_type=jnp.float32)
        pre_up = jnp.dot(x, up_ref[...], preferred_element_type=jnp.float32)
        sigmoid_gate = jax.nn.sigmoid(pre_gate)
        activated = pre_gate * sigmoid_gate
        hidden_ref[both] = (activated * pre_up).astype(jnp.bfloat16)
        grad_hidden = lax.dot_general(
            dy, down_ref[...], contract_last, preferred_element_type=jnp.float32
        )
        gate_delta = (
            grad_hidden * pre_up * sigmoid_gate * (1.0 + pre_gate * (1.0 - sigmoid_gate))
        ).astype(jnp.bfloat16)
        up_delta = (grad_hidden * activated).astype(jnp.bfloat16)
        gate_delta_ref[both] = gate_delta
        up_delta_ref[both] = up_delta
        total = lax.dot_general(
            gate_delta, gate_ref[...], contract_last, preferred_element_type=jnp.float32
        )
        total = total + lax.dot_general(
            up_delta, up_ref[...], contract_last, preferred_element_type=jnp.float32
        )
        total = total.astype(jnp.bfloat16)
        for half, core in enumerate((my_core, 1 - my_core)):
            for j in range(devices):
                row = half * ROWS + j * tok_dev
                shares_ref[(block * devices + j) * CORES + core] = total[row : row + tok_dev]
        return carry

    blocks = mine_ref.shape[0] // ROWS
    if blocks == 1:
        step(0, 0)
    else:
        lax.fori_loop(0, blocks, step, 0)


def rows_pass(mine, other, w_gate, w_up, w_down, tok_dev):
    half, _ = mine.shape
    width, hidden = w_gate.shape
    rows = 2 * half
    bf16 = functools.partial(jax.ShapeDtypeStruct, dtype=jnp.bfloat16)
    weights = 3 * width * hidden * 2
    moved = weights + rows * (6 * width + 3 * hidden) * 2
    return pl.pallas_call(
        rows_kernel,
        out_shape=(
            bf16((rows // tok_dev, tok_dev, width)),
            bf16((rows, width)),
            bf16((rows, width)),
            bf16((rows, hidden)),
            bf16((rows, hidden)),
            bf16((rows, hidden)),
        ),
        in_specs=[VMEM] * 5,
        out_specs=(VMEM,) * 6,
        cost_estimate=pl.CostEstimate(
            flops=10 * rows * width * hidden, bytes_accessed=moved, transcendentals=rows * hidden
        ),
        compiler_params=pltpu.CompilerParams(vmem_limit_bytes=(12 << 20) + 2 * moved),
    )(mine, other, w_gate, w_up, w_down)


def local(tokens, out_grad, expert_ids, gate_scores, w_gate, w_up, w_down):
    tok_dev = tokens.shape[1]
    devices = lax.axis_size("expert") * lax.axis_size("dp")
    chips = devices // CORES
    same_core = [[chip * CORES + core for chip in range(chips)] for core in range(CORES)]
    core_pairs = [(d, d ^ 1) for d in range(devices)]
    slabs = fetch(w_gate, w_up, w_down)
    copies = pack(tokens, out_grad, expert_ids, gate_scores, chips)
    mine = lax.all_to_all(copies, BOTH, 0, 0, axis_index_groups=same_core, tiled=True)
    other = lax.ppermute(mine, BOTH, core_pairs)
    half = chips * tok_dev
    shares, x, dy, gate_delta, up_delta, hidden = rows_pass(
        mine.reshape(half, -1), other.reshape(half, -1), *slabs, tok_dev
    )
    shares = lax.all_to_all(shares, BOTH, 0, 0, tiled=True)
    token_grad = jnp.sum(shares.astype(jnp.float32), axis=0)
    grad_down = jnp.dot(hidden.T, dy, preferred_element_type=jnp.float32)
    grad_gate = jnp.dot(x.T, gate_delta, preferred_element_type=jnp.float32)
    grad_up = jnp.dot(x.T, up_delta, preferred_element_type=jnp.float32)
    return tuple(g.astype(jnp.bfloat16)[None] for g in (token_grad, grad_gate, grad_up, grad_down))


def solution(mesh):
    return jax.shard_map(
        local,
        mesh=mesh,
        in_specs=(
            P("dp", "expert", None),
            P("dp", "expert", None),
            P("dp", None, None),
            P("dp", None, None),
            P("expert", None, "dp"),
            P("expert", None, "dp"),
            P("expert", "dp", None),
        ),
        out_specs=(
            P("dp", "expert", None),
            P("expert", None, "dp"),
            P("expert", None, "dp"),
            P("expert", "dp", None),
        ),
        check_vma=False,
    )
```

```python
import functools

import jax
import jax.numpy as jnp
from jax import lax
from jax.experimental import pallas as pl
from jax.experimental.pallas import tpu as pltpu
from jax.sharding import PartitionSpec as P

LANES = 128
CORES = 2
BOTH = ("expert", "dp")
ROWS = 64
TILE = 16
PIECES = 4
VMEM = pl.BlockSpec(memory_space=pltpu.VMEM)
HBM = pl.BlockSpec(memory_space=pltpu.HBM)


def pack_kernel(
    tokens_hbm, grad_hbm, ids_hbm, scores_hbm, out_ref,
    tokens_ref, grad_ref, ids_ref, scores_ref, sems,
):
    copies = [
        pltpu.make_async_copy(src, dst, sems.at[i])
        for i, (src, dst) in enumerate((
            (ids_hbm, ids_ref),
            (scores_hbm, scores_ref),
            (tokens_hbm, tokens_ref),
            (grad_hbm, grad_ref),
        ))
    ]
    for copy in copies:
        copy.start()
    for copy in copies:
        copy.wait()
    chips, tok_dev, _ = out_ref.shape
    width = tokens_ref.shape[2]
    first = lax.axis_index("expert") * tok_dev
    ids = ids_ref[0]
    scores = scores_ref[0].astype(jnp.float32)
    token = lax.broadcasted_iota(jnp.int32, ids.shape, 1)
    lane = lax.broadcasted_iota(jnp.int32, (ids.shape[0], LANES), 1)
    row = lax.broadcasted_iota(jnp.int32, (tok_dev, LANES), 0)
    table = jnp.zeros((tok_dev, LANES), jnp.float32)
    for i in range(tok_dev):
        mine = token == first + i
        named = jnp.sum(jnp.where(mine, ids, 0), axis=1, keepdims=True)
        score = jnp.sum(jnp.where(mine, scores, 0.0), axis=1, keepdims=True)
        weights = jnp.sum(jnp.where(lane == named, score, 0.0), axis=0, keepdims=True)
        table = jnp.where(row == i, weights, table)
    table = table.astype(jnp.bfloat16)

    def write(chip, carry):
        out_ref[chip, :, :width] = tokens_ref[0]
        out_ref[chip, :, width : 2 * width] = grad_ref[0]
        out_ref[chip, :, 2 * width :] = table
        return carry

    lax.fori_loop(0, chips, write, 0, unroll=chips <= 16)


def pack(tokens, out_grad, expert_ids, gate_scores, chips):
    _, tok_dev, width = tokens.shape
    operands = [
        pltpu.with_memory_space_constraint(a, pltpu.HBM)
        for a in (
            tokens, out_grad, jnp.swapaxes(expert_ids, 1, 2), jnp.swapaxes(gate_scores, 1, 2)
        )
    ]
    return pl.pallas_call(
        pack_kernel,
        out_shape=jax.ShapeDtypeStruct((chips, tok_dev, 2 * width + LANES), jnp.bfloat16),
        in_specs=[HBM] * 4,
        out_specs=VMEM,
        scratch_shapes=[pltpu.VMEM(a.shape, a.dtype) for a in operands]
        + [pltpu.SemaphoreType.DMA((4,))],
        compiler_params=pltpu.CompilerParams(vmem_limit_bytes=16 << 20),
    )(*operands)


def copy_pieces(src, dst, sems):
    rows = dst.shape[0] // PIECES
    parts = [pl.ds(piece * rows, rows) for piece in range(PIECES)]
    copies = [
        pltpu.make_async_copy(src.at[0, part], dst.at[part], sems.at[piece])
        for piece, part in enumerate(parts)
    ]
    for copy in copies:
        copy.start()
    return copies


def lay_out(src_ref, x_ref, dy_ref, table_ref, first):
    chips, tok_dev, _ = src_ref.shape
    width = x_ref.shape[1]
    my_expert = lax.axis_index("expert")
    lane = lax.broadcasted_iota(jnp.int32, (TILE, LANES), 1)
    per_tile = TILE // tok_dev

    def step(tile, carry):
        rows = pl.ds(pl.multiple_of(first + tile * TILE, TILE), TILE)
        for j in range(per_tile):
            part = slice(j * tok_dev, (j + 1) * tok_dev)
            chip = tile * per_tile + j
            table_ref[part] = src_ref[chip, :, 2 * width :]
        table = table_ref[...].astype(jnp.float32)
        weight = jnp.sum(jnp.where(lane == my_expert, table, 0.0), axis=1, keepdims=True)
        blocks = [src_ref[tile * per_tile + j] for j in range(per_tile)]
        x_ref[rows] = jnp.concatenate([b[:, :width] for b in blocks], axis=0)
        raw = jnp.concatenate([b[:, width : 2 * width] for b in blocks], axis=0)
        dy_ref[rows] = (raw.astype(jnp.float32) * weight).astype(jnp.bfloat16)
        return carry

    tiles = chips // per_tile
    lax.fori_loop(0, tiles, step, 0, unroll=tiles <= 2)


def fetch_kernel(
    mine_ref, gate_hbm, up_hbm, gate_ref, up_ref, x_ref, dy_ref, table_ref, sems
):
    copies = copy_pieces(gate_hbm, gate_ref, sems.at[0])
    copies += copy_pieces(up_hbm, up_ref, sems.at[1])
    lay_out(mine_ref, x_ref, dy_ref, table_ref, 0)
    for copy in copies:
        copy.wait()


def fetch(mine, w_gate, w_up):
    chips, tok_dev, row = mine.shape
    _, width, hidden = w_gate.shape
    half = chips * tok_dev
    moved = 2 * 2 * width * hidden
    gate, up = (pltpu.with_memory_space_constraint(w, pltpu.HBM) for w in (w_gate, w_up))
    return pl.pallas_call(
        fetch_kernel,
        out_shape=(
            pltpu.VMEM((width, hidden), jnp.bfloat16),
            pltpu.VMEM((width, hidden), jnp.bfloat16),
            pltpu.VMEM((half, width), jnp.bfloat16),
            pltpu.VMEM((half, width), jnp.bfloat16),
        ),
        in_specs=[VMEM, HBM, HBM],
        out_specs=(VMEM,) * 4,
        scratch_shapes=[
            pltpu.VMEM((TILE, LANES), jnp.bfloat16),
            pltpu.SemaphoreType.DMA((2, PIECES)),
        ],
        cost_estimate=pl.CostEstimate(flops=0, bytes_accessed=2 * moved, transcendentals=0),
        compiler_params=pltpu.CompilerParams(
            vmem_limit_bytes=(8 << 20) + 2 * moved + 8 * half * row
        ),
    )(mine, gate, up)


def rows_kernel(
    other_ref, my_x_ref, my_dy_ref, gate_ref, up_ref, down_hbm,
    shares_ref, x_ref, dy_ref, gate_delta_ref, up_delta_ref, hidden_ref,
    down_ref, table_ref, sems,
):
    copies = copy_pieces(down_hbm, down_ref, sems)
    tok_dev = shares_ref.shape[1]
    half = my_x_ref.shape[0]
    my_core = lax.axis_index("dp") % CORES
    contract_last = (((1,), (1,)), ((), ()))
    devices = ROWS // tok_dev
    x_ref[:half] = my_x_ref[...]
    dy_ref[:half] = my_dy_ref[...]
    lay_out(other_ref, x_ref, dy_ref, table_ref, half)

    def step(block, copies):
        rows = pl.ds(pl.multiple_of(block * ROWS, ROWS), ROWS)
        x = x_ref[rows]
        pre_gate = jnp.dot(x, gate_ref[...], preferred_element_type=jnp.float32)
        pre_up = jnp.dot(x, up_ref[...], preferred_element_type=jnp.float32)
        sigmoid_gate = jax.nn.sigmoid(pre_gate)
        activated = pre_gate * sigmoid_gate
        hidden_ref[rows] = (activated * pre_up).astype(jnp.bfloat16)
        for copy in copies:
            copy.wait()
        grad_hidden = lax.dot_general(
            dy_ref[rows], down_ref[...], contract_last, preferred_element_type=jnp.float32
        )
        gate_delta = (
            grad_hidden * pre_up * sigmoid_gate * (1.0 + pre_gate * (1.0 - sigmoid_gate))
        ).astype(jnp.bfloat16)
        up_delta = (grad_hidden * activated).astype(jnp.bfloat16)
        gate_delta_ref[rows] = gate_delta
        up_delta_ref[rows] = up_delta
        total = lax.dot_general(
            gate_delta, gate_ref[...], contract_last, preferred_element_type=jnp.float32
        )
        total = total + lax.dot_general(
            up_delta, up_ref[...], contract_last, preferred_element_type=jnp.float32
        )
        total = total.astype(jnp.bfloat16)
        for j in range(devices):
            place = block * devices + j
            chip = place % (half // tok_dev)
            core = jnp.where(place < half // tok_dev, my_core, 1 - my_core)
            shares_ref[chip * CORES + core] = total[j * tok_dev : (j + 1) * tok_dev]

    step(0, copies)
    blocks = x_ref.shape[0] // ROWS
    if blocks > 1:
        pl.loop(1, blocks)(lambda block: step(block, []))


def rows_pass(other, my_x, my_dy, gate, up, w_down):
    chips, tok_dev, row = other.shape
    width, hidden = gate.shape
    rows = 2 * chips * tok_dev
    bf16 = functools.partial(jax.ShapeDtypeStruct, dtype=jnp.bfloat16)
    moved = (3 * width * hidden + rows * (6 * width + 3 * hidden)) * 2
    return pl.pallas_call(
        rows_kernel,
        out_shape=(
            bf16((rows // tok_dev, tok_dev, width)),
            bf16((rows, width)),
            bf16((rows, width)),
            bf16((rows, hidden)),
            bf16((rows, hidden)),
            bf16((rows, hidden)),
        ),
        in_specs=[VMEM] * 5 + [HBM],
        out_specs=(VMEM,) * 6,
        scratch_shapes=[
            pltpu.VMEM((hidden, width), jnp.bfloat16),
            pltpu.VMEM((TILE, LANES), jnp.bfloat16),
            pltpu.SemaphoreType.DMA((PIECES,)),
        ],
        cost_estimate=pl.CostEstimate(
            flops=10 * rows * width * hidden, bytes_accessed=moved, transcendentals=rows * hidden
        ),
        compiler_params=pltpu.CompilerParams(vmem_limit_bytes=(12 << 20) + 2 * moved),
    )(other, my_x, my_dy, gate, up, pltpu.with_memory_space_constraint(w_down, pltpu.HBM))


def local(tokens, out_grad, expert_ids, gate_scores, w_gate, w_up, w_down):
    devices = lax.axis_size("expert") * lax.axis_size("dp")
    chips = devices // CORES
    same_core = [[chip * CORES + core for chip in range(chips)] for core in range(CORES)]
    core_pairs = [(d, d ^ 1) for d in range(devices)]
    copies = pack(tokens, out_grad, expert_ids, gate_scores, chips)
    mine = lax.all_to_all(copies, BOTH, 0, 0, axis_index_groups=same_core, tiled=True)
    other = lax.ppermute(mine, BOTH, core_pairs)
    gate, up, my_x, my_dy = fetch(mine, w_gate, w_up)
    shares, x, dy, gate_delta, up_delta, hidden = rows_pass(
        other, my_x, my_dy, gate, up, w_down
    )
    shares = lax.all_to_all(shares, BOTH, 0, 0, tiled=True)
    token_grad = jnp.sum(shares.astype(jnp.float32), axis=0)
    grad_down = jnp.dot(hidden.T, dy, preferred_element_type=jnp.float32)
    grad_gate = jnp.dot(x.T, gate_delta, preferred_element_type=jnp.float32)
    grad_up = jnp.dot(x.T, up_delta, preferred_element_type=jnp.float32)
    return tuple(g.astype(jnp.bfloat16)[None] for g in (token_grad, grad_gate, grad_up, grad_down))


def solution(mesh):
    return jax.shard_map(
        local,
        mesh=mesh,
        in_specs=(
            P("dp", "expert", None),
            P("dp", "expert", None),
            P("dp", None, None),
            P("dp", None, None),
            P("expert", None, "dp"),
            P("expert", None, "dp"),
            P("expert", "dp", None),
        ),
        out_specs=(
            P("dp", "expert", None),
            P("expert", None, "dp"),
            P("expert", None, "dp"),
            P("expert", "dp", None),
        ),
        check_vma=False,
    )
```

```python
import functools

import jax
import jax.numpy as jnp
from jax import lax
from jax.experimental import pallas as pl
from jax.experimental.pallas import tpu as pltpu
from jax.sharding import PartitionSpec as P

LANES = 128
CORES = 2
BOTH = ("expert", "dp")
ROWS = 64
TILE = 16
PIECES = 4
VMEM = pl.BlockSpec(memory_space=pltpu.VMEM)
HBM = pl.BlockSpec(memory_space=pltpu.HBM)


def pack_kernel(
    tokens_hbm, grad_hbm, ids_hbm, scores_hbm, out_ref,
    tokens_ref, grad_ref, ids_ref, scores_ref, sems,
):
    copies = [
        pltpu.make_async_copy(src, dst, sems.at[i])
        for i, (src, dst) in enumerate((
            (ids_hbm, ids_ref),
            (scores_hbm, scores_ref),
            (tokens_hbm, tokens_ref),
            (grad_hbm, grad_ref),
        ))
    ]
    for copy in copies:
        copy.start()
    for copy in copies:
        copy.wait()
    chips, tok_dev, _ = out_ref.shape
    width = tokens_ref.shape[2]
    first = lax.axis_index("expert") * tok_dev
    ids = ids_ref[0]
    scores = scores_ref[0].astype(jnp.float32)
    token = lax.broadcasted_iota(jnp.int32, ids.shape, 1)
    lane = lax.broadcasted_iota(jnp.int32, (ids.shape[0], LANES), 1)
    row = lax.broadcasted_iota(jnp.int32, (tok_dev, LANES), 0)
    table = jnp.zeros((tok_dev, LANES), jnp.float32)
    for i in range(tok_dev):
        mine = token == first + i
        named = jnp.sum(jnp.where(mine, ids, 0), axis=1, keepdims=True)
        score = jnp.sum(jnp.where(mine, scores, 0.0), axis=1, keepdims=True)
        weights = jnp.sum(jnp.where(lane == named, score, 0.0), axis=0, keepdims=True)
        table = jnp.where(row == i, weights, table)
    table = table.astype(jnp.bfloat16)

    def write(chip, carry):
        out_ref[chip, :, :width] = tokens_ref[0]
        out_ref[chip, :, width : 2 * width] = grad_ref[0]
        out_ref[chip, :, 2 * width :] = table
        return carry

    lax.fori_loop(0, chips, write, 0, unroll=chips <= 16)


def pack(tokens, out_grad, expert_ids, gate_scores, chips):
    _, tok_dev, width = tokens.shape
    operands = [
        pltpu.with_memory_space_constraint(a, pltpu.HBM)
        for a in (
            tokens, out_grad, jnp.swapaxes(expert_ids, 1, 2), jnp.swapaxes(gate_scores, 1, 2)
        )
    ]
    return pl.pallas_call(
        pack_kernel,
        out_shape=jax.ShapeDtypeStruct((chips, tok_dev, 2 * width + LANES), jnp.bfloat16),
        in_specs=[HBM] * 4,
        out_specs=VMEM,
        scratch_shapes=[pltpu.VMEM(a.shape, a.dtype) for a in operands]
        + [pltpu.SemaphoreType.DMA((4,))],
        compiler_params=pltpu.CompilerParams(vmem_limit_bytes=16 << 20),
    )(*operands)


def copy_pieces(src, dst, sems):
    rows = dst.shape[0] // PIECES
    parts = [pl.ds(piece * rows, rows) for piece in range(PIECES)]
    copies = [
        pltpu.make_async_copy(src.at[0, part], dst.at[part], sems.at[piece])
        for piece, part in enumerate(parts)
    ]
    for copy in copies:
        copy.start()
    return copies


def lay_out(src_ref, x_ref, dy_ref, table_ref, first):
    chips, tok_dev, _ = src_ref.shape
    width = x_ref.shape[1]
    my_expert = lax.axis_index("expert")
    lane = lax.broadcasted_iota(jnp.int32, (TILE, LANES), 1)
    per_tile = TILE // tok_dev

    def step(tile, carry):
        rows = pl.ds(pl.multiple_of(first + tile * TILE, TILE), TILE)
        for j in range(per_tile):
            part = slice(j * tok_dev, (j + 1) * tok_dev)
            chip = tile * per_tile + j
            table_ref[part] = src_ref[chip, :, 2 * width :]
        table = table_ref[...].astype(jnp.float32)
        weight = jnp.sum(jnp.where(lane == my_expert, table, 0.0), axis=1, keepdims=True)
        blocks = [src_ref[tile * per_tile + j] for j in range(per_tile)]
        x_ref[rows] = jnp.concatenate([b[:, :width] for b in blocks], axis=0)
        raw = jnp.concatenate([b[:, width : 2 * width] for b in blocks], axis=0)
        dy_ref[rows] = (raw.astype(jnp.float32) * weight).astype(jnp.bfloat16)
        return carry

    tiles = chips // per_tile
    lax.fori_loop(0, tiles, step, 0, unroll=tiles <= 2)


def fetch_kernel(
    mine_ref, gate_hbm, up_hbm, gate_ref, up_ref, x_ref, dy_ref, table_ref, sems
):
    copies = copy_pieces(gate_hbm, gate_ref, sems.at[0])
    copies += copy_pieces(up_hbm, up_ref, sems.at[1])
    lay_out(mine_ref, x_ref, dy_ref, table_ref, 0)
    for copy in copies:
        copy.wait()


def fetch(mine, w_gate, w_up):
    chips, tok_dev, row = mine.shape
    _, width, hidden = w_gate.shape
    half = chips * tok_dev
    moved = 2 * 2 * width * hidden
    gate, up = (pltpu.with_memory_space_constraint(w, pltpu.HBM) for w in (w_gate, w_up))
    return pl.pallas_call(
        fetch_kernel,
        out_shape=(
            pltpu.VMEM((width, hidden), jnp.bfloat16),
            pltpu.VMEM((width, hidden), jnp.bfloat16),
            pltpu.VMEM((half, width), jnp.bfloat16),
            pltpu.VMEM((half, width), jnp.bfloat16),
        ),
        in_specs=[VMEM, HBM, HBM],
        out_specs=(VMEM,) * 4,
        scratch_shapes=[
            pltpu.VMEM((TILE, LANES), jnp.bfloat16),
            pltpu.SemaphoreType.DMA((2, PIECES)),
        ],
        cost_estimate=pl.CostEstimate(flops=0, bytes_accessed=2 * moved, transcendentals=0),
        compiler_params=pltpu.CompilerParams(
            vmem_limit_bytes=(8 << 20) + 2 * moved + 8 * half * row
        ),
    )(mine, gate, up)


def rows_kernel(
    other_ref, my_x_ref, my_dy_ref, gate_ref, up_ref, down_hbm,
    shares_ref, x_ref, dy_ref, gate_delta_ref, up_delta_ref, hidden_ref,
    down_ref, table_ref, sems,
):
    copies = copy_pieces(down_hbm, down_ref, sems)
    tok_dev = shares_ref.shape[1]
    half = my_x_ref.shape[0]
    my_core = lax.axis_index("dp") % CORES
    contract_last = (((1,), (1,)), ((), ()))
    devices = ROWS // tok_dev
    x_ref[:half] = my_x_ref[...]
    dy_ref[:half] = my_dy_ref[...]
    lay_out(other_ref, x_ref, dy_ref, table_ref, half)

    def step(block, copies):
        rows = pl.ds(pl.multiple_of(block * ROWS, ROWS), ROWS)
        x = x_ref[rows]
        pre_gate = jnp.dot(x, gate_ref[...], preferred_element_type=jnp.float32)
        pre_up = jnp.dot(x, up_ref[...], preferred_element_type=jnp.float32)
        sigmoid_gate = jax.nn.sigmoid(pre_gate)
        activated = pre_gate * sigmoid_gate
        hidden_ref[rows] = (activated * pre_up).astype(jnp.bfloat16)
        for copy in copies:
            copy.wait()
        grad_hidden = lax.dot_general(
            dy_ref[rows], down_ref[...], contract_last, preferred_element_type=jnp.float32
        )
        gate_delta = (
            grad_hidden * pre_up * sigmoid_gate * (1.0 + pre_gate * (1.0 - sigmoid_gate))
        ).astype(jnp.bfloat16)
        up_delta = (grad_hidden * activated).astype(jnp.bfloat16)
        gate_delta_ref[rows] = gate_delta
        up_delta_ref[rows] = up_delta
        total = lax.dot_general(
            gate_delta, gate_ref[...], contract_last, preferred_element_type=jnp.float32
        )
        total = total + lax.dot_general(
            up_delta, up_ref[...], contract_last, preferred_element_type=jnp.float32
        )
        total = total.astype(jnp.bfloat16)
        for j in range(devices):
            place = block * devices + j
            chip = place % (half // tok_dev)
            core = jnp.where(place < half // tok_dev, my_core, 1 - my_core)
            shares_ref[chip * CORES + core] = total[j * tok_dev : (j + 1) * tok_dev]

    step(0, copies)
    blocks = x_ref.shape[0] // ROWS
    if blocks > 1:
        pl.loop(1, blocks)(lambda block: step(block, []))


def rows_pass(other, my_x, my_dy, gate, up, w_down):
    chips, tok_dev, row = other.shape
    width, hidden = gate.shape
    rows = 2 * chips * tok_dev
    bf16 = functools.partial(jax.ShapeDtypeStruct, dtype=jnp.bfloat16)
    moved = (3 * width * hidden + rows * (6 * width + 3 * hidden)) * 2
    return pl.pallas_call(
        rows_kernel,
        out_shape=(
            bf16((rows // tok_dev, tok_dev, width)),
            bf16((rows, width)),
            bf16((rows, width)),
            bf16((rows, hidden)),
            bf16((rows, hidden)),
            bf16((rows, hidden)),
        ),
        in_specs=[VMEM] * 5 + [HBM],
        out_specs=(VMEM,) * 6,
        scratch_shapes=[
            pltpu.VMEM((hidden, width), jnp.bfloat16),
            pltpu.VMEM((TILE, LANES), jnp.bfloat16),
            pltpu.SemaphoreType.DMA((PIECES,)),
        ],
        cost_estimate=pl.CostEstimate(
            flops=10 * rows * width * hidden, bytes_accessed=moved, transcendentals=rows * hidden
        ),
        compiler_params=pltpu.CompilerParams(vmem_limit_bytes=(12 << 20) + 2 * moved),
    )(other, my_x, my_dy, gate, up, pltpu.with_memory_space_constraint(w_down, pltpu.HBM))


def local(tokens, out_grad, expert_ids, gate_scores, w_gate, w_up, w_down):
    devices = lax.axis_size("expert") * lax.axis_size("dp")
    chips = devices // CORES
    middle = lax.axis_size("dp") // CORES // 2
    order = [(chip + middle) % chips for chip in range(chips)]
    same_core = [[chip * CORES + core for chip in order] for core in range(CORES)]
    everyone = [[chip * CORES + core for chip in order for core in range(CORES)]]
    core_pairs = [(d, d ^ 1) for d in range(devices)]
    copies = pack(tokens, out_grad, expert_ids, gate_scores, chips)
    mine = lax.all_to_all(copies, BOTH, 0, 0, axis_index_groups=same_core, tiled=True)
    other = lax.ppermute(mine, BOTH, core_pairs)
    gate, up, my_x, my_dy = fetch(mine, w_gate, w_up)
    shares, x, dy, gate_delta, up_delta, hidden = rows_pass(
        other, my_x, my_dy, gate, up, w_down
    )
    shares = lax.all_to_all(shares, BOTH, 0, 0, axis_index_groups=everyone, tiled=True)
    token_grad = jnp.sum(shares.astype(jnp.float32), axis=0)
    grad_down = jnp.dot(hidden.T, dy, preferred_element_type=jnp.float32)
    grad_gate = jnp.dot(x.T, gate_delta, preferred_element_type=jnp.float32)
    grad_up = jnp.dot(x.T, up_delta, preferred_element_type=jnp.float32)
    return tuple(g.astype(jnp.bfloat16)[None] for g in (token_grad, grad_gate, grad_up, grad_down))


def solution(mesh):
    return jax.shard_map(
        local,
        mesh=mesh,
        in_specs=(
            P("dp", "expert", None),
            P("dp", "expert", None),
            P("dp", None, None),
            P("dp", None, None),
            P("expert", None, "dp"),
            P("expert", None, "dp"),
            P("expert", "dp", None),
        ),
        out_specs=(
            P("dp", "expert", None),
            P("expert", None, "dp"),
            P("expert", None, "dp"),
            P("expert", "dp", None),
        ),
        check_vma=False,
    )
```

```python
import functools

import jax
import jax.numpy as jnp
from jax import lax
from jax.experimental import pallas as pl
from jax.experimental.pallas import tpu as pltpu
from jax.sharding import PartitionSpec as P

LANES = 128
CORES = 2
BOTH = ("expert", "dp")
ROWS = 64
TILE = 16
CONTRACT_LAST = (((1,), (1,)), ((), ()))
PIECES = 4
VMEM = pl.BlockSpec(memory_space=pltpu.VMEM)
HBM = pl.BlockSpec(memory_space=pltpu.HBM)


def vmem(size):
    return pltpu.CompilerParams(vmem_limit_bytes=min(size, 36 << 20))


def pack_kernel(
    tokens_hbm, grad_hbm, ids_hbm, scores_hbm, out_ref,
    tokens_ref, grad_ref, ids_ref, scores_ref, sems,
):
    copies = [
        pltpu.make_async_copy(src, dst, sems.at[i])
        for i, (src, dst) in enumerate((
            (ids_hbm, ids_ref),
            (scores_hbm, scores_ref),
            (tokens_hbm, tokens_ref),
            (grad_hbm, grad_ref),
        ))
    ]
    for copy in copies:
        copy.start()
    for copy in copies:
        copy.wait()
    chips, tok_dev, _ = out_ref.shape
    width = tokens_ref.shape[2]
    first = lax.axis_index("expert") * tok_dev
    ids = ids_ref[0]
    scores = scores_ref[0].astype(jnp.float32)
    token = lax.broadcasted_iota(jnp.int32, ids.shape, 1)
    lane = lax.broadcasted_iota(jnp.int32, (ids.shape[0], LANES), 1)
    row = lax.broadcasted_iota(jnp.int32, (tok_dev, LANES), 0)
    table = jnp.zeros((tok_dev, LANES), jnp.float32)
    for i in range(tok_dev):
        mine = token == first + i
        named = jnp.sum(jnp.where(mine, ids, 0), axis=1, keepdims=True)
        score = jnp.sum(jnp.where(mine, scores, 0.0), axis=1, keepdims=True)
        weights = jnp.sum(jnp.where(lane == named, score, 0.0), axis=0, keepdims=True)
        table = jnp.where(row == i, weights, table)
    table = table.astype(jnp.bfloat16)

    def write(chip, carry):
        out_ref[chip, :, :width] = tokens_ref[0]
        out_ref[chip, :, width : 2 * width] = grad_ref[0]
        out_ref[chip, :, 2 * width :] = table
        return carry

    lax.fori_loop(0, chips, write, 0, unroll=chips <= 16)


def pack(tokens, out_grad, expert_ids, gate_scores, chips):
    _, tok_dev, width = tokens.shape
    operands = [
        pltpu.with_memory_space_constraint(a, pltpu.HBM)
        for a in (
            tokens, out_grad, jnp.swapaxes(expert_ids, 1, 2), jnp.swapaxes(gate_scores, 1, 2)
        )
    ]
    return pl.pallas_call(
        pack_kernel,
        out_shape=jax.ShapeDtypeStruct((chips, tok_dev, 2 * width + LANES), jnp.bfloat16),
        in_specs=[HBM] * 4,
        out_specs=VMEM,
        scratch_shapes=[pltpu.VMEM(a.shape, a.dtype) for a in operands]
        + [pltpu.SemaphoreType.DMA((4,))],
        compiler_params=vmem(16 << 20),
    )(*operands)


def copy_pieces(src, dst, sems):
    rows = dst.shape[0] // PIECES
    parts = [pl.ds(piece * rows, rows) for piece in range(PIECES)]
    copies = [
        pltpu.make_async_copy(src.at[0, part], dst.at[part], sems.at[piece])
        for piece, part in enumerate(parts)
    ]
    for copy in copies:
        copy.start()
    return copies


def lay_out(src_ref, x_ref, dy_ref, table_ref, first):
    chips, tok_dev, _ = src_ref.shape
    width = x_ref.shape[1]
    my_expert = lax.axis_index("expert")
    lane = lax.broadcasted_iota(jnp.int32, (TILE, LANES), 1)
    per_tile = TILE // tok_dev

    def step(tile, carry):
        rows = pl.ds(pl.multiple_of(first + tile * TILE, TILE), TILE)
        for j in range(per_tile):
            part = slice(j * tok_dev, (j + 1) * tok_dev)
            chip = tile * per_tile + j
            table_ref[part] = src_ref[chip, :, 2 * width :]
        table = table_ref[...].astype(jnp.float32)
        weight = jnp.sum(jnp.where(lane == my_expert, table, 0.0), axis=1, keepdims=True)
        blocks = [src_ref[tile * per_tile + j] for j in range(per_tile)]
        x_ref[rows] = jnp.concatenate([b[:, :width] for b in blocks], axis=0)
        raw = jnp.concatenate([b[:, width : 2 * width] for b in blocks], axis=0)
        dy_ref[rows] = (raw.astype(jnp.float32) * weight).astype(jnp.bfloat16)
        return carry

    tiles = chips // per_tile
    lax.fori_loop(0, tiles, step, 0, unroll=tiles <= 2)


def fetch_kernel(mine_ref, gate_hbm, gate_ref, x_ref, dy_ref, table_ref, sems):
    copies = copy_pieces(gate_hbm, gate_ref, sems)
    lay_out(mine_ref, x_ref, dy_ref, table_ref, 0)
    for copy in copies:
        copy.wait()


def fetch(mine, w_gate):
    chips, tok_dev, row = mine.shape
    _, width, hidden = w_gate.shape
    half = chips * tok_dev
    moved = 2 * width * hidden
    return pl.pallas_call(
        fetch_kernel,
        out_shape=(
            pltpu.VMEM((width, hidden), jnp.bfloat16),
            pltpu.VMEM((half, width), jnp.bfloat16),
            pltpu.VMEM((half, width), jnp.bfloat16),
        ),
        in_specs=[VMEM, HBM],
        out_specs=(VMEM,) * 3,
        scratch_shapes=[
            pltpu.VMEM((TILE, LANES), jnp.bfloat16),
            pltpu.SemaphoreType.DMA((PIECES,)),
        ],
        cost_estimate=pl.CostEstimate(flops=0, bytes_accessed=2 * moved, transcendentals=0),
        compiler_params=vmem((8 << 20) + 2 * moved + 8 * half * row),
    )(mine, pltpu.with_memory_space_constraint(w_gate, pltpu.HBM))


def my_core():
    return lax.axis_index("dp") % CORES


def row_blocks(rows, step):
    step(0, True)
    if rows > ROWS:
        pl.loop(1, rows // ROWS)(lambda block: step(block, False))


def half_total(gate_delta, up_delta, gate_ref, up_ref, core):
    columns = gate_ref.shape[0] // CORES
    part = pl.ds(pl.multiple_of(core * columns, columns), columns)
    total = lax.dot_general(
        gate_delta, gate_ref[part], CONTRACT_LAST, preferred_element_type=jnp.float32
    )
    return total + lax.dot_general(
        up_delta, up_ref[part], CONTRACT_LAST, preferred_element_type=jnp.float32
    )


def rows_kernel(
    other_ref, my_x_ref, my_dy_ref, gate_ref, up_hbm, down_hbm,
    sent_ref, up_ref, x_ref, dy_ref, gate_delta_ref, up_delta_ref, hidden_ref,
    down_ref, table_ref, sems,
):
    up_copies = copy_pieces(up_hbm, up_ref, sems.at[0])
    down_copies = copy_pieces(down_hbm, down_ref, sems.at[1])
    half = my_x_ref.shape[0]
    x_ref[:half] = my_x_ref[...]
    dy_ref[:half] = my_dy_ref[...]
    lay_out(other_ref, x_ref, dy_ref, table_ref, half)
    depth = up_ref.shape[0] // PIECES

    def step(block, first):
        rows = pl.ds(pl.multiple_of(block * ROWS, ROWS), ROWS)
        x = x_ref[rows]
        pre_gate = jnp.dot(x, gate_ref[...], preferred_element_type=jnp.float32)
        sigmoid_gate = jax.nn.sigmoid(pre_gate)
        activated = pre_gate * sigmoid_gate
        pre_up = None
        for piece, copy in enumerate(up_copies):
            if first:
                copy.wait()
            part = slice(piece * depth, (piece + 1) * depth)
            product = jnp.dot(x[:, part], up_ref[part], preferred_element_type=jnp.float32)
            pre_up = product if pre_up is None else pre_up + product
        hidden_ref[rows] = (activated * pre_up).astype(jnp.bfloat16)
        if first:
            for copy in down_copies:
                copy.wait()
        grad_hidden = lax.dot_general(
            dy_ref[rows], down_ref[...], CONTRACT_LAST, preferred_element_type=jnp.float32
        )
        gate_delta = (
            grad_hidden * pre_up * sigmoid_gate * (1.0 + pre_gate * (1.0 - sigmoid_gate))
        ).astype(jnp.bfloat16)
        up_delta = (grad_hidden * activated).astype(jnp.bfloat16)
        gate_delta_ref[rows] = gate_delta
        up_delta_ref[rows] = up_delta
        sent_ref[rows] = half_total(
            gate_delta, up_delta, gate_ref, up_ref, 1 - my_core()
        ).astype(jnp.bfloat16)

    row_blocks(x_ref.shape[0], step)


def rows_pass(other, my_x, my_dy, gate, w_up, w_down):
    chips, tok_dev, row = other.shape
    width, hidden = gate.shape
    rows = 2 * chips * tok_dev
    bf16 = functools.partial(jax.ShapeDtypeStruct, dtype=jnp.bfloat16)
    moved = (3 * width * hidden + rows * (6 * width + 3 * hidden)) * 2
    up, down = (pltpu.with_memory_space_constraint(w, pltpu.HBM) for w in (w_up, w_down))
    return pl.pallas_call(
        rows_kernel,
        out_shape=(
            bf16((rows, width // CORES)),
            pltpu.VMEM((width, hidden), jnp.bfloat16),
            bf16((rows, width)),
            bf16((rows, width)),
            bf16((rows, hidden)),
            bf16((rows, hidden)),
            bf16((rows, hidden)),
        ),
        in_specs=[VMEM] * 4 + [HBM] * 2,
        out_specs=(VMEM,) * 7,
        scratch_shapes=[
            pltpu.VMEM((hidden, width), jnp.bfloat16),
            pltpu.VMEM((TILE, LANES), jnp.bfloat16),
            pltpu.SemaphoreType.DMA((2, PIECES)),
        ],
        cost_estimate=pl.CostEstimate(
            flops=8 * rows * width * hidden, bytes_accessed=moved, transcendentals=rows * hidden
        ),
        compiler_params=vmem((12 << 20) + 2 * moved),
    )(other, my_x, my_dy, gate, up, down)


def finish_kernel(gate_delta_ref, up_delta_ref, gate_ref, up_ref, total_ref):
    def step(block, first):
        rows = pl.ds(pl.multiple_of(block * ROWS, ROWS), ROWS)
        total_ref[rows] = half_total(
            gate_delta_ref[rows], up_delta_ref[rows], gate_ref, up_ref, my_core()
        )

    row_blocks(total_ref.shape[0], step)


def finish(gate_delta, up_delta, gate, up):
    rows, hidden = gate_delta.shape
    columns = gate.shape[0] // CORES
    moved = 4 * columns * hidden + 4 * rows * (columns + hidden)
    return pl.pallas_call(
        finish_kernel,
        out_shape=jax.ShapeDtypeStruct((rows, columns), jnp.float32),
        in_specs=[VMEM] * 4,
        out_specs=VMEM,
        cost_estimate=pl.CostEstimate(
            flops=4 * rows * columns * hidden, bytes_accessed=moved, transcendentals=0
        ),
        compiler_params=vmem((16 << 20) + 2 * moved),
    )(gate_delta, up_delta, gate, up)


def share_kernel(total_ref, got_ref, shares_ref):
    devices, tok_dev, _ = shares_ref.shape
    chips = devices // CORES
    per_tile = TILE // tok_dev
    tiles = devices // per_tile
    core = my_core()

    def step(tile, carry):
        rows = pl.ds(pl.multiple_of(tile * TILE, TILE), TILE)
        there = pl.ds(pl.multiple_of((tile + tiles // 2) % tiles * TILE, TILE), TILE)
        total = (total_ref[rows] + got_ref[there].astype(jnp.float32)).astype(jnp.bfloat16)
        for j in range(per_tile):
            place = tile * per_tile + j
            owner = jnp.where(place < chips, core, 1 - core)
            shares_ref[(place % chips) * CORES + owner] = total[j * tok_dev : (j + 1) * tok_dev]
        return carry

    lax.fori_loop(0, tiles, step, 0, unroll=tiles <= 4)


def share(total, got, tok_dev):
    rows, columns = total.shape
    return pl.pallas_call(
        share_kernel,
        out_shape=jax.ShapeDtypeStruct((rows // tok_dev, tok_dev, columns), jnp.bfloat16),
        in_specs=[VMEM] * 2,
        out_specs=VMEM,
        compiler_params=vmem((8 << 20) + 32 * rows * columns),
    )(total, got)


def sum_kernel(shares_ref, out_hbm, out_ref, sem):
    devices, tok_dev, columns = shares_ref.shape
    for core in range(CORES):
        zero = jnp.zeros((tok_dev, columns), jnp.float32)
        total = lax.fori_loop(
            0,
            devices // CORES,
            lambda i, acc: acc + shares_ref[i * CORES + core].astype(jnp.float32),
            zero,
            unroll=devices <= 32,
        )
        out_ref[0, :, core * columns : (core + 1) * columns] = total.astype(jnp.bfloat16)
    copy = pltpu.make_async_copy(out_ref, out_hbm, sem)
    copy.start()
    copy.wait()


def sum_shares(shares):
    devices, tok_dev, columns = shares.shape
    out = (1, tok_dev, CORES * columns)
    return pl.pallas_call(
        sum_kernel,
        out_shape=pltpu.HBM(out, jnp.bfloat16),
        in_specs=[VMEM],
        out_specs=HBM,
        scratch_shapes=[pltpu.VMEM(out, jnp.bfloat16), pltpu.SemaphoreType.DMA],
        compiler_params=vmem(16 << 20),
    )(shares)


def local(tokens, out_grad, expert_ids, gate_scores, w_gate, w_up, w_down):
    devices = lax.axis_size("expert") * lax.axis_size("dp")
    chips = devices // CORES
    middle = lax.axis_size("dp") // CORES // 2
    order = [(chip + middle) % chips for chip in range(chips)]
    same_core = [[chip * CORES + core for chip in order] for core in range(CORES)]
    everyone = [[chip * CORES + core for chip in order for core in range(CORES)]]
    core_pairs = [(d, d ^ 1) for d in range(devices)]
    copies = pack(tokens, out_grad, expert_ids, gate_scores, chips)
    mine = lax.all_to_all(copies, BOTH, 0, 0, axis_index_groups=same_core, tiled=True)
    other = lax.ppermute(mine, BOTH, core_pairs)
    gate, my_x, my_dy = fetch(mine, w_gate)
    sent, up, x, dy, gate_delta, up_delta, hidden = rows_pass(
        other, my_x, my_dy, gate, w_up, w_down
    )
    got = lax.ppermute(sent, BOTH, core_pairs)
    total = finish(gate_delta, up_delta, gate, up)
    shares = share(total, got, tokens.shape[1])
    shares = lax.all_to_all(shares, BOTH, 0, 0, axis_index_groups=everyone, tiled=True)
    token_grad = sum_shares(shares)
    grad_down = jnp.dot(hidden.T, dy, preferred_element_type=jnp.float32)
    grad_gate = jnp.dot(x.T, gate_delta, preferred_element_type=jnp.float32)
    grad_up = jnp.dot(x.T, up_delta, preferred_element_type=jnp.float32)
    weight_grads = (grad_gate, grad_up, grad_down)
    return (token_grad,) + tuple(g.astype(jnp.bfloat16)[None] for g in weight_grads)


def solution(mesh):
    return jax.shard_map(
        local,
        mesh=mesh,
        in_specs=(
            P("dp", "expert", None),
            P("dp", "expert", None),
            P("dp", None, None),
            P("dp", None, None),
            P("expert", None, "dp"),
            P("expert", None, "dp"),
            P("expert", "dp", None),
        ),
        out_specs=(
            P("dp", "expert", None),
            P("expert", None, "dp"),
            P("expert", None, "dp"),
            P("expert", "dp", None),
        ),
        check_vma=False,
    )
```

```python
import functools

import jax
import jax.numpy as jnp
from jax import lax
from jax.experimental import pallas as pl
from jax.experimental.pallas import tpu as pltpu
from jax.sharding import PartitionSpec as P

LANES = 128
CORES = 2
BOTH = ("expert", "dp")
ROWS = 64
TILE = 16
CONTRACT_LAST = (((1,), (1,)), ((), ()))
PIECES = 4
VMEM = pl.BlockSpec(memory_space=pltpu.VMEM)
HBM = pl.BlockSpec(memory_space=pltpu.HBM)


def vmem(size):
    return pltpu.CompilerParams(vmem_limit_bytes=min(size, 36 << 20))


def chip_at(place):
    per_expert = lax.axis_size("dp") // CORES
    return (place + per_expert // 2) % (per_expert * lax.axis_size("expert"))


def pack_kernel(
    tokens_hbm, grad_hbm, ids_hbm, scores_hbm, out_ref,
    tokens_ref, grad_ref, ids_ref, scores_ref, weighted_ref, sems,
):
    copies = [
        pltpu.make_async_copy(src, dst, sems.at[i])
        for i, (src, dst) in enumerate((
            (ids_hbm, ids_ref),
            (scores_hbm, scores_ref),
            (tokens_hbm, tokens_ref),
            (grad_hbm, grad_ref),
        ))
    ]
    for copy in copies:
        copy.start()
    for copy in copies:
        copy.wait()
    chips, tok_dev, _ = out_ref.shape
    width = tokens_ref.shape[2]
    experts = lax.axis_size("expert")
    first = lax.axis_index("expert") * tok_dev
    ids = ids_ref[0]
    scores = scores_ref[0].astype(jnp.float32)
    token = lax.broadcasted_iota(jnp.int32, ids.shape, 1)
    lane = lax.broadcasted_iota(jnp.int32, (ids.shape[0], LANES), 1)
    row = lax.broadcasted_iota(jnp.int32, (tok_dev, LANES), 0)
    table = jnp.zeros((tok_dev, LANES), jnp.float32)
    for i in range(tok_dev):
        mine = token == first + i
        named = jnp.sum(jnp.where(mine, ids, 0), axis=1, keepdims=True)
        score = jnp.sum(jnp.where(mine, scores, 0.0), axis=1, keepdims=True)
        weights = jnp.sum(jnp.where(lane == named, score, 0.0), axis=0, keepdims=True)
        table = jnp.where(row == i, weights, table)
    grad = grad_ref[0].astype(jnp.float32)
    for expert in range(experts):
        weighted_ref[expert] = (grad * table[:, expert : expert + 1]).astype(jnp.bfloat16)

    def write(place, carry):
        out_ref[place, :, :width] = tokens_ref[0]
        out_ref[place, :, width:] = weighted_ref[chip_at(place) // (chips // experts)]
        return carry

    lax.fori_loop(0, chips, write, 0, unroll=chips <= 16)


def pack(tokens, out_grad, expert_ids, gate_scores, chips):
    _, tok_dev, width = tokens.shape
    operands = [
        pltpu.with_memory_space_constraint(a, pltpu.HBM)
        for a in (
            tokens, out_grad, jnp.swapaxes(expert_ids, 1, 2), jnp.swapaxes(gate_scores, 1, 2)
        )
    ]
    return pl.pallas_call(
        pack_kernel,
        out_shape=jax.ShapeDtypeStruct((chips, tok_dev, 2 * width), jnp.bfloat16),
        in_specs=[HBM] * 4,
        out_specs=VMEM,
        scratch_shapes=[pltpu.VMEM(a.shape, a.dtype) for a in operands]
        + [
            pltpu.VMEM((lax.axis_size("expert"), tok_dev, width), jnp.bfloat16),
            pltpu.SemaphoreType.DMA((4,)),
        ],
        compiler_params=vmem(16 << 20),
    )(*operands)


def copy_pieces(src, dst, sems):
    rows = dst.shape[0] // PIECES
    parts = [pl.ds(piece * rows, rows) for piece in range(PIECES)]
    copies = [
        pltpu.make_async_copy(src.at[0, part], dst.at[part], sems.at[piece])
        for piece, part in enumerate(parts)
    ]
    for copy in copies:
        copy.start()
    return copies


def lay_out(src_ref, x_ref, dy_ref, first):
    chips, tok_dev, _ = src_ref.shape
    width = x_ref.shape[1]
    per_tile = TILE // tok_dev

    def step(tile, carry):
        rows = pl.ds(pl.multiple_of(first + tile * TILE, TILE), TILE)
        blocks = [src_ref[tile * per_tile + j] for j in range(per_tile)]
        x_ref[rows] = jnp.concatenate([b[:, :width] for b in blocks], axis=0)
        dy_ref[rows] = jnp.concatenate([b[:, width:] for b in blocks], axis=0)
        return carry

    tiles = chips // per_tile
    lax.fori_loop(0, tiles, step, 0, unroll=tiles <= 2)


def fetch_kernel(mine_ref, gate_hbm, gate_ref, x_ref, dy_ref, sems):
    copies = copy_pieces(gate_hbm, gate_ref, sems)
    lay_out(mine_ref, x_ref, dy_ref, 0)
    for copy in copies:
        copy.wait()


def fetch(mine, w_gate):
    chips, tok_dev, row = mine.shape
    _, width, hidden = w_gate.shape
    half = chips * tok_dev
    moved = 2 * width * hidden
    return pl.pallas_call(
        fetch_kernel,
        out_shape=(
            pltpu.VMEM((width, hidden), jnp.bfloat16),
            pltpu.VMEM((half, width), jnp.bfloat16),
            pltpu.VMEM((half, width), jnp.bfloat16),
        ),
        in_specs=[VMEM, HBM],
        out_specs=(VMEM,) * 3,
        scratch_shapes=[pltpu.SemaphoreType.DMA((PIECES,))],
        cost_estimate=pl.CostEstimate(flops=0, bytes_accessed=2 * moved, transcendentals=0),
        compiler_params=vmem((8 << 20) + 2 * moved + 8 * half * row),
    )(mine, pltpu.with_memory_space_constraint(w_gate, pltpu.HBM))


def my_core():
    return lax.axis_index("dp") % CORES


def row_blocks(rows, step):
    step(0, True)
    if rows > ROWS:
        pl.loop(1, rows // ROWS)(lambda block: step(block, False))


def half_total(gate_delta, up_delta, gate_ref, up_ref, core):
    columns = gate_ref.shape[0] // CORES
    part = pl.ds(pl.multiple_of(core * columns, columns), columns)
    total = lax.dot_general(
        gate_delta, gate_ref[part], CONTRACT_LAST, preferred_element_type=jnp.float32
    )
    return total + lax.dot_general(
        up_delta, up_ref[part], CONTRACT_LAST, preferred_element_type=jnp.float32
    )


def store_groups(ref, first, total):
    rows, columns = total.shape
    groups = columns // LANES
    for c in range(groups):
        ref[pl.ds(first + c, rows, stride=groups)] = total[:, c * LANES : (c + 1) * LANES]


def rows_kernel(
    other_ref, my_x_ref, my_dy_ref, gate_ref, up_hbm, down_hbm,
    sent_ref, up_ref, x_ref, dy_ref, gate_delta_ref, up_delta_ref, hidden_ref,
    down_ref, total_ref, sems,
):
    up_copies = copy_pieces(up_hbm, up_ref, sems.at[0])
    down_copies = copy_pieces(down_hbm, down_ref, sems.at[1])
    half = my_x_ref.shape[0]
    x_ref[:half] = my_x_ref[...]
    dy_ref[:half] = my_dy_ref[...]
    lay_out(other_ref, x_ref, dy_ref, half)
    depth = up_ref.shape[0] // PIECES

    def step(block, first):
        rows = pl.ds(pl.multiple_of(block * ROWS, ROWS), ROWS)
        x = x_ref[rows]
        pre_gate = jnp.dot(x, gate_ref[...], preferred_element_type=jnp.float32)
        sigmoid_gate = jax.nn.sigmoid(pre_gate)
        activated = pre_gate * sigmoid_gate
        pre_up = None
        for piece, copy in enumerate(up_copies):
            if first:
                copy.wait()
            part = slice(piece * depth, (piece + 1) * depth)
            product = jnp.dot(x[:, part], up_ref[part], preferred_element_type=jnp.float32)
            pre_up = product if pre_up is None else pre_up + product
        hidden_ref[rows] = (activated * pre_up).astype(jnp.bfloat16)
        if first:
            for copy in down_copies:
                copy.wait()
        grad_hidden = lax.dot_general(
            dy_ref[rows], down_ref[...], CONTRACT_LAST, preferred_element_type=jnp.float32
        )
        gate_delta = (
            grad_hidden * pre_up * sigmoid_gate * (1.0 + pre_gate * (1.0 - sigmoid_gate))
        ).astype(jnp.bfloat16)
        up_delta = (grad_hidden * activated).astype(jnp.bfloat16)
        gate_delta_ref[rows] = gate_delta
        up_delta_ref[rows] = up_delta
        total = half_total(gate_delta, up_delta, gate_ref, up_ref, 1 - my_core())
        store_groups(total_ref, 0, total)
        size = total_ref.shape[0]
        part = pl.ds(pl.multiple_of(block * size, size), size)
        sent_ref[part] = total_ref[...].astype(jnp.bfloat16)

    row_blocks(x_ref.shape[0], step)


def rows_pass(other, my_x, my_dy, gate, w_up, w_down):
    chips, tok_dev, row = other.shape
    width, hidden = gate.shape
    rows = 2 * chips * tok_dev
    groups = width // CORES // LANES
    bf16 = functools.partial(jax.ShapeDtypeStruct, dtype=jnp.bfloat16)
    moved = (3 * width * hidden + rows * (6 * width + 3 * hidden)) * 2
    up, down = (pltpu.with_memory_space_constraint(w, pltpu.HBM) for w in (w_up, w_down))
    return pl.pallas_call(
        rows_kernel,
        out_shape=(
            bf16((rows * groups, LANES)),
            pltpu.VMEM((width, hidden), jnp.bfloat16),
            bf16((rows, width)),
            bf16((rows, width)),
            bf16((rows, hidden)),
            bf16((rows, hidden)),
            bf16((rows, hidden)),
        ),
        in_specs=[VMEM] * 4 + [HBM] * 2,
        out_specs=(VMEM,) * 7,
        scratch_shapes=[
            pltpu.VMEM((hidden, width), jnp.bfloat16),
            pltpu.VMEM((ROWS * groups, LANES), jnp.float32),
            pltpu.SemaphoreType.DMA((2, PIECES)),
        ],
        cost_estimate=pl.CostEstimate(
            flops=8 * rows * width * hidden, bytes_accessed=moved, transcendentals=rows * hidden
        ),
        compiler_params=vmem((12 << 20) + 2 * moved),
    )(other, my_x, my_dy, gate, up, down)


def finish_kernel(gate_delta_ref, up_delta_ref, gate_ref, up_ref, total_ref):
    rows_all = gate_delta_ref.shape[0]
    size = total_ref.shape[0] // rows_all * ROWS

    def step(block, first):
        rows = pl.ds(pl.multiple_of(block * ROWS, ROWS), ROWS)
        total = half_total(
            gate_delta_ref[rows], up_delta_ref[rows], gate_ref, up_ref, my_core()
        )
        store_groups(total_ref, block * size, total)

    row_blocks(rows_all, step)


def finish(gate_delta, up_delta, gate, up):
    rows, hidden = gate_delta.shape
    columns = gate.shape[0] // CORES
    moved = 4 * columns * hidden + 4 * rows * (columns + hidden)
    return pl.pallas_call(
        finish_kernel,
        out_shape=jax.ShapeDtypeStruct((rows * columns // LANES, LANES), jnp.float32),
        in_specs=[VMEM] * 4,
        out_specs=VMEM,
        cost_estimate=pl.CostEstimate(
            flops=4 * rows * columns * hidden, bytes_accessed=moved, transcendentals=0
        ),
        compiler_params=vmem((16 << 20) + 2 * moved),
    )(gate_delta, up_delta, gate, up)


def share_kernel(total_ref, got_ref, shares_ref):
    devices, size, _ = shares_ref.shape
    chips = devices // CORES
    core = my_core()

    def step(place, carry):
        here = pl.ds(pl.multiple_of(place * size, size), size)
        there = pl.ds(pl.multiple_of((place + chips) % devices * size, size), size)
        owner = jnp.where(place < chips, core, 1 - core)
        total = total_ref[here] + got_ref[there].astype(jnp.float32)
        shares_ref[place % chips * CORES + owner] = total.astype(jnp.bfloat16)
        return carry

    lax.fori_loop(0, devices, step, 0, unroll=devices <= 32)


def share(total, got, devices):
    size = total.shape[0] // devices
    return pl.pallas_call(
        share_kernel,
        out_shape=jax.ShapeDtypeStruct((devices, size, LANES), jnp.bfloat16),
        in_specs=[VMEM] * 2,
        out_specs=VMEM,
        compiler_params=vmem((8 << 20) + 32 * total.size),
    )(total, got)


def sum_kernel(shares_ref, out_hbm, wide_ref, out_ref, sem):
    devices, size, _ = shares_ref.shape
    _, tok_dev, width = out_ref.shape
    groups = size // tok_dev
    for core in range(CORES):
        total = lax.fori_loop(
            0,
            devices // CORES,
            lambda i, acc: acc + shares_ref[i * CORES + core].astype(jnp.float32),
            jnp.zeros((size, LANES), jnp.float32),
            unroll=devices <= 32,
        )
        for row in range(size):
            token, lane = row // groups, (core * groups + row % groups) * LANES
            wide_ref[token : token + 1, lane : lane + LANES] = total[row : row + 1]
    out_ref[0] = wide_ref[...].astype(jnp.bfloat16)
    copy = pltpu.make_async_copy(out_ref, out_hbm, sem)
    copy.start()
    copy.wait()


def sum_shares(shares, tok_dev):
    _, size, _ = shares.shape
    width = CORES * size // tok_dev * LANES
    return pl.pallas_call(
        sum_kernel,
        out_shape=pltpu.HBM((1, tok_dev, width), jnp.bfloat16),
        in_specs=[VMEM],
        out_specs=HBM,
        scratch_shapes=[
            pltpu.VMEM((tok_dev, width), jnp.float32),
            pltpu.VMEM((1, tok_dev, width), jnp.bfloat16),
            pltpu.SemaphoreType.DMA,
        ],
        compiler_params=vmem(16 << 20),
    )(shares)


def local(tokens, out_grad, expert_ids, gate_scores, w_gate, w_up, w_down):
    devices = lax.axis_size("expert") * lax.axis_size("dp")
    chips = devices // CORES
    order = [chip_at(place) for place in range(chips)]
    same_core = [[chip * CORES + core for chip in order] for core in range(CORES)]
    everyone = [[chip * CORES + core for chip in order for core in range(CORES)]]
    core_pairs = [(d, d ^ 1) for d in range(devices)]
    copies = pack(tokens, out_grad, expert_ids, gate_scores, chips)
    mine = lax.all_to_all(copies, BOTH, 0, 0, axis_index_groups=same_core, tiled=True)
    other = lax.ppermute(mine, BOTH, core_pairs)
    gate, my_x, my_dy = fetch(mine, w_gate)
    sent, up, x, dy, gate_delta, up_delta, hidden = rows_pass(
        other, my_x, my_dy, gate, w_up, w_down
    )
    got = lax.ppermute(sent, BOTH, core_pairs)
    total = finish(gate_delta, up_delta, gate, up)
    shares = share(total, got, devices)
    shares, gate_delta, up_delta, hidden = lax.optimization_barrier(
        (shares, gate_delta, up_delta, hidden)
    )
    shares = lax.all_to_all(shares, BOTH, 0, 0, axis_index_groups=everyone, tiled=True)
    token_grad = sum_shares(shares, tokens.shape[1])
    grad_down = jnp.dot(hidden.T, dy, preferred_element_type=jnp.float32)
    grad_gate = jnp.dot(x.T, gate_delta, preferred_element_type=jnp.float32)
    grad_up = jnp.dot(x.T, up_delta, preferred_element_type=jnp.float32)
    weight_grads = (grad_gate, grad_up, grad_down)
    return (token_grad,) + tuple(g.astype(jnp.bfloat16)[None] for g in weight_grads)


def solution(mesh):
    return jax.shard_map(
        local,
        mesh=mesh,
        in_specs=(
            P("dp", "expert", None),
            P("dp", "expert", None),
            P("dp", None, None),
            P("dp", None, None),
            P("expert", None, "dp"),
            P("expert", None, "dp"),
            P("expert", "dp", None),
        ),
        out_specs=(
            P("dp", "expert", None),
            P("expert", None, "dp"),
            P("expert", None, "dp"),
            P("expert", "dp", None),
        ),
        check_vma=False,
    )
```

```python
import functools

import jax
import jax.numpy as jnp
from jax import lax
from jax.experimental import pallas as pl
from jax.experimental.pallas import tpu as pltpu
from jax.sharding import PartitionSpec as P

LANES = 128
CORES = 2
BOTH = ("expert", "dp")
ROWS = 64
TILE = 16
CONTRACT_LAST = (((1,), (1,)), ((), ()))
PIECES = 4
VMEM = pl.BlockSpec(memory_space=pltpu.VMEM)
HBM = pl.BlockSpec(memory_space=pltpu.HBM)


def vmem(size):
    return pltpu.CompilerParams(vmem_limit_bytes=min(size, 36 << 20))


def chip_at(place):
    experts = lax.axis_size("expert")
    per_expert = lax.axis_size("dp") // CORES
    upper = 1 - place % 2
    rank = place // 2 // experts
    within = per_expert // 2 + upper * rank - (1 - upper) * (1 + rank)
    return place // 2 % experts * per_expert + within


def pack_kernel(
    tokens_hbm, grad_hbm, ids_hbm, scores_hbm, out_ref,
    tokens_ref, grad_ref, ids_ref, scores_ref, weighted_ref, sems,
):
    copies = [
        pltpu.make_async_copy(src, dst, sems.at[i])
        for i, (src, dst) in enumerate((
            (ids_hbm, ids_ref),
            (scores_hbm, scores_ref),
            (tokens_hbm, tokens_ref),
            (grad_hbm, grad_ref),
        ))
    ]
    for copy in copies:
        copy.start()
    for copy in copies:
        copy.wait()
    chips, tok_dev, _ = out_ref.shape
    width = tokens_ref.shape[2]
    experts = lax.axis_size("expert")
    first = lax.axis_index("expert") * tok_dev
    ids = ids_ref[0]
    scores = scores_ref[0].astype(jnp.float32)
    token = lax.broadcasted_iota(jnp.int32, ids.shape, 1)
    lane = lax.broadcasted_iota(jnp.int32, (ids.shape[0], LANES), 1)
    row = lax.broadcasted_iota(jnp.int32, (tok_dev, LANES), 0)
    table = jnp.zeros((tok_dev, LANES), jnp.float32)
    for i in range(tok_dev):
        mine = token == first + i
        named = jnp.sum(jnp.where(mine, ids, 0), axis=1, keepdims=True)
        score = jnp.sum(jnp.where(mine, scores, 0.0), axis=1, keepdims=True)
        weights = jnp.sum(jnp.where(lane == named, score, 0.0), axis=0, keepdims=True)
        table = jnp.where(row == i, weights, table)
    grad = grad_ref[0].astype(jnp.float32)
    for expert in range(experts):
        weighted_ref[expert] = (grad * table[:, expert : expert + 1]).astype(jnp.bfloat16)

    def write(place, carry):
        out_ref[place, :, :width] = tokens_ref[0]
        out_ref[place, :, width:] = weighted_ref[chip_at(place) // (chips // experts)]
        return carry

    lax.fori_loop(0, chips, write, 0, unroll=chips <= 16)


def pack(tokens, out_grad, expert_ids, gate_scores, chips):
    _, tok_dev, width = tokens.shape
    operands = [
        pltpu.with_memory_space_constraint(a, pltpu.HBM)
        for a in (
            tokens, out_grad, jnp.swapaxes(expert_ids, 1, 2), jnp.swapaxes(gate_scores, 1, 2)
        )
    ]
    return pl.pallas_call(
        pack_kernel,
        out_shape=jax.ShapeDtypeStruct((chips, tok_dev, 2 * width), jnp.bfloat16),
        in_specs=[HBM] * 4,
        out_specs=VMEM,
        scratch_shapes=[pltpu.VMEM(a.shape, a.dtype) for a in operands]
        + [
            pltpu.VMEM((lax.axis_size("expert"), tok_dev, width), jnp.bfloat16),
            pltpu.SemaphoreType.DMA((4,)),
        ],
        compiler_params=vmem(16 << 20),
    )(*operands)


def copy_pieces(src, dst, sems):
    rows = dst.shape[0] // PIECES
    parts = [pl.ds(piece * rows, rows) for piece in range(PIECES)]
    copies = [
        pltpu.make_async_copy(src.at[0, part], dst.at[part], sems.at[piece])
        for piece, part in enumerate(parts)
    ]
    for copy in copies:
        copy.start()
    return copies


def lay_out(src_ref, x_ref, dy_ref, first):
    chips, tok_dev, _ = src_ref.shape
    width = x_ref.shape[1]
    per_tile = TILE // tok_dev

    def step(tile, carry):
        rows = pl.ds(pl.multiple_of(first + tile * TILE, TILE), TILE)
        blocks = [src_ref[tile * per_tile + j] for j in range(per_tile)]
        x_ref[rows] = jnp.concatenate([b[:, :width] for b in blocks], axis=0)
        dy_ref[rows] = jnp.concatenate([b[:, width:] for b in blocks], axis=0)
        return carry

    tiles = chips // per_tile
    lax.fori_loop(0, tiles, step, 0, unroll=tiles <= 2)


def fetch_kernel(mine_ref, gate_hbm, gate_ref, x_ref, dy_ref, sems):
    copies = copy_pieces(gate_hbm, gate_ref, sems)
    lay_out(mine_ref, x_ref, dy_ref, 0)
    for copy in copies:
        copy.wait()


def fetch(mine, w_gate):
    chips, tok_dev, row = mine.shape
    _, width, hidden = w_gate.shape
    half = chips * tok_dev
    moved = 2 * width * hidden
    return pl.pallas_call(
        fetch_kernel,
        out_shape=(
            pltpu.VMEM((width, hidden), jnp.bfloat16),
            pltpu.VMEM((half, width), jnp.bfloat16),
            pltpu.VMEM((half, width), jnp.bfloat16),
        ),
        in_specs=[VMEM, HBM],
        out_specs=(VMEM,) * 3,
        scratch_shapes=[pltpu.SemaphoreType.DMA((PIECES,))],
        cost_estimate=pl.CostEstimate(flops=0, bytes_accessed=2 * moved, transcendentals=0),
        compiler_params=vmem((8 << 20) + 2 * moved + 8 * half * row),
    )(mine, pltpu.with_memory_space_constraint(w_gate, pltpu.HBM))


def my_core():
    return lax.axis_index("dp") % CORES


def row_blocks(rows, step):
    step(0, True)
    if rows > ROWS:
        pl.loop(1, rows // ROWS)(lambda block: step(block, False))


def half_total(gate_delta, up_delta, gate_ref, up_ref, core):
    columns = gate_ref.shape[0] // CORES
    part = pl.ds(pl.multiple_of(core * columns, columns), columns)
    total = lax.dot_general(
        gate_delta, gate_ref[part], CONTRACT_LAST, preferred_element_type=jnp.float32
    )
    return total + lax.dot_general(
        up_delta, up_ref[part], CONTRACT_LAST, preferred_element_type=jnp.float32
    )


def store_groups(ref, first, total):
    rows, columns = total.shape
    groups = columns // LANES
    for c in range(groups):
        ref[pl.ds(first + c, rows, stride=groups)] = total[:, c * LANES : (c + 1) * LANES]


def rows_kernel(
    other_ref, my_x_ref, my_dy_ref, gate_ref, up_hbm, down_hbm,
    sent_ref, up_ref, x_ref, dy_ref, gate_delta_ref, up_delta_ref, hidden_ref,
    down_ref, total_ref, sems,
):
    up_copies = copy_pieces(up_hbm, up_ref, sems.at[0])
    down_copies = copy_pieces(down_hbm, down_ref, sems.at[1])
    half = my_x_ref.shape[0]
    x_ref[:half] = my_x_ref[...]
    dy_ref[:half] = my_dy_ref[...]
    lay_out(other_ref, x_ref, dy_ref, half)
    depth = up_ref.shape[0] // PIECES

    def step(block, first):
        rows = pl.ds(pl.multiple_of(block * ROWS, ROWS), ROWS)
        x = x_ref[rows]
        pre_gate = jnp.dot(x, gate_ref[...], preferred_element_type=jnp.float32)
        sigmoid_gate = jax.nn.sigmoid(pre_gate)
        activated = pre_gate * sigmoid_gate
        pre_up = None
        for piece, copy in enumerate(up_copies):
            if first:
                copy.wait()
            part = slice(piece * depth, (piece + 1) * depth)
            product = jnp.dot(x[:, part], up_ref[part], preferred_element_type=jnp.float32)
            pre_up = product if pre_up is None else pre_up + product
        hidden_ref[rows] = (activated * pre_up).astype(jnp.bfloat16)
        if first:
            for copy in down_copies:
                copy.wait()
        grad_hidden = lax.dot_general(
            dy_ref[rows], down_ref[...], CONTRACT_LAST, preferred_element_type=jnp.float32
        )
        gate_delta = (
            grad_hidden * pre_up * sigmoid_gate * (1.0 + pre_gate * (1.0 - sigmoid_gate))
        ).astype(jnp.bfloat16)
        up_delta = (grad_hidden * activated).astype(jnp.bfloat16)
        gate_delta_ref[rows] = gate_delta
        up_delta_ref[rows] = up_delta
        total = half_total(gate_delta, up_delta, gate_ref, up_ref, 1 - my_core())
        store_groups(total_ref, 0, total)
        size = total_ref.shape[0]
        part = pl.ds(pl.multiple_of(block * size, size), size)
        sent_ref[part] = total_ref[...].astype(jnp.bfloat16)

    row_blocks(x_ref.shape[0], step)


def rows_pass(other, my_x, my_dy, gate, w_up, w_down):
    chips, tok_dev, row = other.shape
    width, hidden = gate.shape
    rows = 2 * chips * tok_dev
    groups = width // CORES // LANES
    bf16 = functools.partial(jax.ShapeDtypeStruct, dtype=jnp.bfloat16)
    moved = (3 * width * hidden + rows * (6 * width + 3 * hidden)) * 2
    up, down = (pltpu.with_memory_space_constraint(w, pltpu.HBM) for w in (w_up, w_down))
    return pl.pallas_call(
        rows_kernel,
        out_shape=(
            bf16((rows * groups, LANES)),
            pltpu.VMEM((width, hidden), jnp.bfloat16),
            bf16((rows, width)),
            bf16((rows, width)),
            bf16((rows, hidden)),
            bf16((rows, hidden)),
            bf16((rows, hidden)),
        ),
        in_specs=[VMEM] * 4 + [HBM] * 2,
        out_specs=(VMEM,) * 7,
        scratch_shapes=[
            pltpu.VMEM((hidden, width), jnp.bfloat16),
            pltpu.VMEM((ROWS * groups, LANES), jnp.float32),
            pltpu.SemaphoreType.DMA((2, PIECES)),
        ],
        cost_estimate=pl.CostEstimate(
            flops=8 * rows * width * hidden, bytes_accessed=moved, transcendentals=rows * hidden
        ),
        compiler_params=vmem((12 << 20) + 2 * moved),
    )(other, my_x, my_dy, gate, up, down)


def finish_kernel(gate_delta_ref, up_delta_ref, gate_ref, up_ref, total_ref):
    rows_all = gate_delta_ref.shape[0]
    size = total_ref.shape[0] // rows_all * ROWS

    def step(block, first):
        rows = pl.ds(pl.multiple_of(block * ROWS, ROWS), ROWS)
        total = half_total(
            gate_delta_ref[rows], up_delta_ref[rows], gate_ref, up_ref, my_core()
        )
        store_groups(total_ref, block * size, total)

    row_blocks(rows_all, step)


def finish(gate_delta, up_delta, gate, up):
    rows, hidden = gate_delta.shape
    columns = gate.shape[0] // CORES
    moved = 4 * columns * hidden + 4 * rows * (columns + hidden)
    return pl.pallas_call(
        finish_kernel,
        out_shape=jax.ShapeDtypeStruct((rows * columns // LANES, LANES), jnp.float32),
        in_specs=[VMEM] * 4,
        out_specs=VMEM,
        cost_estimate=pl.CostEstimate(
            flops=4 * rows * columns * hidden, bytes_accessed=moved, transcendentals=0
        ),
        compiler_params=vmem((16 << 20) + 2 * moved),
    )(gate_delta, up_delta, gate, up)


def share_kernel(total_ref, got_ref, shares_ref):
    devices, size, _ = shares_ref.shape
    chips = devices // CORES
    core = my_core()

    def step(place, carry):
        here = pl.ds(pl.multiple_of(place * size, size), size)
        there = pl.ds(pl.multiple_of((place + chips) % devices * size, size), size)
        owner = jnp.where(place < chips, core, 1 - core)
        total = total_ref[here] + got_ref[there].astype(jnp.float32)
        shares_ref[place % chips * CORES + owner] = total.astype(jnp.bfloat16)
        return carry

    lax.fori_loop(0, devices, step, 0, unroll=devices <= 32)


def share(total, got, devices):
    size = total.shape[0] // devices
    return pl.pallas_call(
        share_kernel,
        out_shape=pltpu.VMEM((devices, size, LANES), jnp.bfloat16),
        in_specs=[VMEM] * 2,
        out_specs=VMEM,
        compiler_params=vmem((8 << 20) + 32 * total.size),
    )(total, got)


def sum_kernel(shares_ref, out_hbm, wide_ref, out_ref, sem):
    devices, size, _ = shares_ref.shape
    _, tok_dev, width = out_ref.shape
    groups = size // tok_dev
    for core in range(CORES):
        total = lax.fori_loop(
            0,
            devices // CORES,
            lambda i, acc: acc + shares_ref[i * CORES + core].astype(jnp.float32),
            jnp.zeros((size, LANES), jnp.float32),
            unroll=devices <= 32,
        )
        for row in range(size):
            token, lane = row // groups, (core * groups + row % groups) * LANES
            wide_ref[token : token + 1, lane : lane + LANES] = total[row : row + 1]
    out_ref[0] = wide_ref[...].astype(jnp.bfloat16)
    copy = pltpu.make_async_copy(out_ref, out_hbm, sem)
    copy.start()
    copy.wait()


def sum_shares(shares, tok_dev):
    _, size, _ = shares.shape
    width = CORES * size // tok_dev * LANES
    return pl.pallas_call(
        sum_kernel,
        out_shape=pltpu.HBM((1, tok_dev, width), jnp.bfloat16),
        in_specs=[VMEM],
        out_specs=HBM,
        scratch_shapes=[
            pltpu.VMEM((tok_dev, width), jnp.float32),
            pltpu.VMEM((1, tok_dev, width), jnp.bfloat16),
            pltpu.SemaphoreType.DMA,
        ],
        compiler_params=vmem(16 << 20),
    )(shares)


def local(tokens, out_grad, expert_ids, gate_scores, w_gate, w_up, w_down):
    devices = lax.axis_size("expert") * lax.axis_size("dp")
    chips = devices // CORES
    order = [chip_at(place) for place in range(chips)]
    same_core = [[chip * CORES + core for chip in order] for core in range(CORES)]
    everyone = [[chip * CORES + core for chip in order for core in range(CORES)]]
    core_pairs = [(d, d ^ 1) for d in range(devices)]
    copies = pack(tokens, out_grad, expert_ids, gate_scores, chips)
    mine = lax.all_to_all(copies, BOTH, 0, 0, axis_index_groups=same_core, tiled=True)
    other = lax.ppermute(mine, BOTH, core_pairs)
    gate, my_x, my_dy = fetch(mine, w_gate)
    sent, up, x, dy, gate_delta, up_delta, hidden = rows_pass(
        other, my_x, my_dy, gate, w_up, w_down
    )
    got = lax.ppermute(sent, BOTH, core_pairs)
    total = finish(gate_delta, up_delta, gate, up)
    shares = share(total, got, devices)
    shares, gate_delta, up_delta, hidden = lax.optimization_barrier(
        (shares, gate_delta, up_delta, hidden)
    )
    shares = lax.all_to_all(shares, BOTH, 0, 0, axis_index_groups=everyone, tiled=True)
    token_grad = sum_shares(shares, tokens.shape[1])
    grad_down = jnp.dot(hidden.T, dy, preferred_element_type=jnp.float32)
    grad_gate = jnp.dot(x.T, gate_delta, preferred_element_type=jnp.float32)
    grad_up = jnp.dot(x.T, up_delta, preferred_element_type=jnp.float32)
    weight_grads = (grad_gate, grad_up, grad_down)
    return (token_grad,) + tuple(g.astype(jnp.bfloat16)[None] for g in weight_grads)


def solution(mesh):
    return jax.shard_map(
        local,
        mesh=mesh,
        in_specs=(
            P("dp", "expert", None),
            P("dp", "expert", None),
            P("dp", None, None),
            P("dp", None, None),
            P("expert", None, "dp"),
            P("expert", None, "dp"),
            P("expert", "dp", None),
        ),
        out_specs=(
            P("dp", "expert", None),
            P("expert", None, "dp"),
            P("expert", None, "dp"),
            P("expert", "dp", None),
        ),
        check_vma=False,
    )
```

```python
import functools

import jax
import jax.numpy as jnp
from jax import lax
from jax.experimental import pallas as pl
from jax.experimental.pallas import tpu as pltpu
from jax.sharding import PartitionSpec as P

LANES = 128
CORES = 2
BOTH = ("expert", "dp")
ROWS = 64
TILE = 16
CONTRACT_LAST = (((1,), (1,)), ((), ()))
PIECES = 4
VMEM = pl.BlockSpec(memory_space=pltpu.VMEM)
HBM = pl.BlockSpec(memory_space=pltpu.HBM)


def vmem(size):
    return pltpu.CompilerParams(vmem_limit_bytes=min(size, 36 << 20))


def chip_at(place):
    experts = lax.axis_size("expert")
    per_expert = lax.axis_size("dp") // CORES
    upper = 1 - place % 2
    rank = place // 2 // experts
    within = per_expert // 2 + upper * rank - (1 - upper) * (1 + rank)
    return place // 2 % experts * per_expert + within


def pack_kernel(
    tokens_hbm, grad_hbm, ids_hbm, scores_hbm, out_ref,
    tokens_ref, grad_ref, ids_ref, scores_ref, weighted_ref, sems,
):
    copies = [
        pltpu.make_async_copy(src, dst, sems.at[i])
        for i, (src, dst) in enumerate((
            (ids_hbm, ids_ref),
            (scores_hbm, scores_ref),
            (tokens_hbm, tokens_ref),
            (grad_hbm, grad_ref),
        ))
    ]
    for copy in copies:
        copy.start()
    for copy in copies:
        copy.wait()
    chips, tok_dev, _ = out_ref.shape
    width = tokens_ref.shape[2]
    experts = lax.axis_size("expert")
    first = lax.axis_index("expert") * tok_dev
    ids = ids_ref[0]
    scores = scores_ref[0].astype(jnp.float32)
    token = lax.broadcasted_iota(jnp.int32, ids.shape, 1)
    lane = lax.broadcasted_iota(jnp.int32, (ids.shape[0], LANES), 1)
    row = lax.broadcasted_iota(jnp.int32, (tok_dev, LANES), 0)
    table = jnp.zeros((tok_dev, LANES), jnp.float32)
    for i in range(tok_dev):
        mine = token == first + i
        named = jnp.sum(jnp.where(mine, ids, 0), axis=1, keepdims=True)
        score = jnp.sum(jnp.where(mine, scores, 0.0), axis=1, keepdims=True)
        weights = jnp.sum(jnp.where(lane == named, score, 0.0), axis=0, keepdims=True)
        table = jnp.where(row == i, weights, table)
    grad = grad_ref[0].astype(jnp.float32)
    for expert in range(experts):
        weighted_ref[expert] = (grad * table[:, expert : expert + 1]).astype(jnp.bfloat16)

    def write(place, carry):
        out_ref[place, :, :width] = tokens_ref[0]
        out_ref[place, :, width:] = weighted_ref[chip_at(place) // (chips // experts)]
        return carry

    lax.fori_loop(0, chips, write, 0, unroll=chips <= 16)


def pack(tokens, out_grad, expert_ids, gate_scores, chips):
    _, tok_dev, width = tokens.shape
    operands = [
        pltpu.with_memory_space_constraint(a, pltpu.HBM)
        for a in (
            tokens, out_grad, jnp.swapaxes(expert_ids, 1, 2), jnp.swapaxes(gate_scores, 1, 2)
        )
    ]
    return pl.pallas_call(
        pack_kernel,
        out_shape=jax.ShapeDtypeStruct((chips, tok_dev, 2 * width), jnp.bfloat16),
        in_specs=[HBM] * 4,
        out_specs=VMEM,
        scratch_shapes=[pltpu.VMEM(a.shape, a.dtype) for a in operands]
        + [
            pltpu.VMEM((lax.axis_size("expert"), tok_dev, width), jnp.bfloat16),
            pltpu.SemaphoreType.DMA((4,)),
        ],
        compiler_params=vmem(16 << 20),
    )(*operands)


def copy_pieces(src, dst, sems):
    rows = dst.shape[0] // PIECES
    parts = [pl.ds(piece * rows, rows) for piece in range(PIECES)]
    copies = [
        pltpu.make_async_copy(src.at[0, part], dst.at[part], sems.at[piece])
        for piece, part in enumerate(parts)
    ]
    for copy in copies:
        copy.start()
    return copies


def lay_out(src_ref, x_ref, dy_ref, first):
    chips, tok_dev, _ = src_ref.shape
    width = x_ref.shape[1]
    per_tile = TILE // tok_dev

    def step(tile, carry):
        rows = pl.ds(pl.multiple_of(first + tile * TILE, TILE), TILE)
        blocks = [src_ref[tile * per_tile + j] for j in range(per_tile)]
        x_ref[rows] = jnp.concatenate([b[:, :width] for b in blocks], axis=0)
        dy_ref[rows] = jnp.concatenate([b[:, width:] for b in blocks], axis=0)
        return carry

    tiles = chips // per_tile
    lax.fori_loop(0, tiles, step, 0, unroll=tiles <= 2)


def fetch_kernel(mine_ref, gate_hbm, gate_ref, x_ref, dy_ref, sems):
    copies = copy_pieces(gate_hbm, gate_ref, sems)
    lay_out(mine_ref, x_ref, dy_ref, 0)
    for copy in copies:
        copy.wait()


def fetch(mine, w_gate):
    chips, tok_dev, row = mine.shape
    _, width, hidden = w_gate.shape
    half = chips * tok_dev
    moved = 2 * width * hidden
    return pl.pallas_call(
        fetch_kernel,
        out_shape=(
            pltpu.VMEM((width, hidden), jnp.bfloat16),
            pltpu.VMEM((half, width), jnp.bfloat16),
            pltpu.VMEM((half, width), jnp.bfloat16),
        ),
        in_specs=[VMEM, HBM],
        out_specs=(VMEM,) * 3,
        scratch_shapes=[pltpu.SemaphoreType.DMA((PIECES,))],
        cost_estimate=pl.CostEstimate(flops=0, bytes_accessed=2 * moved, transcendentals=0),
        compiler_params=vmem((8 << 20) + 2 * moved + 8 * half * row),
    )(mine, pltpu.with_memory_space_constraint(w_gate, pltpu.HBM))


def my_core():
    return lax.axis_index("dp") % CORES


def row_blocks(rows, step):
    step(0, True)
    if rows > ROWS:
        pl.loop(1, rows // ROWS)(lambda block: step(block, False))


def half_total(gate_delta, up_delta, gate_ref, up_ref, core):
    columns = gate_ref.shape[0] // CORES
    part = pl.ds(pl.multiple_of(core * columns, columns), columns)
    total = lax.dot_general(
        gate_delta, gate_ref[part], CONTRACT_LAST, preferred_element_type=jnp.float32
    )
    return total + lax.dot_general(
        up_delta, up_ref[part], CONTRACT_LAST, preferred_element_type=jnp.float32
    )


def store_groups(ref, first, total):
    rows, columns = total.shape
    groups = columns // LANES
    for c in range(groups):
        ref[pl.ds(first + c, rows, stride=groups)] = total[:, c * LANES : (c + 1) * LANES]


def rows_kernel(
    other_ref, my_x_ref, my_dy_ref, gate_ref, up_hbm, down_hbm,
    sent_ref, up_ref, x_ref, dy_ref, gate_delta_ref, up_delta_ref, hidden_ref,
    down_ref, total_ref, sems,
):
    down_copies = copy_pieces(down_hbm, down_ref, sems.at[0])
    up_copies = copy_pieces(up_hbm, up_ref, sems.at[1])
    half = my_x_ref.shape[0]
    x_ref[:half] = my_x_ref[...]
    dy_ref[:half] = my_dy_ref[...]
    lay_out(other_ref, x_ref, dy_ref, half)
    depth = up_ref.shape[0] // PIECES

    def step(block, first):
        rows = pl.ds(pl.multiple_of(block * ROWS, ROWS), ROWS)
        x = x_ref[rows]
        pre_gate = jnp.dot(x, gate_ref[...], preferred_element_type=jnp.float32)
        sigmoid_gate = jax.nn.sigmoid(pre_gate)
        activated = pre_gate * sigmoid_gate
        slope = sigmoid_gate * (1.0 + pre_gate * (1.0 - sigmoid_gate))
        if first:
            for copy in down_copies:
                copy.wait()
        grad_hidden = lax.dot_general(
            dy_ref[rows], down_ref[...], CONTRACT_LAST, preferred_element_type=jnp.float32
        )
        pre_up = None
        for piece, copy in enumerate(up_copies):
            if first:
                copy.wait()
            part = slice(piece * depth, (piece + 1) * depth)
            product = jnp.dot(x[:, part], up_ref[part], preferred_element_type=jnp.float32)
            pre_up = product if pre_up is None else pre_up + product
        hidden_ref[rows] = (activated * pre_up).astype(jnp.bfloat16)
        gate_delta = (grad_hidden * pre_up * slope).astype(jnp.bfloat16)
        up_delta = (grad_hidden * activated).astype(jnp.bfloat16)
        gate_delta_ref[rows] = gate_delta
        up_delta_ref[rows] = up_delta
        total = half_total(gate_delta, up_delta, gate_ref, up_ref, 1 - my_core())
        store_groups(total_ref, 0, total)
        size = total_ref.shape[0]
        part = pl.ds(pl.multiple_of(block * size, size), size)
        sent_ref[part] = total_ref[...].astype(jnp.bfloat16)

    row_blocks(x_ref.shape[0], step)


def rows_pass(other, my_x, my_dy, gate, w_up, w_down):
    chips, tok_dev, row = other.shape
    width, hidden = gate.shape
    rows = 2 * chips * tok_dev
    groups = width // CORES // LANES
    bf16 = functools.partial(jax.ShapeDtypeStruct, dtype=jnp.bfloat16)
    moved = (3 * width * hidden + rows * (6 * width + 3 * hidden)) * 2
    up, down = (pltpu.with_memory_space_constraint(w, pltpu.HBM) for w in (w_up, w_down))
    return pl.pallas_call(
        rows_kernel,
        out_shape=(
            bf16((rows * groups, LANES)),
            pltpu.VMEM((width, hidden), jnp.bfloat16),
            bf16((rows, width)),
            bf16((rows, width)),
            bf16((rows, hidden)),
            bf16((rows, hidden)),
            bf16((rows, hidden)),
        ),
        in_specs=[VMEM] * 4 + [HBM] * 2,
        out_specs=(VMEM,) * 7,
        scratch_shapes=[
            pltpu.VMEM((hidden, width), jnp.bfloat16),
            pltpu.VMEM((ROWS * groups, LANES), jnp.float32),
            pltpu.SemaphoreType.DMA((2, PIECES)),
        ],
        cost_estimate=pl.CostEstimate(
            flops=8 * rows * width * hidden, bytes_accessed=moved, transcendentals=rows * hidden
        ),
        compiler_params=vmem((12 << 20) + 2 * moved),
    )(other, my_x, my_dy, gate, up, down)


def finish_kernel(gate_delta_ref, up_delta_ref, gate_ref, up_ref, total_ref):
    rows_all = gate_delta_ref.shape[0]
    size = total_ref.shape[0] // rows_all * ROWS

    def step(block, first):
        rows = pl.ds(pl.multiple_of(block * ROWS, ROWS), ROWS)
        total = half_total(
            gate_delta_ref[rows], up_delta_ref[rows], gate_ref, up_ref, my_core()
        )
        store_groups(total_ref, block * size, total)

    row_blocks(rows_all, step)


def finish(gate_delta, up_delta, gate, up):
    rows, hidden = gate_delta.shape
    columns = gate.shape[0] // CORES
    moved = 4 * columns * hidden + 4 * rows * (columns + hidden)
    return pl.pallas_call(
        finish_kernel,
        out_shape=jax.ShapeDtypeStruct((rows * columns // LANES, LANES), jnp.float32),
        in_specs=[VMEM] * 4,
        out_specs=VMEM,
        cost_estimate=pl.CostEstimate(
            flops=4 * rows * columns * hidden, bytes_accessed=moved, transcendentals=0
        ),
        compiler_params=vmem((16 << 20) + 2 * moved),
    )(gate_delta, up_delta, gate, up)


def share_kernel(total_ref, got_ref, shares_ref):
    devices, size, _ = shares_ref.shape
    chips = devices // CORES
    core = my_core()

    def step(place, carry):
        here = pl.ds(pl.multiple_of(place * size, size), size)
        there = pl.ds(pl.multiple_of((place + chips) % devices * size, size), size)
        owner = jnp.where(place < chips, core, 1 - core)
        total = total_ref[here] + got_ref[there].astype(jnp.float32)
        shares_ref[chip_at(place % chips) * CORES + owner] = total.astype(jnp.bfloat16)
        return carry

    lax.fori_loop(0, devices, step, 0, unroll=devices <= 32)


def share(total, got, devices):
    size = total.shape[0] // devices
    return pl.pallas_call(
        share_kernel,
        out_shape=pltpu.VMEM((devices, size, LANES), jnp.bfloat16),
        in_specs=[VMEM] * 2,
        out_specs=VMEM,
        compiler_params=vmem((8 << 20) + 32 * total.size),
    )(total, got)


def sum_kernel(shares_ref, out_hbm, wide_ref, out_ref, sem):
    devices, size, _ = shares_ref.shape
    _, tok_dev, width = out_ref.shape
    groups = size // tok_dev
    for core in range(CORES):
        total = lax.fori_loop(
            0,
            devices // CORES,
            lambda i, acc: acc + shares_ref[i * CORES + core].astype(jnp.float32),
            jnp.zeros((size, LANES), jnp.float32),
            unroll=devices <= 32,
        )
        for row in range(size):
            token, lane = row // groups, (core * groups + row % groups) * LANES
            wide_ref[token : token + 1, lane : lane + LANES] = total[row : row + 1]
    out_ref[0] = wide_ref[...].astype(jnp.bfloat16)
    copy = pltpu.make_async_copy(out_ref, out_hbm, sem)
    copy.start()
    copy.wait()


def sum_shares(shares, tok_dev):
    _, size, _ = shares.shape
    width = CORES * size // tok_dev * LANES
    return pl.pallas_call(
        sum_kernel,
        out_shape=pltpu.HBM((1, tok_dev, width), jnp.bfloat16),
        in_specs=[VMEM],
        out_specs=HBM,
        scratch_shapes=[
            pltpu.VMEM((tok_dev, width), jnp.float32),
            pltpu.VMEM((1, tok_dev, width), jnp.bfloat16),
            pltpu.SemaphoreType.DMA,
        ],
        compiler_params=vmem(16 << 20),
    )(shares)


def local(tokens, out_grad, expert_ids, gate_scores, w_gate, w_up, w_down):
    devices = lax.axis_size("expert") * lax.axis_size("dp")
    chips = devices // CORES
    order = [chip_at(place) for place in range(chips)]
    same_core = [[chip * CORES + core for chip in order] for core in range(CORES)]
    core_pairs = [(d, d ^ 1) for d in range(devices)]
    copies = pack(tokens, out_grad, expert_ids, gate_scores, chips)
    mine = lax.all_to_all(copies, BOTH, 0, 0, axis_index_groups=same_core, tiled=True)
    other = lax.ppermute(mine, BOTH, core_pairs)
    gate, my_x, my_dy = fetch(mine, w_gate)
    sent, up, x, dy, gate_delta, up_delta, hidden = rows_pass(
        other, my_x, my_dy, gate, w_up, w_down
    )
    got = lax.ppermute(sent, BOTH, core_pairs)
    total = finish(gate_delta, up_delta, gate, up)
    shares = share(total, got, devices)
    shares, gate_delta, up_delta, hidden = lax.optimization_barrier(
        (shares, gate_delta, up_delta, hidden)
    )
    shares = lax.all_to_all(shares, BOTH, 0, 0, tiled=True)
    token_grad = sum_shares(shares, tokens.shape[1])
    grad_down = jnp.dot(hidden.T, dy, preferred_element_type=jnp.float32)
    grad_gate = jnp.dot(x.T, gate_delta, preferred_element_type=jnp.float32)
    grad_up = jnp.dot(x.T, up_delta, preferred_element_type=jnp.float32)
    weight_grads = (grad_gate, grad_up, grad_down)
    return (token_grad,) + tuple(g.astype(jnp.bfloat16)[None] for g in weight_grads)


def solution(mesh):
    return jax.shard_map(
        local,
        mesh=mesh,
        in_specs=(
            P("dp", "expert", None),
            P("dp", "expert", None),
            P("dp", None, None),
            P("dp", None, None),
            P("expert", None, "dp"),
            P("expert", None, "dp"),
            P("expert", "dp", None),
        ),
        out_specs=(
            P("dp", "expert", None),
            P("expert", None, "dp"),
            P("expert", None, "dp"),
            P("expert", "dp", None),
        ),
        check_vma=False,
    )
```

```python
import functools

import jax
import jax.numpy as jnp
from jax import lax
from jax.experimental import pallas as pl
from jax.experimental.pallas import tpu as pltpu
from jax.sharding import PartitionSpec as P

LANES = 128
CORES = 2
BOTH = ("expert", "dp")
ROWS = 64
TILE = 16
CONTRACT_LAST = (((1,), (1,)), ((), ()))
PIECES = 4
VMEM = pl.BlockSpec(memory_space=pltpu.VMEM)
HBM = pl.BlockSpec(memory_space=pltpu.HBM)


def vmem(size):
    return pltpu.CompilerParams(vmem_limit_bytes=min(size, 36 << 20))


def chip_at(place):
    experts = lax.axis_size("expert")
    per_expert = lax.axis_size("dp") // CORES
    upper = 1 - place % 2
    rank = place // 2 // experts
    within = per_expert // 2 + upper * rank - (1 - upper) * (1 + rank)
    return place // 2 % experts * per_expert + within


def pack_kernel(
    tokens_hbm, grad_hbm, ids_hbm, scores_hbm, out_ref,
    tokens_ref, grad_ref, ids_ref, scores_ref, wide_ref, block_ref, sems,
):
    copies = [
        pltpu.make_async_copy(src, dst, sems.at[i])
        for i, (src, dst) in enumerate((
            (ids_hbm, ids_ref),
            (scores_hbm, scores_ref),
            (tokens_hbm, tokens_ref),
            (grad_hbm, grad_ref),
        ))
    ]
    for copy in copies:
        copy.start()
    for copy in copies:
        copy.wait()
    chips, size, _ = out_ref.shape
    _, tok_dev, width = tokens_ref.shape
    experts = lax.axis_size("expert")
    first = lax.axis_index("expert") * tok_dev
    ids = ids_ref[0]
    scores = scores_ref[0].astype(jnp.float32)
    token = lax.broadcasted_iota(jnp.int32, ids.shape, 1)
    lane = lax.broadcasted_iota(jnp.int32, (ids.shape[0], LANES), 1)
    row = lax.broadcasted_iota(jnp.int32, (tok_dev, LANES), 0)
    table = jnp.zeros((tok_dev, LANES), jnp.float32)
    for i in range(tok_dev):
        mine = token == first + i
        named = jnp.sum(jnp.where(mine, ids, 0), axis=1, keepdims=True)
        score = jnp.sum(jnp.where(mine, scores, 0.0), axis=1, keepdims=True)
        weights = jnp.sum(jnp.where(lane == named, score, 0.0), axis=0, keepdims=True)
        table = jnp.where(row == i, weights, table)
    def put(first, value):
        for c in range(width // LANES):
            at = first + c * tok_dev
            wide_ref[at : at + tok_dev] = value[:, c * LANES : (c + 1) * LANES]

    put(0, tokens_ref[0].astype(jnp.float32))
    grad = grad_ref[0].astype(jnp.float32)
    for expert in range(experts):
        put(size // 2, grad * table[:, expert : expert + 1])
        block_ref[expert] = wide_ref[...].astype(jnp.bfloat16)

    def write(place, carry):
        out_ref[place] = block_ref[chip_at(place) // (chips // experts)]
        return carry

    lax.fori_loop(0, chips, write, 0, unroll=chips <= 16)


def pack(tokens, out_grad, expert_ids, gate_scores, chips):
    size = 2 * tokens.size // LANES
    operands = [
        pltpu.with_memory_space_constraint(a, pltpu.HBM)
        for a in (
            tokens, out_grad, jnp.swapaxes(expert_ids, 1, 2), jnp.swapaxes(gate_scores, 1, 2)
        )
    ]
    return pl.pallas_call(
        pack_kernel,
        out_shape=jax.ShapeDtypeStruct((chips, size, LANES), jnp.bfloat16),
        in_specs=[HBM] * 4,
        out_specs=VMEM,
        scratch_shapes=[pltpu.VMEM(a.shape, a.dtype) for a in operands]
        + [
            pltpu.VMEM((size, LANES), jnp.float32),
            pltpu.VMEM((lax.axis_size("expert"), size, LANES), jnp.bfloat16),
            pltpu.SemaphoreType.DMA((4,)),
        ],
        compiler_params=vmem(16 << 20),
    )(*operands)


def copy_pieces(src, dst, sems):
    rows = dst.shape[0] // PIECES
    parts = [pl.ds(piece * rows, rows) for piece in range(PIECES)]
    copies = [
        pltpu.make_async_copy(src.at[0, part], dst.at[part], sems.at[piece])
        for piece, part in enumerate(parts)
    ]
    for copy in copies:
        copy.start()
    return copies


def lay_out(src_ref, x_ref, dy_ref, wide_ref, first):
    chips, size, _ = src_ref.shape
    groups = x_ref.shape[1] // LANES
    tok_dev = size // 2 // groups

    def step(tile, carry):
        for j in range(TILE):
            wide_ref[j * size : (j + 1) * size] = src_ref[tile * TILE + j].astype(jnp.float32)
        for t in range(tok_dev):
            rows = pl.ds(pl.multiple_of(first + t * chips + tile * TILE, TILE), TILE)
            for c in range(groups):
                lanes = slice(c * LANES, (c + 1) * LANES)
                for half, ref in enumerate((x_ref, dy_ref)):
                    at = half * size // 2 + c * tok_dev + t
                    ref[rows, lanes] = wide_ref[pl.ds(at, TILE, stride=size)].astype(
                        jnp.bfloat16
                    )
        return carry

    tiles = chips // TILE
    if tiles == 1:
        step(0, 0)
    else:
        lax.fori_loop(0, tiles, step, 0)


def fetch_kernel(mine_ref, gate_hbm, gate_ref, x_ref, dy_ref, wide_ref, sems):
    copies = copy_pieces(gate_hbm, gate_ref, sems)
    lay_out(mine_ref, x_ref, dy_ref, wide_ref, 0)
    for copy in copies:
        copy.wait()


def fetch(mine, w_gate):
    chips, size, _ = mine.shape
    _, width, hidden = w_gate.shape
    half = chips * size * LANES // 2 // width
    moved = 2 * width * hidden
    return pl.pallas_call(
        fetch_kernel,
        out_shape=(
            pltpu.VMEM((width, hidden), jnp.bfloat16),
            pltpu.VMEM((half, width), jnp.bfloat16),
            pltpu.VMEM((half, width), jnp.bfloat16),
        ),
        in_specs=[VMEM, HBM],
        out_specs=(VMEM,) * 3,
        scratch_shapes=[
            pltpu.VMEM((TILE * size, LANES), jnp.float32),
            pltpu.SemaphoreType.DMA((PIECES,)),
        ],
        cost_estimate=pl.CostEstimate(flops=0, bytes_accessed=2 * moved, transcendentals=0),
        compiler_params=vmem((8 << 20) + 2 * moved + 8 * mine.size),
    )(mine, pltpu.with_memory_space_constraint(w_gate, pltpu.HBM))


def my_core():
    return lax.axis_index("dp") % CORES


def row_blocks(rows, step):
    step(0, True)
    if rows > ROWS:
        pl.loop(1, rows // ROWS)(lambda block: step(block, False))


def half_total(gate_delta, up_delta, gate_ref, up_ref, core):
    columns = gate_ref.shape[0] // CORES
    part = pl.ds(pl.multiple_of(core * columns, columns), columns)
    total = lax.dot_general(
        gate_delta, gate_ref[part], CONTRACT_LAST, preferred_element_type=jnp.float32
    )
    return total + lax.dot_general(
        up_delta, up_ref[part], CONTRACT_LAST, preferred_element_type=jnp.float32
    )


def store_groups(ref, block, total):
    rows, columns = total.shape
    groups = columns // LANES
    chips = lax.axis_size("expert") * lax.axis_size("dp") // CORES
    half = ref.shape[0] // groups // CORES
    tok_dev = half // chips
    for tile in range(rows // TILE):
        row = block * rows + tile * TILE
        token = row % half // chips
        device = row // half * chips + row % chips
        first = (device * tok_dev + token) * groups
        part = total[tile * TILE : (tile + 1) * TILE]
        for c in range(groups):
            ref[pl.ds(first + c, TILE, stride=tok_dev * groups)] = part[
                :, c * LANES : (c + 1) * LANES
            ]


def rows_kernel(
    other_ref, my_x_ref, my_dy_ref, gate_ref, up_hbm, down_hbm,
    sent_ref, up_ref, x_ref, dy_ref, gate_delta_ref, up_delta_ref, hidden_ref,
    down_ref, wide_ref, total_ref, sems,
):
    down_copies = copy_pieces(down_hbm, down_ref, sems.at[0])
    up_copies = copy_pieces(up_hbm, up_ref, sems.at[1])
    half = my_x_ref.shape[0]
    x_ref[:half] = my_x_ref[...]
    dy_ref[:half] = my_dy_ref[...]
    lay_out(other_ref, x_ref, dy_ref, wide_ref, half)
    depth = up_ref.shape[0] // PIECES

    def step(block, first):
        rows = pl.ds(pl.multiple_of(block * ROWS, ROWS), ROWS)
        x = x_ref[rows]
        pre_gate = jnp.dot(x, gate_ref[...], preferred_element_type=jnp.float32)
        sigmoid_gate = jax.nn.sigmoid(pre_gate)
        activated = pre_gate * sigmoid_gate
        slope = sigmoid_gate * (1.0 + pre_gate * (1.0 - sigmoid_gate))
        if first:
            for copy in down_copies:
                copy.wait()
        grad_hidden = lax.dot_general(
            dy_ref[rows], down_ref[...], CONTRACT_LAST, preferred_element_type=jnp.float32
        )
        pre_up = None
        for piece, copy in enumerate(up_copies):
            if first:
                copy.wait()
            part = slice(piece * depth, (piece + 1) * depth)
            product = jnp.dot(x[:, part], up_ref[part], preferred_element_type=jnp.float32)
            pre_up = product if pre_up is None else pre_up + product
        hidden_ref[rows] = (activated * pre_up).astype(jnp.bfloat16)
        gate_delta = (grad_hidden * pre_up * slope).astype(jnp.bfloat16)
        up_delta = (grad_hidden * activated).astype(jnp.bfloat16)
        gate_delta_ref[rows] = gate_delta
        up_delta_ref[rows] = up_delta
        total = half_total(gate_delta, up_delta, gate_ref, up_ref, 1 - my_core())
        store_groups(total_ref, block, total)

    row_blocks(x_ref.shape[0], step)
    sent_ref[...] = total_ref[...].astype(jnp.bfloat16)


def rows_pass(other, my_x, my_dy, gate, w_up, w_down):
    chips, size, _ = other.shape
    width, hidden = gate.shape
    rows = CORES * my_x.shape[0]
    groups = width // CORES // LANES
    bf16 = functools.partial(jax.ShapeDtypeStruct, dtype=jnp.bfloat16)
    moved = (3 * width * hidden + rows * (6 * width + 3 * hidden)) * 2
    up, down = (pltpu.with_memory_space_constraint(w, pltpu.HBM) for w in (w_up, w_down))
    return pl.pallas_call(
        rows_kernel,
        out_shape=(
            bf16((rows * groups, LANES)),
            pltpu.VMEM((width, hidden), jnp.bfloat16),
            bf16((rows, width)),
            bf16((rows, width)),
            bf16((rows, hidden)),
            bf16((rows, hidden)),
            bf16((rows, hidden)),
        ),
        in_specs=[VMEM] * 4 + [HBM] * 2,
        out_specs=(VMEM,) * 7,
        scratch_shapes=[
            pltpu.VMEM((hidden, width), jnp.bfloat16),
            pltpu.VMEM((TILE * size, LANES), jnp.float32),
            pltpu.VMEM((rows * groups, LANES), jnp.float32),
            pltpu.SemaphoreType.DMA((2, PIECES)),
        ],
        cost_estimate=pl.CostEstimate(
            flops=8 * rows * width * hidden, bytes_accessed=moved, transcendentals=rows * hidden
        ),
        compiler_params=vmem((12 << 20) + 2 * moved),
    )(other, my_x, my_dy, gate, up, down)


def finish_kernel(gate_delta_ref, up_delta_ref, gate_ref, up_ref, total_ref):
    def step(block, first):
        rows = pl.ds(pl.multiple_of(block * ROWS, ROWS), ROWS)
        total = half_total(
            gate_delta_ref[rows], up_delta_ref[rows], gate_ref, up_ref, my_core()
        )
        store_groups(total_ref, block, total)

    row_blocks(gate_delta_ref.shape[0], step)


def finish(gate_delta, up_delta, gate, up):
    rows, hidden = gate_delta.shape
    columns = gate.shape[0] // CORES
    moved = 4 * columns * hidden + 4 * rows * (columns + hidden)
    return pl.pallas_call(
        finish_kernel,
        out_shape=jax.ShapeDtypeStruct((rows * columns // LANES, LANES), jnp.float32),
        in_specs=[VMEM] * 4,
        out_specs=VMEM,
        cost_estimate=pl.CostEstimate(
            flops=4 * rows * columns * hidden, bytes_accessed=moved, transcendentals=0
        ),
        compiler_params=vmem((16 << 20) + 2 * moved),
    )(gate_delta, up_delta, gate, up)


def share_kernel(total_ref, got_ref, shares_ref):
    devices, size, _ = shares_ref.shape
    chips = devices // CORES
    core = my_core()

    def step(place, carry):
        here = pl.ds(pl.multiple_of(place * size, size), size)
        there = pl.ds(pl.multiple_of((place + chips) % devices * size, size), size)
        owner = jnp.where(place < chips, core, 1 - core)
        total = total_ref[here] + got_ref[there].astype(jnp.float32)
        shares_ref[chip_at(place % chips) * CORES + owner] = total.astype(jnp.bfloat16)
        return carry

    lax.fori_loop(0, devices, step, 0, unroll=devices <= 32)


def share(total, got, devices):
    size = total.shape[0] // devices
    return pl.pallas_call(
        share_kernel,
        out_shape=pltpu.VMEM((devices, size, LANES), jnp.bfloat16),
        in_specs=[VMEM] * 2,
        out_specs=VMEM,
        compiler_params=vmem((8 << 20) + 32 * total.size),
    )(total, got)


def sum_kernel(shares_ref, out_hbm, wide_ref, out_ref, sem):
    devices, size, _ = shares_ref.shape
    _, tok_dev, width = out_ref.shape
    groups = size // tok_dev
    for core in range(CORES):
        total = lax.fori_loop(
            0,
            devices // CORES,
            lambda i, acc: acc + shares_ref[i * CORES + core].astype(jnp.float32),
            jnp.zeros((size, LANES), jnp.float32),
            unroll=devices <= 32,
        )
        for row in range(size):
            token, lane = row // groups, (core * groups + row % groups) * LANES
            wide_ref[token : token + 1, lane : lane + LANES] = total[row : row + 1]
    out_ref[0] = wide_ref[...].astype(jnp.bfloat16)
    copy = pltpu.make_async_copy(out_ref, out_hbm, sem)
    copy.start()
    copy.wait()


def sum_shares(shares, tok_dev):
    _, size, _ = shares.shape
    width = CORES * size // tok_dev * LANES
    return pl.pallas_call(
        sum_kernel,
        out_shape=pltpu.HBM((1, tok_dev, width), jnp.bfloat16),
        in_specs=[VMEM],
        out_specs=HBM,
        scratch_shapes=[
            pltpu.VMEM((tok_dev, width), jnp.float32),
            pltpu.VMEM((1, tok_dev, width), jnp.bfloat16),
            pltpu.SemaphoreType.DMA,
        ],
        compiler_params=vmem(16 << 20),
    )(shares)


def local(tokens, out_grad, expert_ids, gate_scores, w_gate, w_up, w_down):
    devices = lax.axis_size("expert") * lax.axis_size("dp")
    chips = devices // CORES
    order = [chip_at(place) for place in range(chips)]
    same_core = [[chip * CORES + core for chip in order] for core in range(CORES)]
    core_pairs = [(d, d ^ 1) for d in range(devices)]
    copies = pack(tokens, out_grad, expert_ids, gate_scores, chips)
    mine = lax.all_to_all(copies, BOTH, 0, 0, axis_index_groups=same_core, tiled=True)
    other = lax.ppermute(mine, BOTH, core_pairs)
    gate, my_x, my_dy = fetch(mine, w_gate)
    sent, up, x, dy, gate_delta, up_delta, hidden = rows_pass(
        other, my_x, my_dy, gate, w_up, w_down
    )
    got = lax.ppermute(sent, BOTH, core_pairs)
    total = finish(gate_delta, up_delta, gate, up)
    shares = share(total, got, devices)
    shares, gate_delta, up_delta, hidden = lax.optimization_barrier(
        (shares, gate_delta, up_delta, hidden)
    )
    shares = lax.all_to_all(shares, BOTH, 0, 0, tiled=True)
    token_grad = sum_shares(shares, tokens.shape[1])
    grad_down = jnp.dot(hidden.T, dy, preferred_element_type=jnp.float32)
    grad_gate = jnp.dot(x.T, gate_delta, preferred_element_type=jnp.float32)
    grad_up = jnp.dot(x.T, up_delta, preferred_element_type=jnp.float32)
    weight_grads = (grad_gate, grad_up, grad_down)
    return (token_grad,) + tuple(g.astype(jnp.bfloat16)[None] for g in weight_grads)


def solution(mesh):
    return jax.shard_map(
        local,
        mesh=mesh,
        in_specs=(
            P("dp", "expert", None),
            P("dp", "expert", None),
            P("dp", None, None),
            P("dp", None, None),
            P("expert", None, "dp"),
            P("expert", None, "dp"),
            P("expert", "dp", None),
        ),
        out_specs=(
            P("dp", "expert", None),
            P("expert", None, "dp"),
            P("expert", None, "dp"),
            P("expert", "dp", None),
        ),
        check_vma=False,
    )
```

```python
import functools

import jax
import jax.numpy as jnp
from jax import lax
from jax.experimental import pallas as pl
from jax.experimental.pallas import tpu as pltpu
from jax.sharding import PartitionSpec as P

LANES = 128
CORES = 2
BOTH = ("expert", "dp")
ROWS = 64
TILE = 16
CONTRACT_LAST = (((1,), (1,)), ((), ()))
PIECES = 4
VMEM = pl.BlockSpec(memory_space=pltpu.VMEM)
HBM = pl.BlockSpec(memory_space=pltpu.HBM)


def vmem(size):
    return pltpu.CompilerParams(vmem_limit_bytes=min(size, 36 << 20))


def chip_at(place):
    experts = lax.axis_size("expert")
    per_expert = lax.axis_size("dp") // CORES
    upper = 1 - place % 2
    rank = place // 2 // experts
    within = per_expert // 2 + upper * rank - (1 - upper) * (1 + rank)
    return place // 2 % experts * per_expert + within


def pack_kernel(
    tokens_hbm, grad_hbm, ids_hbm, scores_hbm, out_ref,
    tokens_ref, grad_ref, ids_ref, scores_ref, wide_ref, block_ref, sems,
):
    copies = [
        pltpu.make_async_copy(src, dst, sems.at[i])
        for i, (src, dst) in enumerate((
            (ids_hbm, ids_ref),
            (scores_hbm, scores_ref),
            (tokens_hbm, tokens_ref),
            (grad_hbm, grad_ref),
        ))
    ]
    for copy in copies:
        copy.start()
    for copy in copies:
        copy.wait()
    chips, size, _ = out_ref.shape
    _, tok_dev, width = tokens_ref.shape
    experts = lax.axis_size("expert")
    first = lax.axis_index("expert") * tok_dev
    ids = ids_ref[0]
    scores = scores_ref[0].astype(jnp.float32)
    token = lax.broadcasted_iota(jnp.int32, ids.shape, 1)
    lane = lax.broadcasted_iota(jnp.int32, (ids.shape[0], LANES), 1)
    row = lax.broadcasted_iota(jnp.int32, (tok_dev, LANES), 0)
    table = jnp.zeros((tok_dev, LANES), jnp.float32)
    for i in range(tok_dev):
        mine = token == first + i
        named = jnp.sum(jnp.where(mine, ids, 0), axis=1, keepdims=True)
        score = jnp.sum(jnp.where(mine, scores, 0.0), axis=1, keepdims=True)
        weights = jnp.sum(jnp.where(lane == named, score, 0.0), axis=0, keepdims=True)
        table = jnp.where(row == i, weights, table)
    def put(first, value):
        for c in range(width // LANES):
            at = first + c * tok_dev
            wide_ref[at : at + tok_dev] = value[:, c * LANES : (c + 1) * LANES]

    put(0, tokens_ref[0].astype(jnp.float32))
    grad = grad_ref[0].astype(jnp.float32)
    for expert in range(experts):
        put(size // 2, grad * table[:, expert : expert + 1])
        block_ref[expert] = wide_ref[...].astype(jnp.bfloat16)

    def write(place, carry):
        out_ref[place] = block_ref[chip_at(place) // (chips // experts)]
        return carry

    lax.fori_loop(0, chips, write, 0, unroll=chips <= 16)


def pack(tokens, out_grad, expert_ids, gate_scores, chips):
    size = 2 * tokens.size // LANES
    operands = [
        pltpu.with_memory_space_constraint(a, pltpu.HBM)
        for a in (
            tokens, out_grad, jnp.swapaxes(expert_ids, 1, 2), jnp.swapaxes(gate_scores, 1, 2)
        )
    ]
    return pl.pallas_call(
        pack_kernel,
        out_shape=jax.ShapeDtypeStruct((chips, size, LANES), jnp.bfloat16),
        in_specs=[HBM] * 4,
        out_specs=VMEM,
        scratch_shapes=[pltpu.VMEM(a.shape, a.dtype) for a in operands]
        + [
            pltpu.VMEM((size, LANES), jnp.float32),
            pltpu.VMEM((lax.axis_size("expert"), size, LANES), jnp.bfloat16),
            pltpu.SemaphoreType.DMA((4,)),
        ],
        compiler_params=vmem(16 << 20),
    )(*operands)


def copy_pieces(src, dst, sems):
    rows = dst.shape[0] // PIECES
    parts = [pl.ds(piece * rows, rows) for piece in range(PIECES)]
    return [
        pltpu.make_async_copy(src.at[0, part], dst.at[part], sems.at[piece])
        for piece, part in enumerate(parts)
    ]


def lay_out(src_ref, x_ref, dy_ref, wide_ref, first):
    chips, size, _ = src_ref.shape
    groups = x_ref.shape[1] // LANES
    tok_dev = size // 2 // groups

    def step(tile, carry):
        for j in range(TILE):
            wide_ref[j * size : (j + 1) * size] = src_ref[tile * TILE + j].astype(jnp.float32)
        for t in range(tok_dev):
            rows = pl.ds(pl.multiple_of(first + t * chips + tile * TILE, TILE), TILE)
            for c in range(groups):
                lanes = slice(c * LANES, (c + 1) * LANES)
                for half, ref in enumerate((x_ref, dy_ref)):
                    at = half * size // 2 + c * tok_dev + t
                    ref[rows, lanes] = wide_ref[pl.ds(at, TILE, stride=size)].astype(
                        jnp.bfloat16
                    )
        return carry

    tiles = chips // TILE
    if tiles == 1:
        step(0, 0)
    else:
        lax.fori_loop(0, tiles, step, 0)


def fetch_kernel(mine_ref, gate_hbm, gate_ref, x_ref, dy_ref, wide_ref, sems):
    copies = copy_pieces(gate_hbm, gate_ref, sems)
    for copy in copies:
        copy.start()
    lay_out(mine_ref, x_ref, dy_ref, wide_ref, 0)
    for copy in copies:
        copy.wait()


def fetch(mine, w_gate):
    chips, size, _ = mine.shape
    _, width, hidden = w_gate.shape
    half = chips * size * LANES // 2 // width
    moved = 2 * width * hidden
    return pl.pallas_call(
        fetch_kernel,
        out_shape=(
            pltpu.VMEM((width, hidden), jnp.bfloat16),
            pltpu.VMEM((half, width), jnp.bfloat16),
            pltpu.VMEM((half, width), jnp.bfloat16),
        ),
        in_specs=[VMEM, HBM],
        out_specs=(VMEM,) * 3,
        scratch_shapes=[
            pltpu.VMEM((TILE * size, LANES), jnp.float32),
            pltpu.SemaphoreType.DMA((PIECES,)),
        ],
        cost_estimate=pl.CostEstimate(flops=0, bytes_accessed=2 * moved, transcendentals=0),
        compiler_params=vmem((8 << 20) + 2 * moved + 8 * mine.size),
    )(mine, pltpu.with_memory_space_constraint(w_gate, pltpu.HBM))


def my_core():
    return lax.axis_index("dp") % CORES


def row_blocks(rows, step):
    step(0, True)
    if rows > ROWS:
        pl.loop(1, rows // ROWS)(lambda block: step(block, False))


def half_total(gate_delta, up_delta, gate_ref, up_ref, core):
    columns = gate_ref.shape[0] // CORES
    part = pl.ds(pl.multiple_of(core * columns, columns), columns)
    total = lax.dot_general(
        gate_delta, gate_ref[part], CONTRACT_LAST, preferred_element_type=jnp.float32
    )
    return total + lax.dot_general(
        up_delta, up_ref[part], CONTRACT_LAST, preferred_element_type=jnp.float32
    )


def store_groups(ref, block, total):
    rows, columns = total.shape
    groups = columns // LANES
    chips = lax.axis_size("expert") * lax.axis_size("dp") // CORES
    half = ref.shape[0] // groups // CORES
    tok_dev = half // chips
    for tile in range(rows // TILE):
        row = block * rows + tile * TILE
        token = row % half // chips
        device = row // half * chips + row % chips
        first = (device * tok_dev + token) * groups
        part = total[tile * TILE : (tile + 1) * TILE]
        for c in range(groups):
            ref[pl.ds(first + c, TILE, stride=tok_dev * groups)] = part[
                :, c * LANES : (c + 1) * LANES
            ]


def rows_kernel(
    other_ref, my_x_ref, my_dy_ref, gate_ref, up_hbm, down_hbm,
    sent_ref, up_ref, x_ref, dy_ref, gate_delta_ref, up_delta_ref, hidden_ref,
    down_ref, wide_ref, total_ref, sems,
):
    down_copies = copy_pieces(down_hbm, down_ref, sems.at[0])
    up_copies = copy_pieces(up_hbm, up_ref, sems.at[1])
    for copy in down_copies:
        copy.start()
    half = my_x_ref.shape[0]
    x_ref[:half] = my_x_ref[...]
    dy_ref[:half] = my_dy_ref[...]
    lay_out(other_ref, x_ref, dy_ref, wide_ref, half)
    depth = up_ref.shape[0] // PIECES

    def step(block, first):
        rows = pl.ds(pl.multiple_of(block * ROWS, ROWS), ROWS)
        x = x_ref[rows]
        pre_gate = jnp.dot(x, gate_ref[...], preferred_element_type=jnp.float32)
        sigmoid_gate = jax.nn.sigmoid(pre_gate)
        activated = pre_gate * sigmoid_gate
        slope = sigmoid_gate * (1.0 + pre_gate * (1.0 - sigmoid_gate))
        if first:
            for copy, later in zip(down_copies, up_copies):
                copy.wait()
                later.start()
        grad_hidden = lax.dot_general(
            dy_ref[rows], down_ref[...], CONTRACT_LAST, preferred_element_type=jnp.float32
        )
        pre_up = None
        for piece, copy in enumerate(up_copies):
            if first:
                copy.wait()
            part = slice(piece * depth, (piece + 1) * depth)
            product = jnp.dot(x[:, part], up_ref[part], preferred_element_type=jnp.float32)
            pre_up = product if pre_up is None else pre_up + product
        hidden_ref[rows] = (activated * pre_up).astype(jnp.bfloat16)
        gate_delta = (grad_hidden * pre_up * slope).astype(jnp.bfloat16)
        up_delta = (grad_hidden * activated).astype(jnp.bfloat16)
        gate_delta_ref[rows] = gate_delta
        up_delta_ref[rows] = up_delta
        total = half_total(gate_delta, up_delta, gate_ref, up_ref, 1 - my_core())
        store_groups(total_ref, block, total)

    row_blocks(x_ref.shape[0], step)
    sent_ref[...] = total_ref[...].astype(jnp.bfloat16)


def rows_pass(other, my_x, my_dy, gate, w_up, w_down):
    chips, size, _ = other.shape
    width, hidden = gate.shape
    rows = CORES * my_x.shape[0]
    groups = width // CORES // LANES
    bf16 = functools.partial(jax.ShapeDtypeStruct, dtype=jnp.bfloat16)
    moved = (3 * width * hidden + rows * (6 * width + 3 * hidden)) * 2
    up, down = (pltpu.with_memory_space_constraint(w, pltpu.HBM) for w in (w_up, w_down))
    return pl.pallas_call(
        rows_kernel,
        out_shape=(
            bf16((rows * groups, LANES)),
            pltpu.VMEM((width, hidden), jnp.bfloat16),
            bf16((rows, width)),
            bf16((rows, width)),
            bf16((rows, hidden)),
            bf16((rows, hidden)),
            bf16((rows, hidden)),
        ),
        in_specs=[VMEM] * 4 + [HBM] * 2,
        out_specs=(VMEM,) * 7,
        scratch_shapes=[
            pltpu.VMEM((hidden, width), jnp.bfloat16),
            pltpu.VMEM((TILE * size, LANES), jnp.float32),
            pltpu.VMEM((rows * groups, LANES), jnp.float32),
            pltpu.SemaphoreType.DMA((2, PIECES)),
        ],
        cost_estimate=pl.CostEstimate(
            flops=8 * rows * width * hidden, bytes_accessed=moved, transcendentals=rows * hidden
        ),
        compiler_params=vmem((12 << 20) + 2 * moved),
    )(other, my_x, my_dy, gate, up, down)


def finish_kernel(gate_delta_ref, up_delta_ref, gate_ref, up_ref, total_ref):
    def step(block, first):
        rows = pl.ds(pl.multiple_of(block * ROWS, ROWS), ROWS)
        total = half_total(
            gate_delta_ref[rows], up_delta_ref[rows], gate_ref, up_ref, my_core()
        )
        store_groups(total_ref, block, total)

    row_blocks(gate_delta_ref.shape[0], step)


def finish(gate_delta, up_delta, gate, up):
    rows, hidden = gate_delta.shape
    columns = gate.shape[0] // CORES
    moved = 4 * columns * hidden + 4 * rows * (columns + hidden)
    return pl.pallas_call(
        finish_kernel,
        out_shape=jax.ShapeDtypeStruct((rows * columns // LANES, LANES), jnp.float32),
        in_specs=[VMEM] * 4,
        out_specs=VMEM,
        cost_estimate=pl.CostEstimate(
            flops=4 * rows * columns * hidden, bytes_accessed=moved, transcendentals=0
        ),
        compiler_params=vmem((16 << 20) + 2 * moved),
    )(gate_delta, up_delta, gate, up)


def share_kernel(total_ref, got_ref, shares_ref):
    devices, size, _ = shares_ref.shape
    chips = devices // CORES
    core = my_core()

    def step(place, carry):
        here = pl.ds(pl.multiple_of(place * size, size), size)
        there = pl.ds(pl.multiple_of((place + chips) % devices * size, size), size)
        owner = jnp.where(place < chips, core, 1 - core)
        total = total_ref[here] + got_ref[there].astype(jnp.float32)
        shares_ref[chip_at(place % chips) * CORES + owner] = total.astype(jnp.bfloat16)
        return carry

    lax.fori_loop(0, devices, step, 0, unroll=devices <= 32)


def share(total, got, devices):
    size = total.shape[0] // devices
    return pl.pallas_call(
        share_kernel,
        out_shape=pltpu.VMEM((devices, size, LANES), jnp.bfloat16),
        in_specs=[VMEM] * 2,
        out_specs=VMEM,
        compiler_params=vmem((8 << 20) + 32 * total.size),
    )(total, got)


def sum_kernel(shares_ref, out_hbm, wide_ref, out_ref, sem):
    devices, size, _ = shares_ref.shape
    _, tok_dev, width = out_ref.shape
    groups = size // tok_dev
    for core in range(CORES):
        total = lax.fori_loop(
            0,
            devices // CORES,
            lambda i, acc: acc + shares_ref[i * CORES + core].astype(jnp.float32),
            jnp.zeros((size, LANES), jnp.float32),
            unroll=devices <= 32,
        )
        for row in range(size):
            token, lane = row // groups, (core * groups + row % groups) * LANES
            wide_ref[token : token + 1, lane : lane + LANES] = total[row : row + 1]
    out_ref[0] = wide_ref[...].astype(jnp.bfloat16)
    copy = pltpu.make_async_copy(out_ref, out_hbm, sem)
    copy.start()
    copy.wait()


def sum_shares(shares, tok_dev):
    _, size, _ = shares.shape
    width = CORES * size // tok_dev * LANES
    return pl.pallas_call(
        sum_kernel,
        out_shape=pltpu.HBM((1, tok_dev, width), jnp.bfloat16),
        in_specs=[VMEM],
        out_specs=HBM,
        scratch_shapes=[
            pltpu.VMEM((tok_dev, width), jnp.float32),
            pltpu.VMEM((1, tok_dev, width), jnp.bfloat16),
            pltpu.SemaphoreType.DMA,
        ],
        compiler_params=vmem(16 << 20),
    )(shares)


def local(tokens, out_grad, expert_ids, gate_scores, w_gate, w_up, w_down):
    devices = lax.axis_size("expert") * lax.axis_size("dp")
    chips = devices // CORES
    order = [chip_at(place) for place in range(chips)]
    same_core = [[chip * CORES + core for chip in order] for core in range(CORES)]
    core_pairs = [(d, d ^ 1) for d in range(devices)]
    copies = pack(tokens, out_grad, expert_ids, gate_scores, chips)
    mine = lax.all_to_all(copies, BOTH, 0, 0, axis_index_groups=same_core, tiled=True)
    other = lax.ppermute(mine, BOTH, core_pairs)
    gate, my_x, my_dy = fetch(mine, w_gate)
    sent, up, x, dy, gate_delta, up_delta, hidden = rows_pass(
        other, my_x, my_dy, gate, w_up, w_down
    )
    got = lax.ppermute(sent, BOTH, core_pairs)
    total = finish(gate_delta, up_delta, gate, up)
    shares = share(total, got, devices)
    shares, gate_delta, up_delta, hidden = lax.optimization_barrier(
        (shares, gate_delta, up_delta, hidden)
    )
    shares = lax.all_to_all(shares, BOTH, 0, 0, tiled=True)
    token_grad = sum_shares(shares, tokens.shape[1])
    grad_down = jnp.dot(hidden.T, dy, preferred_element_type=jnp.float32)
    grad_gate = jnp.dot(x.T, gate_delta, preferred_element_type=jnp.float32)
    grad_up = jnp.dot(x.T, up_delta, preferred_element_type=jnp.float32)
    weight_grads = (grad_gate, grad_up, grad_down)
    return (token_grad,) + tuple(g.astype(jnp.bfloat16)[None] for g in weight_grads)


def solution(mesh):
    return jax.shard_map(
        local,
        mesh=mesh,
        in_specs=(
            P("dp", "expert", None),
            P("dp", "expert", None),
            P("dp", None, None),
            P("dp", None, None),
            P("expert", None, "dp"),
            P("expert", None, "dp"),
            P("expert", "dp", None),
        ),
        out_specs=(
            P("dp", "expert", None),
            P("expert", None, "dp"),
            P("expert", None, "dp"),
            P("expert", "dp", None),
        ),
        check_vma=False,
    )
```

```python
import functools

import jax
import jax.numpy as jnp
from jax import lax
from jax.experimental import pallas as pl
from jax.experimental.pallas import tpu as pltpu
from jax.sharding import PartitionSpec as P

LANES = 128
CORES = 2
BOTH = ("expert", "dp")
ROWS = 64
TILE = 16
CONTRACT_LAST = (((1,), (1,)), ((), ()))
PIECES = 4
VMEM = pl.BlockSpec(memory_space=pltpu.VMEM)
HBM = pl.BlockSpec(memory_space=pltpu.HBM)


def vmem(size):
    return pltpu.CompilerParams(vmem_limit_bytes=min(size, 36 << 20))


def chip_at(place):
    experts = lax.axis_size("expert")
    per_expert = lax.axis_size("dp") // CORES
    upper = 1 - place % 2
    rank = place // 2 // experts
    within = per_expert // 2 + upper * rank - (1 - upper) * (1 + rank)
    return place // 2 % experts * per_expert + within


def pack_kernel(
    tokens_hbm, grad_hbm, ids_hbm, scores_hbm, out_ref,
    tokens_ref, grad_ref, ids_ref, scores_ref, weighted_ref, sems,
):
    copies = [
        pltpu.make_async_copy(src, dst, sems.at[i])
        for i, (src, dst) in enumerate((
            (ids_hbm, ids_ref),
            (scores_hbm, scores_ref),
            (tokens_hbm, tokens_ref),
            (grad_hbm, grad_ref),
        ))
    ]
    for copy in copies:
        copy.start()
    for copy in copies:
        copy.wait()
    chips, tok_dev, _ = out_ref.shape
    width = tokens_ref.shape[2]
    experts = lax.axis_size("expert")
    first = lax.axis_index("expert") * tok_dev
    ids = ids_ref[0]
    scores = scores_ref[0].astype(jnp.float32)
    token = lax.broadcasted_iota(jnp.int32, ids.shape, 1)
    lane = lax.broadcasted_iota(jnp.int32, (ids.shape[0], LANES), 1)
    row = lax.broadcasted_iota(jnp.int32, (tok_dev, LANES), 0)
    table = jnp.zeros((tok_dev, LANES), jnp.float32)
    for i in range(tok_dev):
        mine = token == first + i
        named = jnp.sum(jnp.where(mine, ids, 0), axis=1, keepdims=True)
        score = jnp.sum(jnp.where(mine, scores, 0.0), axis=1, keepdims=True)
        weights = jnp.sum(jnp.where(lane == named, score, 0.0), axis=0, keepdims=True)
        table = jnp.where(row == i, weights, table)
    grad = grad_ref[0].astype(jnp.float32)
    for expert in range(experts):
        weighted_ref[expert] = (grad * table[:, expert : expert + 1]).astype(jnp.bfloat16)

    def write(place, carry):
        out_ref[place, :, :width] = tokens_ref[0]
        out_ref[place, :, width:] = weighted_ref[chip_at(place) // (chips // experts)]
        return carry

    lax.fori_loop(0, chips, write, 0, unroll=chips <= 16)


def pack(tokens, out_grad, expert_ids, gate_scores, chips):
    _, tok_dev, width = tokens.shape
    operands = [
        pltpu.with_memory_space_constraint(a, pltpu.HBM)
        for a in (
            tokens, out_grad, jnp.swapaxes(expert_ids, 1, 2), jnp.swapaxes(gate_scores, 1, 2)
        )
    ]
    return pl.pallas_call(
        pack_kernel,
        out_shape=jax.ShapeDtypeStruct((chips, tok_dev, 2 * width), jnp.bfloat16),
        in_specs=[HBM] * 4,
        out_specs=VMEM,
        scratch_shapes=[pltpu.VMEM(a.shape, a.dtype) for a in operands]
        + [
            pltpu.VMEM((lax.axis_size("expert"), tok_dev, width), jnp.bfloat16),
            pltpu.SemaphoreType.DMA((4,)),
        ],
        compiler_params=vmem(16 << 20),
    )(*operands)


def copy_pieces(src, dst, sems):
    rows = dst.shape[0] // PIECES
    parts = [pl.ds(piece * rows, rows) for piece in range(PIECES)]
    copies = [
        pltpu.make_async_copy(src.at[0, part], dst.at[part], sems.at[piece])
        for piece, part in enumerate(parts)
    ]
    for copy in copies:
        copy.start()
    return copies


def lay_out(src_ref, x_ref, dy_ref, first):
    chips, tok_dev, _ = src_ref.shape
    width = x_ref.shape[1]
    per_tile = TILE // tok_dev

    def step(tile, carry):
        rows = pl.ds(pl.multiple_of(first + tile * TILE, TILE), TILE)
        blocks = [src_ref[tile * per_tile + j] for j in range(per_tile)]
        x_ref[rows] = jnp.concatenate([b[:, :width] for b in blocks], axis=0)
        dy_ref[rows] = jnp.concatenate([b[:, width:] for b in blocks], axis=0)
        return carry

    tiles = chips // per_tile
    lax.fori_loop(0, tiles, step, 0, unroll=tiles <= 2)


def fetch_kernel(mine_ref, gate_hbm, gate_ref, x_ref, dy_ref, sems):
    copies = copy_pieces(gate_hbm, gate_ref, sems)
    lay_out(mine_ref, x_ref, dy_ref, 0)
    for copy in copies:
        copy.wait()


def fetch(mine, w_gate):
    chips, tok_dev, row = mine.shape
    _, width, hidden = w_gate.shape
    half = chips * tok_dev
    moved = 2 * width * hidden
    return pl.pallas_call(
        fetch_kernel,
        out_shape=(
            pltpu.VMEM((width, hidden), jnp.bfloat16),
            pltpu.VMEM((half, width), jnp.bfloat16),
            pltpu.VMEM((half, width), jnp.bfloat16),
        ),
        in_specs=[VMEM, HBM],
        out_specs=(VMEM,) * 3,
        scratch_shapes=[pltpu.SemaphoreType.DMA((PIECES,))],
        cost_estimate=pl.CostEstimate(flops=0, bytes_accessed=2 * moved, transcendentals=0),
        compiler_params=vmem((8 << 20) + 2 * moved + 8 * half * row),
    )(mine, pltpu.with_memory_space_constraint(w_gate, pltpu.HBM))


def my_core():
    return lax.axis_index("dp") % CORES


def row_blocks(rows, step):
    step(0, True)
    if rows > ROWS:
        pl.loop(1, rows // ROWS)(lambda block: step(block, False))


def half_total(gate_delta, up_delta, gate_ref, up_ref, core):
    columns = gate_ref.shape[0] // CORES
    part = pl.ds(pl.multiple_of(core * columns, columns), columns)
    total = lax.dot_general(
        gate_delta, gate_ref[part], CONTRACT_LAST, preferred_element_type=jnp.float32
    )
    return total + lax.dot_general(
        up_delta, up_ref[part], CONTRACT_LAST, preferred_element_type=jnp.float32
    )


def store_groups(ref, first, total):
    rows, columns = total.shape
    groups = columns // LANES
    for c in range(groups):
        ref[pl.ds(first + c, rows, stride=groups)] = total[:, c * LANES : (c + 1) * LANES]


def rows_kernel(
    other_ref, my_x_ref, my_dy_ref, gate_ref, up_hbm, down_hbm,
    sent_ref, up_ref, x_ref, dy_ref, gate_delta_ref, up_delta_ref, hidden_ref,
    down_ref, total_ref, sems,
):
    down_copies = copy_pieces(down_hbm, down_ref, sems.at[0])
    up_copies = copy_pieces(up_hbm, up_ref, sems.at[1])
    half = my_x_ref.shape[0]
    x_ref[:half] = my_x_ref[...]
    dy_ref[:half] = my_dy_ref[...]
    x_ref[half:] = other_ref[:, : x_ref.shape[1]]
    dy_ref[half:] = other_ref[:, x_ref.shape[1] :]
    depth = up_ref.shape[0] // PIECES

    def step(block, first):
        rows = pl.ds(pl.multiple_of(block * ROWS, ROWS), ROWS)
        x = x_ref[rows]
        pre_gate = jnp.dot(x, gate_ref[...], preferred_element_type=jnp.float32)
        sigmoid_gate = jax.nn.sigmoid(pre_gate)
        activated = pre_gate * sigmoid_gate
        slope = sigmoid_gate * (1.0 + pre_gate * (1.0 - sigmoid_gate))
        if first:
            for copy in down_copies:
                copy.wait()
        grad_hidden = lax.dot_general(
            dy_ref[rows], down_ref[...], CONTRACT_LAST, preferred_element_type=jnp.float32
        )
        pre_up = None
        for piece, copy in enumerate(up_copies):
            if first:
                copy.wait()
            part = slice(piece * depth, (piece + 1) * depth)
            product = jnp.dot(x[:, part], up_ref[part], preferred_element_type=jnp.float32)
            pre_up = product if pre_up is None else pre_up + product
        hidden_ref[rows] = (activated * pre_up).astype(jnp.bfloat16)
        gate_delta = (grad_hidden * pre_up * slope).astype(jnp.bfloat16)
        up_delta = (grad_hidden * activated).astype(jnp.bfloat16)
        gate_delta_ref[rows] = gate_delta
        up_delta_ref[rows] = up_delta
        total = half_total(gate_delta, up_delta, gate_ref, up_ref, 1 - my_core())
        store_groups(total_ref, 0, total)
        size = total_ref.shape[0]
        part = pl.ds(pl.multiple_of(block * size, size), size)
        sent_ref[part] = total_ref[...].astype(jnp.bfloat16)

    row_blocks(x_ref.shape[0], step)


def rows_pass(other, my_x, my_dy, gate, w_up, w_down):
    width, hidden = gate.shape
    rows = CORES * other.shape[0]
    groups = width // CORES // LANES
    bf16 = functools.partial(jax.ShapeDtypeStruct, dtype=jnp.bfloat16)
    moved = (3 * width * hidden + rows * (6 * width + 3 * hidden)) * 2
    up, down = (pltpu.with_memory_space_constraint(w, pltpu.HBM) for w in (w_up, w_down))
    return pl.pallas_call(
        rows_kernel,
        out_shape=(
            bf16((rows * groups, LANES)),
            pltpu.VMEM((width, hidden), jnp.bfloat16),
            bf16((rows, width)),
            bf16((rows, width)),
            bf16((rows, hidden)),
            bf16((rows, hidden)),
            bf16((rows, hidden)),
        ),
        in_specs=[VMEM] * 4 + [HBM] * 2,
        out_specs=(VMEM,) * 7,
        scratch_shapes=[
            pltpu.VMEM((hidden, width), jnp.bfloat16),
            pltpu.VMEM((ROWS * groups, LANES), jnp.float32),
            pltpu.SemaphoreType.DMA((2, PIECES)),
        ],
        cost_estimate=pl.CostEstimate(
            flops=8 * rows * width * hidden, bytes_accessed=moved, transcendentals=rows * hidden
        ),
        compiler_params=vmem((12 << 20) + 2 * moved),
    )(other, my_x, my_dy, gate, up, down)


def finish_kernel(gate_delta_ref, up_delta_ref, gate_ref, up_ref, total_ref):
    rows_all = gate_delta_ref.shape[0]
    size = total_ref.shape[0] // rows_all * ROWS

    def step(block, first):
        rows = pl.ds(pl.multiple_of(block * ROWS, ROWS), ROWS)
        total = half_total(
            gate_delta_ref[rows], up_delta_ref[rows], gate_ref, up_ref, my_core()
        )
        store_groups(total_ref, block * size, total)

    row_blocks(rows_all, step)


def finish(gate_delta, up_delta, gate, up):
    rows, hidden = gate_delta.shape
    columns = gate.shape[0] // CORES
    moved = 4 * columns * hidden + 4 * rows * (columns + hidden)
    return pl.pallas_call(
        finish_kernel,
        out_shape=jax.ShapeDtypeStruct((rows * columns // LANES, LANES), jnp.float32),
        in_specs=[VMEM] * 4,
        out_specs=VMEM,
        cost_estimate=pl.CostEstimate(
            flops=4 * rows * columns * hidden, bytes_accessed=moved, transcendentals=0
        ),
        compiler_params=vmem((16 << 20) + 2 * moved),
    )(gate_delta, up_delta, gate, up)


def share_kernel(total_ref, got_ref, shares_ref):
    devices, size, _ = shares_ref.shape
    chips = devices // CORES
    core = my_core()

    def step(place, carry):
        here = pl.ds(pl.multiple_of(place * size, size), size)
        there = pl.ds(pl.multiple_of((place + chips) % devices * size, size), size)
        owner = jnp.where(place < chips, core, 1 - core)
        total = total_ref[here] + got_ref[there].astype(jnp.float32)
        shares_ref[chip_at(place % chips) * CORES + owner] = total.astype(jnp.bfloat16)
        return carry

    lax.fori_loop(0, devices, step, 0, unroll=devices <= 32)


def share(total, got, devices):
    size = total.shape[0] // devices
    return pl.pallas_call(
        share_kernel,
        out_shape=pltpu.VMEM((devices, size, LANES), jnp.bfloat16),
        in_specs=[VMEM] * 2,
        out_specs=VMEM,
        compiler_params=vmem((8 << 20) + 32 * total.size),
    )(total, got)


def sum_kernel(shares_ref, out_hbm, wide_ref, out_ref, sem):
    devices, size, _ = shares_ref.shape
    _, tok_dev, width = out_ref.shape
    groups = size // tok_dev
    for core in range(CORES):
        total = lax.fori_loop(
            0,
            devices // CORES,
            lambda i, acc: acc + shares_ref[i * CORES + core].astype(jnp.float32),
            jnp.zeros((size, LANES), jnp.float32),
            unroll=devices <= 32,
        )
        for row in range(size):
            token, lane = row // groups, (core * groups + row % groups) * LANES
            wide_ref[token : token + 1, lane : lane + LANES] = total[row : row + 1]
    out_ref[0] = wide_ref[...].astype(jnp.bfloat16)
    copy = pltpu.make_async_copy(out_ref, out_hbm, sem)
    copy.start()
    copy.wait()


def sum_shares(shares, tok_dev):
    _, size, _ = shares.shape
    width = CORES * size // tok_dev * LANES
    return pl.pallas_call(
        sum_kernel,
        out_shape=pltpu.HBM((1, tok_dev, width), jnp.bfloat16),
        in_specs=[VMEM],
        out_specs=HBM,
        scratch_shapes=[
            pltpu.VMEM((tok_dev, width), jnp.float32),
            pltpu.VMEM((1, tok_dev, width), jnp.bfloat16),
            pltpu.SemaphoreType.DMA,
        ],
        compiler_params=vmem(16 << 20),
    )(shares)


def local(tokens, out_grad, expert_ids, gate_scores, w_gate, w_up, w_down):
    devices = lax.axis_size("expert") * lax.axis_size("dp")
    chips = devices // CORES
    order = [chip_at(place) for place in range(chips)]
    same_core = [[chip * CORES + core for chip in order] for core in range(CORES)]
    core_pairs = [(d, d ^ 1) for d in range(devices)]
    copies = pack(tokens, out_grad, expert_ids, gate_scores, chips)
    mine = lax.all_to_all(copies, BOTH, 0, 0, axis_index_groups=same_core, tiled=True)
    other = lax.ppermute(mine, BOTH, core_pairs)
    gate, my_x, my_dy = fetch(mine, w_gate)
    sent, up, x, dy, gate_delta, up_delta, hidden = rows_pass(
        other.reshape(my_x.shape[0], -1), my_x, my_dy, gate, w_up, w_down
    )
    got = lax.ppermute(sent, BOTH, core_pairs)
    total = finish(gate_delta, up_delta, gate, up)
    shares = share(total, got, devices)
    shares, gate_delta, up_delta, hidden = lax.optimization_barrier(
        (shares, gate_delta, up_delta, hidden)
    )
    shares = lax.all_to_all(shares, BOTH, 0, 0, tiled=True)
    token_grad = sum_shares(shares, tokens.shape[1])
    grad_down = jnp.dot(hidden.T, dy, preferred_element_type=jnp.float32)
    grad_gate = jnp.dot(x.T, gate_delta, preferred_element_type=jnp.float32)
    grad_up = jnp.dot(x.T, up_delta, preferred_element_type=jnp.float32)
    weight_grads = (grad_gate, grad_up, grad_down)
    return (token_grad,) + tuple(g.astype(jnp.bfloat16)[None] for g in weight_grads)


def solution(mesh):
    return jax.shard_map(
        local,
        mesh=mesh,
        in_specs=(
            P("dp", "expert", None),
            P("dp", "expert", None),
            P("dp", None, None),
            P("dp", None, None),
            P("expert", None, "dp"),
            P("expert", None, "dp"),
            P("expert", "dp", None),
        ),
        out_specs=(
            P("dp", "expert", None),
            P("expert", None, "dp"),
            P("expert", None, "dp"),
            P("expert", "dp", None),
        ),
        check_vma=False,
    )
```

```python
import functools

import jax
import jax.numpy as jnp
from jax import lax
from jax.experimental import pallas as pl
from jax.experimental.pallas import tpu as pltpu
from jax.sharding import PartitionSpec as P

LANES = 128
CORES = 2
BOTH = ("expert", "dp")
ROWS = 64
TILE = 16
CONTRACT_LAST = (((1,), (1,)), ((), ()))
PIECES = 4
VMEM = pl.BlockSpec(memory_space=pltpu.VMEM)
HBM = pl.BlockSpec(memory_space=pltpu.HBM)


def vmem(size):
    return pltpu.CompilerParams(vmem_limit_bytes=min(size, 36 << 20))


def chip_at(place):
    return lax.axis_size("expert") * lax.axis_size("dp") // CORES - 1 - place


def pack_kernel(
    tokens_hbm, grad_hbm, ids_hbm, scores_hbm, out_ref,
    tokens_ref, grad_ref, ids_ref, scores_ref, weighted_ref, sems,
):
    copies = [
        pltpu.make_async_copy(src, dst, sems.at[i])
        for i, (src, dst) in enumerate((
            (ids_hbm, ids_ref),
            (scores_hbm, scores_ref),
            (tokens_hbm, tokens_ref),
            (grad_hbm, grad_ref),
        ))
    ]
    for copy in copies:
        copy.start()
    for copy in copies:
        copy.wait()
    chips, tok_dev, _ = out_ref.shape
    width = tokens_ref.shape[2]
    experts = lax.axis_size("expert")
    first = lax.axis_index("expert") * tok_dev
    ids = ids_ref[0]
    scores = scores_ref[0].astype(jnp.float32)
    token = lax.broadcasted_iota(jnp.int32, ids.shape, 1)
    lane = lax.broadcasted_iota(jnp.int32, (ids.shape[0], LANES), 1)
    row = lax.broadcasted_iota(jnp.int32, (tok_dev, LANES), 0)
    table = jnp.zeros((tok_dev, LANES), jnp.float32)
    for i in range(tok_dev):
        mine = token == first + i
        named = jnp.sum(jnp.where(mine, ids, 0), axis=1, keepdims=True)
        score = jnp.sum(jnp.where(mine, scores, 0.0), axis=1, keepdims=True)
        weights = jnp.sum(jnp.where(lane == named, score, 0.0), axis=0, keepdims=True)
        table = jnp.where(row == i, weights, table)
    grad = grad_ref[0].astype(jnp.float32)
    for expert in range(experts):
        weighted_ref[expert] = (grad * table[:, expert : expert + 1]).astype(jnp.bfloat16)

    def write(place, carry):
        out_ref[place, :, :width] = tokens_ref[0]
        out_ref[place, :, width:] = weighted_ref[chip_at(place) // (chips // experts)]
        return carry

    lax.fori_loop(0, chips, write, 0, unroll=chips <= 16)


def pack(tokens, out_grad, expert_ids, gate_scores, chips):
    _, tok_dev, width = tokens.shape
    operands = [
        pltpu.with_memory_space_constraint(a, pltpu.HBM)
        for a in (
            tokens, out_grad, jnp.swapaxes(expert_ids, 1, 2), jnp.swapaxes(gate_scores, 1, 2)
        )
    ]
    return pl.pallas_call(
        pack_kernel,
        out_shape=jax.ShapeDtypeStruct((chips, tok_dev, 2 * width), jnp.bfloat16),
        in_specs=[HBM] * 4,
        out_specs=VMEM,
        scratch_shapes=[pltpu.VMEM(a.shape, a.dtype) for a in operands]
        + [
            pltpu.VMEM((lax.axis_size("expert"), tok_dev, width), jnp.bfloat16),
            pltpu.SemaphoreType.DMA((4,)),
        ],
        compiler_params=vmem(16 << 20),
    )(*operands)


def copy_pieces(src, dst, sems):
    rows = dst.shape[0] // PIECES
    parts = [pl.ds(piece * rows, rows) for piece in range(PIECES)]
    copies = [
        pltpu.make_async_copy(src.at[0, part], dst.at[part], sems.at[piece])
        for piece, part in enumerate(parts)
    ]
    for copy in copies:
        copy.start()
    return copies


def lay_out(src_ref, x_ref, dy_ref, first):
    chips, tok_dev, _ = src_ref.shape
    width = x_ref.shape[1]
    per_tile = TILE // tok_dev

    def step(tile, carry):
        rows = pl.ds(pl.multiple_of(first + tile * TILE, TILE), TILE)
        blocks = [src_ref[tile * per_tile + j] for j in range(per_tile)]
        x_ref[rows] = jnp.concatenate([b[:, :width] for b in blocks], axis=0)
        dy_ref[rows] = jnp.concatenate([b[:, width:] for b in blocks], axis=0)
        return carry

    tiles = chips // per_tile
    lax.fori_loop(0, tiles, step, 0, unroll=tiles <= 2)


def fetch_kernel(mine_ref, gate_hbm, gate_ref, x_ref, dy_ref, sems):
    copies = copy_pieces(gate_hbm, gate_ref, sems)
    lay_out(mine_ref, x_ref, dy_ref, 0)
    for copy in copies:
        copy.wait()


def fetch(mine, w_gate):
    chips, tok_dev, row = mine.shape
    _, width, hidden = w_gate.shape
    half = chips * tok_dev
    moved = 2 * width * hidden
    return pl.pallas_call(
        fetch_kernel,
        out_shape=(
            pltpu.VMEM((width, hidden), jnp.bfloat16),
            pltpu.VMEM((half, width), jnp.bfloat16),
            pltpu.VMEM((half, width), jnp.bfloat16),
        ),
        in_specs=[VMEM, HBM],
        out_specs=(VMEM,) * 3,
        scratch_shapes=[pltpu.SemaphoreType.DMA((PIECES,))],
        cost_estimate=pl.CostEstimate(flops=0, bytes_accessed=2 * moved, transcendentals=0),
        compiler_params=vmem((8 << 20) + 2 * moved + 8 * half * row),
    )(mine, pltpu.with_memory_space_constraint(w_gate, pltpu.HBM))


def my_core():
    return lax.axis_index("dp") % CORES


def row_blocks(rows, step):
    step(0, True)
    if rows > ROWS:
        pl.loop(1, rows // ROWS)(lambda block: step(block, False))


def half_total(gate_delta, up_delta, gate_ref, up_ref, core):
    columns = gate_ref.shape[0] // CORES
    part = pl.ds(pl.multiple_of(core * columns, columns), columns)
    total = lax.dot_general(
        gate_delta, gate_ref[part], CONTRACT_LAST, preferred_element_type=jnp.float32
    )
    return total + lax.dot_general(
        up_delta, up_ref[part], CONTRACT_LAST, preferred_element_type=jnp.float32
    )


def store_groups(ref, first, total):
    rows, columns = total.shape
    groups = columns // LANES
    for c in range(groups):
        ref[pl.ds(first + c, rows, stride=groups)] = total[:, c * LANES : (c + 1) * LANES]


def rows_kernel(
    other_ref, my_x_ref, my_dy_ref, gate_ref, up_hbm, down_hbm,
    sent_ref, up_ref, x_ref, dy_ref, gate_delta_ref, up_delta_ref, hidden_ref,
    down_ref, total_ref, sems,
):
    up_copies = copy_pieces(up_hbm, up_ref, sems.at[0])
    down_copies = copy_pieces(down_hbm, down_ref, sems.at[1])
    half = my_x_ref.shape[0]
    x_ref[:half] = my_x_ref[...]
    dy_ref[:half] = my_dy_ref[...]
    lay_out(other_ref, x_ref, dy_ref, half)
    depth = up_ref.shape[0] // PIECES

    def step(block, first):
        rows = pl.ds(pl.multiple_of(block * ROWS, ROWS), ROWS)
        x = x_ref[rows]
        pre_gate = jnp.dot(x, gate_ref[...], preferred_element_type=jnp.float32)
        sigmoid_gate = jax.nn.sigmoid(pre_gate)
        activated = pre_gate * sigmoid_gate
        pre_up = None
        for piece, copy in enumerate(up_copies):
            if first:
                copy.wait()
            part = slice(piece * depth, (piece + 1) * depth)
            product = jnp.dot(x[:, part], up_ref[part], preferred_element_type=jnp.float32)
            pre_up = product if pre_up is None else pre_up + product
        hidden_ref[rows] = (activated * pre_up).astype(jnp.bfloat16)
        if first:
            for copy in down_copies:
                copy.wait()
        grad_hidden = lax.dot_general(
            dy_ref[rows], down_ref[...], CONTRACT_LAST, preferred_element_type=jnp.float32
        )
        gate_delta = (
            grad_hidden * pre_up * sigmoid_gate * (1.0 + pre_gate * (1.0 - sigmoid_gate))
        ).astype(jnp.bfloat16)
        up_delta = (grad_hidden * activated).astype(jnp.bfloat16)
        gate_delta_ref[rows] = gate_delta
        up_delta_ref[rows] = up_delta
        total = half_total(gate_delta, up_delta, gate_ref, up_ref, 1 - my_core())
        store_groups(total_ref, 0, total)
        size = total_ref.shape[0]
        part = pl.ds(pl.multiple_of(block * size, size), size)
        sent_ref[part] = total_ref[...].astype(jnp.bfloat16)

    row_blocks(x_ref.shape[0], step)


def rows_pass(other, my_x, my_dy, gate, w_up, w_down):
    chips, tok_dev, row = other.shape
    width, hidden = gate.shape
    rows = 2 * chips * tok_dev
    groups = width // CORES // LANES
    bf16 = functools.partial(jax.ShapeDtypeStruct, dtype=jnp.bfloat16)
    moved = (3 * width * hidden + rows * (6 * width + 3 * hidden)) * 2
    up, down = (pltpu.with_memory_space_constraint(w, pltpu.HBM) for w in (w_up, w_down))
    return pl.pallas_call(
        rows_kernel,
        out_shape=(
            bf16((rows * groups, LANES)),
            pltpu.VMEM((width, hidden), jnp.bfloat16),
            bf16((rows, width)),
            bf16((rows, width)),
            bf16((rows, hidden)),
            bf16((rows, hidden)),
            bf16((rows, hidden)),
        ),
        in_specs=[VMEM] * 4 + [HBM] * 2,
        out_specs=(VMEM,) * 7,
        scratch_shapes=[
            pltpu.VMEM((hidden, width), jnp.bfloat16),
            pltpu.VMEM((ROWS * groups, LANES), jnp.float32),
            pltpu.SemaphoreType.DMA((2, PIECES)),
        ],
        cost_estimate=pl.CostEstimate(
            flops=8 * rows * width * hidden, bytes_accessed=moved, transcendentals=rows * hidden
        ),
        compiler_params=vmem((12 << 20) + 2 * moved),
    )(other, my_x, my_dy, gate, up, down)


def finish_kernel(gate_delta_ref, up_delta_ref, gate_ref, up_ref, total_ref):
    rows_all = gate_delta_ref.shape[0]
    size = total_ref.shape[0] // rows_all * ROWS

    def step(block, first):
        rows = pl.ds(pl.multiple_of(block * ROWS, ROWS), ROWS)
        total = half_total(
            gate_delta_ref[rows], up_delta_ref[rows], gate_ref, up_ref, my_core()
        )
        store_groups(total_ref, block * size, total)

    row_blocks(rows_all, step)


def finish(gate_delta, up_delta, gate, up):
    rows, hidden = gate_delta.shape
    columns = gate.shape[0] // CORES
    moved = 4 * columns * hidden + 4 * rows * (columns + hidden)
    return pl.pallas_call(
        finish_kernel,
        out_shape=jax.ShapeDtypeStruct((rows * columns // LANES, LANES), jnp.float32),
        in_specs=[VMEM] * 4,
        out_specs=VMEM,
        cost_estimate=pl.CostEstimate(
            flops=4 * rows * columns * hidden, bytes_accessed=moved, transcendentals=0
        ),
        compiler_params=vmem((16 << 20) + 2 * moved),
    )(gate_delta, up_delta, gate, up)


def share_kernel(total_ref, got_ref, shares_ref):
    devices, size, _ = shares_ref.shape
    chips = devices // CORES
    core = my_core()

    def step(place, carry):
        here = pl.ds(pl.multiple_of(place * size, size), size)
        there = pl.ds(pl.multiple_of((place + chips) % devices * size, size), size)
        owner = jnp.where(place < chips, core, 1 - core)
        total = total_ref[here] + got_ref[there].astype(jnp.float32)
        shares_ref[place % chips * CORES + owner] = total.astype(jnp.bfloat16)
        return carry

    lax.fori_loop(0, devices, step, 0, unroll=devices <= 32)


def share(total, got, devices):
    size = total.shape[0] // devices
    return pl.pallas_call(
        share_kernel,
        out_shape=pltpu.VMEM((devices, size, LANES), jnp.bfloat16),
        in_specs=[VMEM] * 2,
        out_specs=VMEM,
        compiler_params=vmem((8 << 20) + 32 * total.size),
    )(total, got)


def sum_kernel(shares_ref, out_hbm, wide_ref, out_ref, sem):
    devices, size, _ = shares_ref.shape
    _, tok_dev, width = out_ref.shape
    groups = size // tok_dev
    for core in range(CORES):
        total = lax.fori_loop(
            0,
            devices // CORES,
            lambda i, acc: acc + shares_ref[i * CORES + core].astype(jnp.float32),
            jnp.zeros((size, LANES), jnp.float32),
            unroll=devices <= 32,
        )
        for row in range(size):
            token, lane = row // groups, (core * groups + row % groups) * LANES
            wide_ref[token : token + 1, lane : lane + LANES] = total[row : row + 1]
    out_ref[0] = wide_ref[...].astype(jnp.bfloat16)
    copy = pltpu.make_async_copy(out_ref, out_hbm, sem)
    copy.start()
    copy.wait()


def sum_shares(shares, tok_dev):
    _, size, _ = shares.shape
    width = CORES * size // tok_dev * LANES
    return pl.pallas_call(
        sum_kernel,
        out_shape=pltpu.HBM((1, tok_dev, width), jnp.bfloat16),
        in_specs=[VMEM],
        out_specs=HBM,
        scratch_shapes=[
            pltpu.VMEM((tok_dev, width), jnp.float32),
            pltpu.VMEM((1, tok_dev, width), jnp.bfloat16),
            pltpu.SemaphoreType.DMA,
        ],
        compiler_params=vmem(16 << 20),
    )(shares)


def local(tokens, out_grad, expert_ids, gate_scores, w_gate, w_up, w_down):
    devices = lax.axis_size("expert") * lax.axis_size("dp")
    chips = devices // CORES
    order = [chip_at(place) for place in range(chips)]
    same_core = [[chip * CORES + core for chip in order] for core in range(CORES)]
    everyone = [[chip * CORES + core for chip in order for core in range(CORES)]]
    core_pairs = [(d, d ^ 1) for d in range(devices)]
    copies = pack(tokens, out_grad, expert_ids, gate_scores, chips)
    mine = lax.all_to_all(copies, BOTH, 0, 0, axis_index_groups=same_core, tiled=True)
    other = lax.ppermute(mine, BOTH, core_pairs)
    gate, my_x, my_dy = fetch(mine, w_gate)
    sent, up, x, dy, gate_delta, up_delta, hidden = rows_pass(
        other, my_x, my_dy, gate, w_up, w_down
    )
    got = lax.ppermute(sent, BOTH, core_pairs)
    total = finish(gate_delta, up_delta, gate, up)
    shares = share(total, got, devices)
    shares, gate_delta, up_delta, hidden = lax.optimization_barrier(
        (shares, gate_delta, up_delta, hidden)
    )
    shares = lax.all_to_all(shares, BOTH, 0, 0, axis_index_groups=everyone, tiled=True)
    token_grad = sum_shares(shares, tokens.shape[1])
    grad_down = jnp.dot(hidden.T, dy, preferred_element_type=jnp.float32)
    grad_gate = jnp.dot(x.T, gate_delta, preferred_element_type=jnp.float32)
    grad_up = jnp.dot(x.T, up_delta, preferred_element_type=jnp.float32)
    weight_grads = (grad_gate, grad_up, grad_down)
    return (token_grad,) + tuple(g.astype(jnp.bfloat16)[None] for g in weight_grads)


def solution(mesh):
    return jax.shard_map(
        local,
        mesh=mesh,
        in_specs=(
            P("dp", "expert", None),
            P("dp", "expert", None),
            P("dp", None, None),
            P("dp", None, None),
            P("expert", None, "dp"),
            P("expert", None, "dp"),
            P("expert", "dp", None),
        ),
        out_specs=(
            P("dp", "expert", None),
            P("expert", None, "dp"),
            P("expert", None, "dp"),
            P("expert", "dp", None),
        ),
        check_vma=False,
    )
```

```python
import functools

import jax
import jax.numpy as jnp
from jax import lax
from jax.experimental import pallas as pl
from jax.experimental.pallas import tpu as pltpu
from jax.sharding import PartitionSpec as P

LANES = 128
CORES = 2
BOTH = ("expert", "dp")
ROWS = 64
TILE = 16
CONTRACT_LAST = (((1,), (1,)), ((), ()))
PIECES = 4
VMEM = pl.BlockSpec(memory_space=pltpu.VMEM)
HBM = pl.BlockSpec(memory_space=pltpu.HBM)


def vmem(size):
    return pltpu.CompilerParams(vmem_limit_bytes=min(size, 36 << 20))


def sizes():
    dp = lax.axis_size("dp")
    along_y = 1
    while (2 * along_y) ** 2 <= dp // CORES:
        along_y *= 2
    return lax.axis_size("expert"), dp // CORES // along_y, along_y, CORES


def device_at(expert, z, y, core):
    _, along_z, along_y, _ = sizes()
    return ((expert * along_z + z) * along_y + y) * CORES + core


def place_at(place):
    experts, along_z, _, _ = sizes()
    return place % experts, (place // experts + along_z // 2) % along_z


def my_y():
    return lax.axis_index("dp") // CORES % sizes()[2]


def pack_kernel(
    tokens_hbm, grad_hbm, ids_hbm, scores_hbm, out_ref,
    tokens_ref, grad_ref, ids_ref, scores_ref, weighted_ref, sems,
):
    copies = [
        pltpu.make_async_copy(src, dst, sems.at[i])
        for i, (src, dst) in enumerate((
            (ids_hbm, ids_ref),
            (scores_hbm, scores_ref),
            (tokens_hbm, tokens_ref),
            (grad_hbm, grad_ref),
        ))
    ]
    for copy in copies:
        copy.start()
    for copy in copies:
        copy.wait()
    places, tok_dev, _ = out_ref.shape
    width = tokens_ref.shape[2]
    experts = lax.axis_size("expert")
    first = lax.axis_index("expert") * tok_dev
    ids = ids_ref[0]
    scores = scores_ref[0].astype(jnp.float32)
    token = lax.broadcasted_iota(jnp.int32, ids.shape, 1)
    lane = lax.broadcasted_iota(jnp.int32, (ids.shape[0], LANES), 1)
    row = lax.broadcasted_iota(jnp.int32, (tok_dev, LANES), 0)
    table = jnp.zeros((tok_dev, LANES), jnp.float32)
    for i in range(tok_dev):
        mine = token == first + i
        named = jnp.sum(jnp.where(mine, ids, 0), axis=1, keepdims=True)
        score = jnp.sum(jnp.where(mine, scores, 0.0), axis=1, keepdims=True)
        weights = jnp.sum(jnp.where(lane == named, score, 0.0), axis=0, keepdims=True)
        table = jnp.where(row == i, weights, table)
    grad = grad_ref[0].astype(jnp.float32)
    for expert in range(experts):
        weighted_ref[expert] = (grad * table[:, expert : expert + 1]).astype(jnp.bfloat16)

    def write(place, carry):
        out_ref[place, :, :width] = tokens_ref[0]
        out_ref[place, :, width:] = weighted_ref[place_at(place)[0]]
        return carry

    lax.fori_loop(0, places, write, 0, unroll=places <= 16)


def pack(tokens, out_grad, expert_ids, gate_scores, places):
    _, tok_dev, width = tokens.shape
    operands = [
        pltpu.with_memory_space_constraint(a, pltpu.HBM)
        for a in (
            tokens, out_grad, jnp.swapaxes(expert_ids, 1, 2), jnp.swapaxes(gate_scores, 1, 2)
        )
    ]
    return pl.pallas_call(
        pack_kernel,
        out_shape=jax.ShapeDtypeStruct((places, tok_dev, 2 * width), jnp.bfloat16),
        in_specs=[HBM] * 4,
        out_specs=VMEM,
        scratch_shapes=[pltpu.VMEM(a.shape, a.dtype) for a in operands]
        + [
            pltpu.VMEM((lax.axis_size("expert"), tok_dev, width), jnp.bfloat16),
            pltpu.SemaphoreType.DMA((4,)),
        ],
        compiler_params=vmem(16 << 20),
    )(*operands)


def copy_pieces(src, dst, sems):
    rows = dst.shape[0] // PIECES
    parts = [pl.ds(piece * rows, rows) for piece in range(PIECES)]
    return [
        pltpu.make_async_copy(src.at[0, part], dst.at[part], sems.at[piece])
        for piece, part in enumerate(parts)
    ]


def lay_out(src_ref, x_ref, dy_ref, first):
    chips, tok_dev, _ = src_ref.shape
    width = x_ref.shape[1]
    per_tile = TILE // tok_dev

    def step(tile, carry):
        rows = pl.ds(pl.multiple_of(first + tile * TILE, TILE), TILE)
        blocks = [src_ref[tile * per_tile + j] for j in range(per_tile)]
        x_ref[rows] = jnp.concatenate([b[:, :width] for b in blocks], axis=0)
        dy_ref[rows] = jnp.concatenate([b[:, width:] for b in blocks], axis=0)
        return carry

    tiles = chips // per_tile
    lax.fori_loop(0, tiles, step, 0, unroll=tiles <= 2)


def fetch_kernel(
    mine_ref, gate_hbm, up_hbm, down_hbm, gate_ref, up_ref, down_ref, x_ref, dy_ref, sems
):
    copies = copy_pieces(gate_hbm, gate_ref, sems.at[0])
    copies += copy_pieces(up_hbm, up_ref, sems.at[1])
    copies += copy_pieces(down_hbm, down_ref, sems.at[2])
    for copy in copies:
        copy.start()
    lay_out(mine_ref, x_ref, dy_ref, 0)
    for copy in copies:
        copy.wait()


def fetch(mine, *weights):
    places, tok_dev, row = mine.shape
    rows = (places * tok_dev, row // 2)
    moved = sum(2 * w.size for w in weights)
    weights = [pltpu.with_memory_space_constraint(w, pltpu.HBM) for w in weights]
    return pl.pallas_call(
        fetch_kernel,
        out_shape=tuple(pltpu.VMEM(w.shape[1:], w.dtype) for w in weights)
        + (pltpu.VMEM(rows, jnp.bfloat16), pltpu.VMEM(rows, jnp.bfloat16)),
        in_specs=[VMEM] + [HBM] * 3,
        out_specs=(VMEM,) * 5,
        scratch_shapes=[pltpu.SemaphoreType.DMA((3, PIECES))],
        cost_estimate=pl.CostEstimate(flops=0, bytes_accessed=2 * moved, transcendentals=0),
        compiler_params=vmem((4 << 20) + 2 * moved + 8 * mine.size),
    )(mine, *weights)


def lay_kernel(*refs):
    *src_refs, x_ref, dy_ref = refs
    for i, src_ref in enumerate(src_refs):
        lay_out(src_ref, x_ref, dy_ref, i * (x_ref.shape[0] // len(src_refs)))


def lay(*blocks):
    places, tok_dev, row = blocks[0].shape
    rows = (len(blocks) * places * tok_dev, row // 2)
    return pl.pallas_call(
        lay_kernel,
        out_shape=(pltpu.VMEM(rows, jnp.bfloat16), pltpu.VMEM(rows, jnp.bfloat16)),
        in_specs=[VMEM] * len(blocks),
        out_specs=(VMEM,) * 2,
        cost_estimate=pl.CostEstimate(
            flops=0, bytes_accessed=8 * len(blocks) * blocks[0].size, transcendentals=0
        ),
        compiler_params=vmem((8 << 20) + 8 * len(blocks) * blocks[0].size),
    )(*blocks)


def my_core():
    return lax.axis_index("dp") % CORES


def row_blocks(rows, step):
    step(0, True)
    if rows > ROWS:
        pl.loop(1, rows // ROWS)(lambda block: step(block, False))


def half_total(gate_delta, up_delta, gate_ref, up_ref, core):
    columns = gate_ref.shape[0] // CORES
    part = pl.ds(pl.multiple_of(core * columns, columns), columns)
    total = lax.dot_general(
        gate_delta, gate_ref[part], CONTRACT_LAST, preferred_element_type=jnp.float32
    )
    return total + lax.dot_general(
        up_delta, up_ref[part], CONTRACT_LAST, preferred_element_type=jnp.float32
    )


def store_groups(ref, first, total):
    rows, columns = total.shape
    groups = columns // LANES
    for c in range(groups):
        ref[pl.ds(first + c, rows, stride=groups)] = total[:, c * LANES : (c + 1) * LANES]


def rows_kernel(*refs):
    along_y = sizes()[2]
    other_refs, refs = refs[: along_y - 1], refs[along_y - 1 :]
    my_x_ref, my_dy_ref, laid_x_ref, laid_dy_ref, gate_ref, up_ref, down_ref, *refs = refs
    sent_ref, x_ref, dy_ref, gate_delta_ref, up_delta_ref, hidden_ref, total_ref = refs
    size = my_x_ref.shape[0]
    x_ref[:size] = my_x_ref[...]
    dy_ref[:size] = my_dy_ref[...]
    for i in range(along_y):
        there = pl.ds(size if i == 0 else 2 * i * size, size)
        x_ref[there] = laid_x_ref[i * size : (i + 1) * size]
        dy_ref[there] = laid_dy_ref[i * size : (i + 1) * size]
    for i, other_ref in enumerate(other_refs):
        lay_out(other_ref, x_ref, dy_ref, (2 * i + 3) * size)

    def step(block, first):
        rows = pl.ds(pl.multiple_of(block * ROWS, ROWS), ROWS)
        x = x_ref[rows]
        pre_gate = jnp.dot(x, gate_ref[...], preferred_element_type=jnp.float32)
        pre_up = jnp.dot(x, up_ref[...], preferred_element_type=jnp.float32)
        sigmoid_gate = jax.nn.sigmoid(pre_gate)
        activated = pre_gate * sigmoid_gate
        slope = sigmoid_gate * (1.0 + pre_gate * (1.0 - sigmoid_gate))
        hidden_ref[rows] = (activated * pre_up).astype(jnp.bfloat16)
        grad_hidden = lax.dot_general(
            dy_ref[rows], down_ref[...], CONTRACT_LAST, preferred_element_type=jnp.float32
        )
        gate_delta = (grad_hidden * pre_up * slope).astype(jnp.bfloat16)
        up_delta = (grad_hidden * activated).astype(jnp.bfloat16)
        gate_delta_ref[rows] = gate_delta
        up_delta_ref[rows] = up_delta
        total = half_total(gate_delta, up_delta, gate_ref, up_ref, 1 - my_core())
        store_groups(total_ref, 0, total)
        size = total_ref.shape[0]
        part = pl.ds(pl.multiple_of(block * size, size), size)
        sent_ref[part] = total_ref[...].astype(jnp.bfloat16)

    row_blocks(x_ref.shape[0], step)


def rows_pass(others, my_x, my_dy, laid_x, laid_dy, gate, up, down):
    width, hidden = gate.shape
    rows = CORES * laid_x.shape[0]
    groups = width // CORES // LANES
    bf16 = functools.partial(jax.ShapeDtypeStruct, dtype=jnp.bfloat16)
    moved = rows * (6 * width + 3 * hidden) * 2
    return pl.pallas_call(
        rows_kernel,
        out_shape=(
            bf16((rows * groups, LANES)),
            bf16((rows, width)),
            bf16((rows, width)),
            bf16((rows, hidden)),
            bf16((rows, hidden)),
            bf16((rows, hidden)),
        ),
        in_specs=[VMEM] * (len(others) + 7),
        out_specs=(VMEM,) * 6,
        scratch_shapes=[pltpu.VMEM((ROWS * groups, LANES), jnp.float32)],
        cost_estimate=pl.CostEstimate(
            flops=8 * rows * width * hidden, bytes_accessed=moved, transcendentals=rows * hidden
        ),
        compiler_params=vmem((12 << 20) + 2 * moved),
    )(*others, my_x, my_dy, laid_x, laid_dy, gate, up, down)


def finish_kernel(gate_delta_ref, up_delta_ref, gate_ref, up_ref, total_ref):
    rows_all = gate_delta_ref.shape[0]
    size = total_ref.shape[0] // rows_all * ROWS

    def step(block, first):
        rows = pl.ds(pl.multiple_of(block * ROWS, ROWS), ROWS)
        total = half_total(
            gate_delta_ref[rows], up_delta_ref[rows], gate_ref, up_ref, my_core()
        )
        store_groups(total_ref, block * size, total)

    row_blocks(rows_all, step)


def finish(gate_delta, up_delta, gate, up):
    rows, hidden = gate_delta.shape
    columns = gate.shape[0] // CORES
    moved = 4 * columns * hidden + 4 * rows * (columns + hidden)
    return pl.pallas_call(
        finish_kernel,
        out_shape=jax.ShapeDtypeStruct((rows * columns // LANES, LANES), jnp.float32),
        in_specs=[VMEM] * 4,
        out_specs=VMEM,
        cost_estimate=pl.CostEstimate(
            flops=4 * rows * columns * hidden, bytes_accessed=moved, transcendentals=0
        ),
        compiler_params=vmem((16 << 20) + 2 * moved),
    )(gate_delta, up_delta, gate, up)


def share_kernel(total_ref, got_ref, shares_ref):
    devices, size, _ = shares_ref.shape
    experts, along_z, along_y, _ = sizes()
    places = experts * along_z
    y, core = my_y(), my_core()

    def step(row, carry):
        shift, half, place = row // (CORES * places), row // places % CORES, row % places
        got_row = row + (1 - 2 * half) * places
        here = pl.ds(pl.multiple_of(row * size, size), size)
        there = pl.ds(pl.multiple_of(got_row * size, size), size)
        expert, z = place_at(place)
        owner = device_at(expert, z, (y + shift) % along_y, (core + half) % CORES)
        total = total_ref[here] + got_ref[there].astype(jnp.float32)
        shares_ref[owner] = total.astype(jnp.bfloat16)
        return carry

    lax.fori_loop(0, devices, step, 0, unroll=devices <= 32)


def share(total, got, devices):
    size = total.shape[0] // devices
    return pl.pallas_call(
        share_kernel,
        out_shape=pltpu.VMEM((devices, size, LANES), jnp.bfloat16),
        in_specs=[VMEM] * 2,
        out_specs=VMEM,
        compiler_params=vmem((8 << 20) + 32 * total.size),
    )(total, got)


def sum_kernel(shares_ref, out_hbm, wide_ref, out_ref, sem):
    devices, size, _ = shares_ref.shape
    _, tok_dev, width = out_ref.shape
    groups = size // tok_dev
    for core in range(CORES):
        total = lax.fori_loop(
            0,
            devices // CORES,
            lambda i, acc: acc + shares_ref[i * CORES + core].astype(jnp.float32),
            jnp.zeros((size, LANES), jnp.float32),
            unroll=devices <= 32,
        )
        for row in range(size):
            token, lane = row // groups, (core * groups + row % groups) * LANES
            wide_ref[token : token + 1, lane : lane + LANES] = total[row : row + 1]
    out_ref[0] = wide_ref[...].astype(jnp.bfloat16)
    copy = pltpu.make_async_copy(out_ref, out_hbm, sem)
    copy.start()
    copy.wait()


def sum_shares(shares, tok_dev):
    _, size, _ = shares.shape
    width = CORES * size // tok_dev * LANES
    return pl.pallas_call(
        sum_kernel,
        out_shape=pltpu.HBM((1, tok_dev, width), jnp.bfloat16),
        in_specs=[VMEM],
        out_specs=HBM,
        scratch_shapes=[
            pltpu.VMEM((tok_dev, width), jnp.float32),
            pltpu.VMEM((1, tok_dev, width), jnp.bfloat16),
            pltpu.SemaphoreType.DMA,
        ],
        compiler_params=vmem(16 << 20),
    )(shares)


def local(tokens, out_grad, expert_ids, gate_scores, w_gate, w_up, w_down):
    experts, along_z, along_y, _ = sizes()
    places = experts * along_z
    devices = places * along_y * CORES
    groups = [
        [device_at(expert, z, y, core) for expert, z in map(place_at, range(places))]
        for y in range(along_y)
        for core in range(CORES)
    ]
    core_pairs = [(d, d ^ 1) for d in range(devices)]

    def from_y(shift):
        return [
            (device_at(e, z, (y + shift) % along_y, c), device_at(e, z, y, c))
            for e in range(experts)
            for z in range(along_z)
            for y in range(along_y)
            for c in range(CORES)
        ]

    copies = pack(tokens, out_grad, expert_ids, gate_scores, places)
    mine = lax.all_to_all(copies, BOTH, 0, 0, axis_index_groups=groups, tiled=True)
    beside = [lax.ppermute(mine, BOTH, from_y(shift)) for shift in range(1, along_y)]
    other = lax.ppermute(mine, BOTH, core_pairs)
    gate, up, down, my_x, my_dy = fetch(mine, w_gate, w_up, w_down)
    *beside, my_x = lax.optimization_barrier((*beside, my_x))
    others = [lax.ppermute(piece, BOTH, core_pairs) for piece in beside]
    laid_x, laid_dy = lay(other, *beside)
    sent, x, dy, gate_delta, up_delta, hidden = rows_pass(
        others, my_x, my_dy, laid_x, laid_dy, gate, up, down
    )
    got = lax.ppermute(sent, BOTH, core_pairs)
    total = finish(gate_delta, up_delta, gate, up)
    shares = share(total, got, devices)
    shares, gate_delta, up_delta, hidden = lax.optimization_barrier(
        (shares, gate_delta, up_delta, hidden)
    )
    shares = lax.all_to_all(shares, BOTH, 0, 0, tiled=True)
    token_grad = sum_shares(shares, tokens.shape[1])
    grad_down = jnp.dot(hidden.T, dy, preferred_element_type=jnp.float32)
    grad_gate = jnp.dot(x.T, gate_delta, preferred_element_type=jnp.float32)
    grad_up = jnp.dot(x.T, up_delta, preferred_element_type=jnp.float32)
    weight_grads = (grad_gate, grad_up, grad_down)
    return (token_grad,) + tuple(g.astype(jnp.bfloat16)[None] for g in weight_grads)


def solution(mesh):
    return jax.shard_map(
        local,
        mesh=mesh,
        in_specs=(
            P("dp", "expert", None),
            P("dp", "expert", None),
            P("dp", None, None),
            P("dp", None, None),
            P("expert", None, "dp"),
            P("expert", None, "dp"),
            P("expert", "dp", None),
        ),
        out_specs=(
            P("dp", "expert", None),
            P("expert", None, "dp"),
            P("expert", None, "dp"),
            P("expert", "dp", None),
        ),
        check_vma=False,
    )
```

```python
import functools

import jax
import jax.numpy as jnp
from jax import lax
from jax.experimental import pallas as pl
from jax.experimental.pallas import tpu as pltpu
from jax.sharding import PartitionSpec as P

LANES = 128
CORES = 2
BOTH = ("expert", "dp")
ROWS = 64
TILE = 16
CONTRACT_LAST = (((1,), (1,)), ((), ()))
PIECES = 4
VMEM = pl.BlockSpec(memory_space=pltpu.VMEM)
HBM = pl.BlockSpec(memory_space=pltpu.HBM)


def vmem(size):
    return pltpu.CompilerParams(vmem_limit_bytes=min(size, 36 << 20))


def sizes():
    dp = lax.axis_size("dp")
    along_y = 1
    while (2 * along_y) ** 2 <= dp // CORES:
        along_y *= 2
    return lax.axis_size("expert"), dp // CORES // along_y, along_y, CORES


def device_at(expert, z, y, core):
    _, along_z, along_y, _ = sizes()
    return ((expert * along_z + z) * along_y + y) * CORES + core


def z_at(step):
    upper = 1 - step % 2
    return sizes()[1] // 2 + upper * (step // 2) - (1 - upper) * (1 + step // 2)


def place_at(place):
    experts = sizes()[0]
    pair = place // 2
    return pair % experts, z_at(place % 2 + 2 * (pair // experts))


def order_at(place):
    experts, _, along_y, _ = sizes()
    place, core = place // CORES, place % CORES
    place, turn = place // 2, place % 2
    place, expert = place // experts, place % experts
    return device_at(expert, z_at(turn + 2 * (place // along_y)), place % along_y, core)


def order_of(expert, z, y, core):
    experts, along_z, along_y, _ = sizes()
    upper = (z >= along_z // 2) * 1
    step = upper * (z - along_z // 2) + (1 - upper) * (along_z // 2 - 1 - z)
    return (((step * along_y + y) * experts + expert) * 2 + 1 - upper) * CORES + core


def my_y():
    return lax.axis_index("dp") // CORES % sizes()[2]


def pack_kernel(
    tokens_hbm, grad_hbm, ids_hbm, scores_hbm, out_ref,
    tokens_ref, grad_ref, ids_ref, scores_ref, weighted_ref, sems,
):
    copies = [
        pltpu.make_async_copy(src, dst, sems.at[i])
        for i, (src, dst) in enumerate((
            (ids_hbm, ids_ref),
            (scores_hbm, scores_ref),
            (tokens_hbm, tokens_ref),
            (grad_hbm, grad_ref),
        ))
    ]
    for copy in copies:
        copy.start()
    for copy in copies:
        copy.wait()
    places, tok_dev, _ = out_ref.shape
    width = tokens_ref.shape[2]
    experts = lax.axis_size("expert")
    first = lax.axis_index("expert") * tok_dev
    ids = ids_ref[0]
    scores = scores_ref[0].astype(jnp.float32)
    token = lax.broadcasted_iota(jnp.int32, ids.shape, 1)
    lane = lax.broadcasted_iota(jnp.int32, (ids.shape[0], LANES), 1)
    row = lax.broadcasted_iota(jnp.int32, (tok_dev, LANES), 0)
    table = jnp.zeros((tok_dev, LANES), jnp.float32)
    for i in range(tok_dev):
        mine = token == first + i
        named = jnp.sum(jnp.where(mine, ids, 0), axis=1, keepdims=True)
        score = jnp.sum(jnp.where(mine, scores, 0.0), axis=1, keepdims=True)
        weights = jnp.sum(jnp.where(lane == named, score, 0.0), axis=0, keepdims=True)
        table = jnp.where(row == i, weights, table)
    grad = grad_ref[0].astype(jnp.float32)
    for expert in range(experts):
        weighted_ref[expert] = (grad * table[:, expert : expert + 1]).astype(jnp.bfloat16)

    def write(place, carry):
        out_ref[place, :, :width] = tokens_ref[0]
        out_ref[place, :, width:] = weighted_ref[place_at(place)[0]]
        return carry

    lax.fori_loop(0, places, write, 0, unroll=places <= 16)


def pack(tokens, out_grad, expert_ids, gate_scores, places):
    _, tok_dev, width = tokens.shape
    operands = [
        pltpu.with_memory_space_constraint(a, pltpu.HBM)
        for a in (
            tokens, out_grad, jnp.swapaxes(expert_ids, 1, 2), jnp.swapaxes(gate_scores, 1, 2)
        )
    ]
    return pl.pallas_call(
        pack_kernel,
        out_shape=jax.ShapeDtypeStruct((places, tok_dev, 2 * width), jnp.bfloat16),
        in_specs=[HBM] * 4,
        out_specs=VMEM,
        scratch_shapes=[pltpu.VMEM(a.shape, a.dtype) for a in operands]
        + [
            pltpu.VMEM((lax.axis_size("expert"), tok_dev, width), jnp.bfloat16),
            pltpu.SemaphoreType.DMA((4,)),
        ],
        compiler_params=vmem(16 << 20),
    )(*operands)


def copy_pieces(src, dst, sems):
    rows = dst.shape[0] // PIECES
    parts = [pl.ds(piece * rows, rows) for piece in range(PIECES)]
    return [
        pltpu.make_async_copy(src.at[0, part], dst.at[part], sems.at[piece])
        for piece, part in enumerate(parts)
    ]


def lay_out(src_ref, x_ref, dy_ref, first):
    chips, tok_dev, _ = src_ref.shape
    width = x_ref.shape[1]
    per_tile = TILE // tok_dev

    def step(tile, carry):
        rows = pl.ds(pl.multiple_of(first + tile * TILE, TILE), TILE)
        blocks = [src_ref[tile * per_tile + j] for j in range(per_tile)]
        x_ref[rows] = jnp.concatenate([b[:, :width] for b in blocks], axis=0)
        dy_ref[rows] = jnp.concatenate([b[:, width:] for b in blocks], axis=0)
        return carry

    tiles = chips // per_tile
    lax.fori_loop(0, tiles, step, 0, unroll=tiles <= 2)


def fetch_kernel(
    mine_ref, gate_hbm, up_hbm, down_hbm, gate_ref, up_ref, down_ref, x_ref, dy_ref, sems
):
    copies = copy_pieces(gate_hbm, gate_ref, sems.at[0])
    copies += copy_pieces(up_hbm, up_ref, sems.at[1])
    copies += copy_pieces(down_hbm, down_ref, sems.at[2])
    for copy in copies:
        copy.start()
    lay_out(mine_ref, x_ref, dy_ref, 0)
    for copy in copies:
        copy.wait()


def fetch(mine, *weights):
    places, tok_dev, row = mine.shape
    rows = (places * tok_dev, row // 2)
    moved = sum(2 * w.size for w in weights)
    weights = [pltpu.with_memory_space_constraint(w, pltpu.HBM) for w in weights]
    return pl.pallas_call(
        fetch_kernel,
        out_shape=tuple(pltpu.VMEM(w.shape[1:], w.dtype) for w in weights)
        + (pltpu.VMEM(rows, jnp.bfloat16), pltpu.VMEM(rows, jnp.bfloat16)),
        in_specs=[VMEM] + [HBM] * 3,
        out_specs=(VMEM,) * 5,
        scratch_shapes=[pltpu.SemaphoreType.DMA((3, PIECES))],
        cost_estimate=pl.CostEstimate(flops=0, bytes_accessed=2 * moved, transcendentals=0),
        compiler_params=vmem((4 << 20) + 2 * moved + 8 * mine.size),
    )(mine, *weights)


def lay_kernel(*refs):
    *src_refs, x_ref, dy_ref = refs
    for i, src_ref in enumerate(src_refs):
        lay_out(src_ref, x_ref, dy_ref, i * (x_ref.shape[0] // len(src_refs)))


def lay(*blocks):
    places, tok_dev, row = blocks[0].shape
    rows = (len(blocks) * places * tok_dev, row // 2)
    return pl.pallas_call(
        lay_kernel,
        out_shape=(pltpu.VMEM(rows, jnp.bfloat16), pltpu.VMEM(rows, jnp.bfloat16)),
        in_specs=[VMEM] * len(blocks),
        out_specs=(VMEM,) * 2,
        cost_estimate=pl.CostEstimate(
            flops=0, bytes_accessed=8 * len(blocks) * blocks[0].size, transcendentals=0
        ),
        compiler_params=vmem((8 << 20) + 8 * len(blocks) * blocks[0].size),
    )(*blocks)


def my_core():
    return lax.axis_index("dp") % CORES


def row_blocks(rows, step):
    step(0, True)
    if rows > ROWS:
        pl.loop(1, rows // ROWS)(lambda block: step(block, False))


def half_total(gate_delta, up_delta, gate_ref, up_ref, core):
    columns = gate_ref.shape[0] // CORES
    part = pl.ds(pl.multiple_of(core * columns, columns), columns)
    total = lax.dot_general(
        gate_delta, gate_ref[part], CONTRACT_LAST, preferred_element_type=jnp.float32
    )
    return total + lax.dot_general(
        up_delta, up_ref[part], CONTRACT_LAST, preferred_element_type=jnp.float32
    )


def store_groups(ref, first, total):
    rows, columns = total.shape
    groups = columns // LANES
    for c in range(groups):
        ref[pl.ds(first + c, rows, stride=groups)] = total[:, c * LANES : (c + 1) * LANES]


def rows_kernel(*refs):
    along_y = sizes()[2]
    other_refs, refs = refs[: along_y - 1], refs[along_y - 1 :]
    my_x_ref, my_dy_ref, laid_x_ref, laid_dy_ref, gate_ref, up_ref, down_ref, *refs = refs
    sent_ref, x_ref, dy_ref, gate_delta_ref, up_delta_ref, hidden_ref, total_ref = refs
    size = my_x_ref.shape[0]
    x_ref[:size] = my_x_ref[...]
    dy_ref[:size] = my_dy_ref[...]
    for i in range(along_y):
        there = pl.ds(size if i == 0 else 2 * i * size, size)
        x_ref[there] = laid_x_ref[i * size : (i + 1) * size]
        dy_ref[there] = laid_dy_ref[i * size : (i + 1) * size]
    for i, other_ref in enumerate(other_refs):
        lay_out(other_ref, x_ref, dy_ref, (2 * i + 3) * size)

    def step(block, first):
        rows = pl.ds(pl.multiple_of(block * ROWS, ROWS), ROWS)
        x = x_ref[rows]
        pre_gate = jnp.dot(x, gate_ref[...], preferred_element_type=jnp.float32)
        pre_up = jnp.dot(x, up_ref[...], preferred_element_type=jnp.float32)
        sigmoid_gate = jax.nn.sigmoid(pre_gate)
        activated = pre_gate * sigmoid_gate
        slope = sigmoid_gate * (1.0 + pre_gate * (1.0 - sigmoid_gate))
        hidden_ref[rows] = (activated * pre_up).astype(jnp.bfloat16)
        grad_hidden = lax.dot_general(
            dy_ref[rows], down_ref[...], CONTRACT_LAST, preferred_element_type=jnp.float32
        )
        gate_delta = (grad_hidden * pre_up * slope).astype(jnp.bfloat16)
        up_delta = (grad_hidden * activated).astype(jnp.bfloat16)
        gate_delta_ref[rows] = gate_delta
        up_delta_ref[rows] = up_delta
        total = half_total(gate_delta, up_delta, gate_ref, up_ref, 1 - my_core())
        store_groups(total_ref, 0, total)
        size = total_ref.shape[0]
        part = pl.ds(pl.multiple_of(block * size, size), size)
        sent_ref[part] = total_ref[...].astype(jnp.bfloat16)

    row_blocks(x_ref.shape[0], step)


def rows_pass(others, my_x, my_dy, laid_x, laid_dy, gate, up, down):
    width, hidden = gate.shape
    rows = CORES * laid_x.shape[0]
    groups = width // CORES // LANES
    bf16 = functools.partial(jax.ShapeDtypeStruct, dtype=jnp.bfloat16)
    moved = rows * (6 * width + 3 * hidden) * 2
    return pl.pallas_call(
        rows_kernel,
        out_shape=(
            bf16((rows * groups, LANES)),
            bf16((rows, width)),
            bf16((rows, width)),
            bf16((rows, hidden)),
            bf16((rows, hidden)),
            bf16((rows, hidden)),
        ),
        in_specs=[VMEM] * (len(others) + 7),
        out_specs=(VMEM,) * 6,
        scratch_shapes=[pltpu.VMEM((ROWS * groups, LANES), jnp.float32)],
        cost_estimate=pl.CostEstimate(
            flops=8 * rows * width * hidden, bytes_accessed=moved, transcendentals=rows * hidden
        ),
        compiler_params=vmem((12 << 20) + 2 * moved),
    )(*others, my_x, my_dy, laid_x, laid_dy, gate, up, down)


def finish_kernel(gate_delta_ref, up_delta_ref, gate_ref, up_ref, total_ref):
    rows_all = gate_delta_ref.shape[0]
    size = total_ref.shape[0] // rows_all * ROWS

    def step(block, first):
        rows = pl.ds(pl.multiple_of(block * ROWS, ROWS), ROWS)
        total = half_total(
            gate_delta_ref[rows], up_delta_ref[rows], gate_ref, up_ref, my_core()
        )
        store_groups(total_ref, block * size, total)

    row_blocks(rows_all, step)


def finish(gate_delta, up_delta, gate, up):
    rows, hidden = gate_delta.shape
    columns = gate.shape[0] // CORES
    moved = 4 * columns * hidden + 4 * rows * (columns + hidden)
    return pl.pallas_call(
        finish_kernel,
        out_shape=jax.ShapeDtypeStruct((rows * columns // LANES, LANES), jnp.float32),
        in_specs=[VMEM] * 4,
        out_specs=VMEM,
        cost_estimate=pl.CostEstimate(
            flops=4 * rows * columns * hidden, bytes_accessed=moved, transcendentals=0
        ),
        compiler_params=vmem((16 << 20) + 2 * moved),
    )(gate_delta, up_delta, gate, up)


def share_kernel(total_ref, got_ref, shares_ref):
    devices, size, _ = shares_ref.shape
    experts, along_z, along_y, _ = sizes()
    places = experts * along_z
    y, core = my_y(), my_core()

    def step(row, carry):
        shift, half, place = row // (CORES * places), row // places % CORES, row % places
        got_row = row + (1 - 2 * half) * places
        here = pl.ds(pl.multiple_of(row * size, size), size)
        there = pl.ds(pl.multiple_of(got_row * size, size), size)
        expert, z = place_at(place)
        owner = order_of(expert, z, (y + shift) % along_y, (core + half) % CORES)
        total = total_ref[here] + got_ref[there].astype(jnp.float32)
        shares_ref[owner] = total.astype(jnp.bfloat16)
        return carry

    lax.fori_loop(0, devices, step, 0, unroll=devices <= 32)


def share(total, got, devices):
    size = total.shape[0] // devices
    return pl.pallas_call(
        share_kernel,
        out_shape=pltpu.VMEM((devices, size, LANES), jnp.bfloat16),
        in_specs=[VMEM] * 2,
        out_specs=VMEM,
        compiler_params=vmem((8 << 20) + 32 * total.size),
    )(total, got)


def sum_kernel(shares_ref, out_hbm, wide_ref, out_ref, sem):
    devices, size, _ = shares_ref.shape
    _, tok_dev, width = out_ref.shape
    groups = size // tok_dev
    for core in range(CORES):
        total = lax.fori_loop(
            0,
            devices // CORES,
            lambda i, acc: acc + shares_ref[i * CORES + core].astype(jnp.float32),
            jnp.zeros((size, LANES), jnp.float32),
            unroll=devices <= 32,
        )
        for row in range(size):
            token, lane = row // groups, (core * groups + row % groups) * LANES
            wide_ref[token : token + 1, lane : lane + LANES] = total[row : row + 1]
    out_ref[0] = wide_ref[...].astype(jnp.bfloat16)
    copy = pltpu.make_async_copy(out_ref, out_hbm, sem)
    copy.start()
    copy.wait()


def sum_shares(shares, tok_dev):
    _, size, _ = shares.shape
    width = CORES * size // tok_dev * LANES
    return pl.pallas_call(
        sum_kernel,
        out_shape=pltpu.HBM((1, tok_dev, width), jnp.bfloat16),
        in_specs=[VMEM],
        out_specs=HBM,
        scratch_shapes=[
            pltpu.VMEM((tok_dev, width), jnp.float32),
            pltpu.VMEM((1, tok_dev, width), jnp.bfloat16),
            pltpu.SemaphoreType.DMA,
        ],
        compiler_params=vmem(16 << 20),
    )(shares)


def local(tokens, out_grad, expert_ids, gate_scores, w_gate, w_up, w_down):
    experts, along_z, along_y, _ = sizes()
    places = experts * along_z
    devices = places * along_y * CORES
    groups = [
        [device_at(expert, z, y, core) for expert, z in map(place_at, range(places))]
        for y in range(along_y)
        for core in range(CORES)
    ]
    core_pairs = [(d, d ^ 1) for d in range(devices)]

    def from_y(shift):
        return [
            (device_at(e, z, (y + shift) % along_y, c), device_at(e, z, y, c))
            for e in range(experts)
            for z in range(along_z)
            for y in range(along_y)
            for c in range(CORES)
        ]

    copies = pack(tokens, out_grad, expert_ids, gate_scores, places)
    mine = lax.all_to_all(copies, BOTH, 0, 0, axis_index_groups=groups, tiled=True)
    beside = [lax.ppermute(mine, BOTH, from_y(shift)) for shift in range(1, along_y)]
    other = lax.ppermute(mine, BOTH, core_pairs)
    gate, up, down, my_x, my_dy = fetch(mine, w_gate, w_up, w_down)
    *beside, my_x = lax.optimization_barrier((*beside, my_x))
    others = [lax.ppermute(piece, BOTH, core_pairs) for piece in beside]
    laid_x, laid_dy = lay(other, *beside)
    sent, x, dy, gate_delta, up_delta, hidden = rows_pass(
        others, my_x, my_dy, laid_x, laid_dy, gate, up, down
    )
    got = lax.ppermute(sent, BOTH, core_pairs)
    total = finish(gate_delta, up_delta, gate, up)
    shares = share(total, got, devices)
    shares, gate_delta, up_delta, hidden = lax.optimization_barrier(
        (shares, gate_delta, up_delta, hidden)
    )
    everyone = [[order_at(place) for place in range(devices)]]
    shares = lax.all_to_all(shares, BOTH, 0, 0, axis_index_groups=everyone, tiled=True)
    token_grad = sum_shares(shares, tokens.shape[1])
    grad_down = jnp.dot(hidden.T, dy, preferred_element_type=jnp.float32)
    grad_gate = jnp.dot(x.T, gate_delta, preferred_element_type=jnp.float32)
    grad_up = jnp.dot(x.T, up_delta, preferred_element_type=jnp.float32)
    weight_grads = (grad_gate, grad_up, grad_down)
    return (token_grad,) + tuple(g.astype(jnp.bfloat16)[None] for g in weight_grads)


def solution(mesh):
    return jax.shard_map(
        local,
        mesh=mesh,
        in_specs=(
            P("dp", "expert", None),
            P("dp", "expert", None),
            P("dp", None, None),
            P("dp", None, None),
            P("expert", None, "dp"),
            P("expert", None, "dp"),
            P("expert", "dp", None),
        ),
        out_specs=(
            P("dp", "expert", None),
            P("expert", None, "dp"),
            P("expert", None, "dp"),
            P("expert", "dp", None),
        ),
        check_vma=False,
    )
```

```python
import functools

import jax
import jax.numpy as jnp
from jax import lax
from jax.experimental import pallas as pl
from jax.experimental.pallas import tpu as pltpu
from jax.sharding import PartitionSpec as P

LANES = 128
CORES = 2
BOTH = ("expert", "dp")
ROWS = 64
TILE = 16
CONTRACT_LAST = (((1,), (1,)), ((), ()))
PIECES = 4
VMEM = pl.BlockSpec(memory_space=pltpu.VMEM)
HBM = pl.BlockSpec(memory_space=pltpu.HBM)


def vmem(size):
    return pltpu.CompilerParams(vmem_limit_bytes=min(size, 36 << 20))


def sizes():
    dp = lax.axis_size("dp")
    along_y = 1
    while (2 * along_y) ** 2 <= dp // CORES:
        along_y *= 2
    return lax.axis_size("expert"), dp // CORES // along_y, along_y, CORES


def device_at(expert, z, y, core):
    _, along_z, along_y, _ = sizes()
    return ((expert * along_z + z) * along_y + y) * CORES + core


def z_at(step):
    upper = 1 - step % 2
    return sizes()[1] // 2 + upper * (step // 2) - (1 - upper) * (1 + step // 2)


def place_at(place):
    experts = sizes()[0]
    pair = place // 2
    return pair % experts, z_at(place % 2 + 2 * (pair // experts))


def order_at(place):
    experts, _, along_y, _ = sizes()
    place, core = place // CORES, place % CORES
    place, turn = place // 2, place % 2
    place, expert = place // experts, place % experts
    return device_at(expert, z_at(turn + 2 * (place // along_y)), place % along_y, core)


def order_of(expert, z, y, core):
    experts, along_z, along_y, _ = sizes()
    upper = (z >= along_z // 2) * 1
    step = upper * (z - along_z // 2) + (1 - upper) * (along_z // 2 - 1 - z)
    return (((step * along_y + y) * experts + expert) * 2 + 1 - upper) * CORES + core


def my_y():
    return lax.axis_index("dp") // CORES % sizes()[2]


def pack_kernel(
    tokens_hbm, grad_hbm, ids_hbm, scores_hbm, out_ref,
    tokens_ref, grad_ref, ids_ref, scores_ref, weighted_ref, sems,
):
    copies = [
        pltpu.make_async_copy(src, dst, sems.at[i])
        for i, (src, dst) in enumerate((
            (ids_hbm, ids_ref),
            (scores_hbm, scores_ref),
            (tokens_hbm, tokens_ref),
            (grad_hbm, grad_ref),
        ))
    ]
    for copy in copies:
        copy.start()
    for copy in copies:
        copy.wait()
    places, tok_dev, _ = out_ref.shape
    width = tokens_ref.shape[2]
    experts = lax.axis_size("expert")
    first = lax.axis_index("expert") * tok_dev
    ids = ids_ref[0]
    scores = scores_ref[0].astype(jnp.float32)
    token = lax.broadcasted_iota(jnp.int32, ids.shape, 1)
    lane = lax.broadcasted_iota(jnp.int32, (ids.shape[0], LANES), 1)
    row = lax.broadcasted_iota(jnp.int32, (tok_dev, LANES), 0)
    table = jnp.zeros((tok_dev, LANES), jnp.float32)
    for i in range(tok_dev):
        mine = token == first + i
        named = jnp.sum(jnp.where(mine, ids, 0), axis=1, keepdims=True)
        score = jnp.sum(jnp.where(mine, scores, 0.0), axis=1, keepdims=True)
        weights = jnp.sum(jnp.where(lane == named, score, 0.0), axis=0, keepdims=True)
        table = jnp.where(row == i, weights, table)
    grad = grad_ref[0].astype(jnp.float32)
    for expert in range(experts):
        weighted_ref[expert] = (grad * table[:, expert : expert + 1]).astype(jnp.bfloat16)

    def write(place, carry):
        out_ref[place, :, :width] = tokens_ref[0]
        out_ref[place, :, width:] = weighted_ref[place_at(place)[0]]
        return carry

    lax.fori_loop(0, places, write, 0, unroll=places <= 16)


def pack(tokens, out_grad, expert_ids, gate_scores, places):
    _, tok_dev, width = tokens.shape
    operands = [
        pltpu.with_memory_space_constraint(a, pltpu.HBM)
        for a in (
            tokens, out_grad, jnp.swapaxes(expert_ids, 1, 2), jnp.swapaxes(gate_scores, 1, 2)
        )
    ]
    return pl.pallas_call(
        pack_kernel,
        out_shape=jax.ShapeDtypeStruct((places, tok_dev, 2 * width), jnp.bfloat16),
        in_specs=[HBM] * 4,
        out_specs=VMEM,
        scratch_shapes=[pltpu.VMEM(a.shape, a.dtype) for a in operands]
        + [
            pltpu.VMEM((lax.axis_size("expert"), tok_dev, width), jnp.bfloat16),
            pltpu.SemaphoreType.DMA((4,)),
        ],
        compiler_params=vmem(16 << 20),
    )(*operands)


def copy_pieces(src, dst, sems):
    rows = dst.shape[0] // PIECES
    parts = [pl.ds(piece * rows, rows) for piece in range(PIECES)]
    return [
        pltpu.make_async_copy(src.at[0, part], dst.at[part], sems.at[piece])
        for piece, part in enumerate(parts)
    ]


def halves(ref):
    width = ref.shape[2] // 2
    return ref.at[:, :, pl.ds(0, width)], ref.at[:, :, pl.ds(width, width)]


def lay_out(src_refs, dst_refs, first):
    chips, tok_dev, _ = src_refs[0].shape
    per_tile = TILE // tok_dev

    def step(tile, carry):
        rows = pl.ds(pl.multiple_of(first + tile * TILE, TILE), TILE)
        for src_ref, dst_ref in zip(src_refs, dst_refs):
            blocks = [src_ref[tile * per_tile + j] for j in range(per_tile)]
            dst_ref[rows] = jnp.concatenate(blocks, axis=0)
        return carry

    tiles = chips // per_tile
    lax.fori_loop(0, tiles, step, 0, unroll=tiles <= 2)


def fetch_kernel(
    mine_ref, gate_hbm, up_hbm, down_hbm, gate_ref, up_ref, down_ref, x_ref, dy_ref, sems
):
    copies = copy_pieces(gate_hbm, gate_ref, sems.at[0])
    copies += copy_pieces(up_hbm, up_ref, sems.at[1])
    copies += copy_pieces(down_hbm, down_ref, sems.at[2])
    for copy in copies:
        copy.start()
    lay_out(halves(mine_ref), (x_ref, dy_ref), 0)
    for copy in copies:
        copy.wait()


def fetch(mine, *weights):
    places, tok_dev, row = mine.shape
    rows = (places * tok_dev, row // 2)
    moved = sum(2 * w.size for w in weights)
    weights = [pltpu.with_memory_space_constraint(w, pltpu.HBM) for w in weights]
    return pl.pallas_call(
        fetch_kernel,
        out_shape=tuple(pltpu.VMEM(w.shape[1:], w.dtype) for w in weights)
        + (pltpu.VMEM(rows, jnp.bfloat16), pltpu.VMEM(rows, jnp.bfloat16)),
        in_specs=[VMEM] + [HBM] * 3,
        out_specs=(VMEM,) * 5,
        scratch_shapes=[pltpu.SemaphoreType.DMA((3, PIECES))],
        cost_estimate=pl.CostEstimate(flops=0, bytes_accessed=2 * moved, transcendentals=0),
        compiler_params=vmem((4 << 20) + 2 * moved + 8 * mine.size),
    )(mine, *weights)


def lay_kernel(other_ref, *refs):
    *src_refs, x_ref, dy_ref = refs
    pairs = [halves(other_ref), *zip(src_refs[::2], src_refs[1::2])]
    for i, pair in enumerate(pairs):
        lay_out(pair, (x_ref, dy_ref), i * (x_ref.shape[0] // len(pairs)))


def lay(other, beside):
    places, tok_dev, row = other.shape
    blocks = 1 + len(beside)
    rows = (blocks * places * tok_dev, row // 2)
    return pl.pallas_call(
        lay_kernel,
        out_shape=(pltpu.VMEM(rows, jnp.bfloat16), pltpu.VMEM(rows, jnp.bfloat16)),
        in_specs=[VMEM] * (2 * blocks - 1),
        out_specs=(VMEM,) * 2,
        cost_estimate=pl.CostEstimate(
            flops=0, bytes_accessed=8 * blocks * other.size, transcendentals=0
        ),
        compiler_params=vmem((8 << 20) + 8 * blocks * other.size),
    )(other, *(part for pair in beside for part in pair))


def my_core():
    return lax.axis_index("dp") % CORES


def row_blocks(rows, step):
    step(0, True)
    if rows > ROWS:
        pl.loop(1, rows // ROWS)(lambda block: step(block, False))


def half_total(gate_delta, up_delta, gate_ref, up_ref, core):
    columns = gate_ref.shape[0] // CORES
    part = pl.ds(pl.multiple_of(core * columns, columns), columns)
    total = lax.dot_general(
        gate_delta, gate_ref[part], CONTRACT_LAST, preferred_element_type=jnp.float32
    )
    return total + lax.dot_general(
        up_delta, up_ref[part], CONTRACT_LAST, preferred_element_type=jnp.float32
    )


def store_groups(ref, first, total):
    rows, columns = total.shape
    groups = columns // LANES
    for c in range(groups):
        ref[pl.ds(first + c, rows, stride=groups)] = total[:, c * LANES : (c + 1) * LANES]


def rows_kernel(*refs):
    along_y = sizes()[2]
    other_refs, refs = refs[: 2 * along_y - 2], refs[2 * along_y - 2 :]
    my_x_ref, my_dy_ref, laid_x_ref, laid_dy_ref, gate_ref, up_ref, down_ref, *refs = refs
    sent_ref, x_ref, dy_ref, gate_delta_ref, up_delta_ref, hidden_ref, total_ref = refs
    size = my_x_ref.shape[0]
    x_ref[:size] = my_x_ref[...]
    dy_ref[:size] = my_dy_ref[...]
    for i in range(along_y):
        there = pl.ds(size if i == 0 else 2 * i * size, size)
        x_ref[there] = laid_x_ref[i * size : (i + 1) * size]
        dy_ref[there] = laid_dy_ref[i * size : (i + 1) * size]
    for i, pair in enumerate(zip(other_refs[::2], other_refs[1::2])):
        lay_out(pair, (x_ref, dy_ref), (2 * i + 3) * size)

    def step(block, first):
        rows = pl.ds(pl.multiple_of(block * ROWS, ROWS), ROWS)
        x = x_ref[rows]
        pre_gate = jnp.dot(x, gate_ref[...], preferred_element_type=jnp.float32)
        pre_up = jnp.dot(x, up_ref[...], preferred_element_type=jnp.float32)
        sigmoid_gate = jax.nn.sigmoid(pre_gate)
        activated = pre_gate * sigmoid_gate
        slope = sigmoid_gate * (1.0 + pre_gate * (1.0 - sigmoid_gate))
        hidden_ref[rows] = (activated * pre_up).astype(jnp.bfloat16)
        grad_hidden = lax.dot_general(
            dy_ref[rows], down_ref[...], CONTRACT_LAST, preferred_element_type=jnp.float32
        )
        gate_delta = (grad_hidden * pre_up * slope).astype(jnp.bfloat16)
        up_delta = (grad_hidden * activated).astype(jnp.bfloat16)
        gate_delta_ref[rows] = gate_delta
        up_delta_ref[rows] = up_delta
        total = half_total(gate_delta, up_delta, gate_ref, up_ref, 1 - my_core())
        store_groups(total_ref, 0, total)
        size = total_ref.shape[0]
        part = pl.ds(pl.multiple_of(block * size, size), size)
        sent_ref[part] = total_ref[...].astype(jnp.bfloat16)

    row_blocks(x_ref.shape[0], step)


def rows_pass(others, my_x, my_dy, laid_x, laid_dy, gate, up, down):
    width, hidden = gate.shape
    rows = CORES * laid_x.shape[0]
    groups = width // CORES // LANES
    bf16 = functools.partial(jax.ShapeDtypeStruct, dtype=jnp.bfloat16)
    moved = rows * (6 * width + 3 * hidden) * 2
    return pl.pallas_call(
        rows_kernel,
        out_shape=(
            bf16((rows * groups, LANES)),
            bf16((rows, width)),
            bf16((rows, width)),
            bf16((rows, hidden)),
            bf16((rows, hidden)),
            bf16((rows, hidden)),
        ),
        in_specs=[VMEM] * (2 * len(others) + 7),
        out_specs=(VMEM,) * 6,
        scratch_shapes=[pltpu.VMEM((ROWS * groups, LANES), jnp.float32)],
        cost_estimate=pl.CostEstimate(
            flops=8 * rows * width * hidden, bytes_accessed=moved, transcendentals=rows * hidden
        ),
        compiler_params=vmem((12 << 20) + 2 * moved),
    )(*(part for pair in others for part in pair), my_x, my_dy, laid_x, laid_dy, gate, up, down)


def finish_kernel(gate_delta_ref, up_delta_ref, gate_ref, up_ref, total_ref):
    rows_all = gate_delta_ref.shape[0]
    size = total_ref.shape[0] // rows_all * ROWS

    def step(block, first):
        rows = pl.ds(pl.multiple_of(block * ROWS, ROWS), ROWS)
        total = half_total(
            gate_delta_ref[rows], up_delta_ref[rows], gate_ref, up_ref, my_core()
        )
        store_groups(total_ref, block * size, total)

    row_blocks(rows_all, step)


def finish(gate_delta, up_delta, gate, up):
    rows, hidden = gate_delta.shape
    columns = gate.shape[0] // CORES
    moved = 4 * columns * hidden + 4 * rows * (columns + hidden)
    return pl.pallas_call(
        finish_kernel,
        out_shape=jax.ShapeDtypeStruct((rows * columns // LANES, LANES), jnp.float32),
        in_specs=[VMEM] * 4,
        out_specs=VMEM,
        cost_estimate=pl.CostEstimate(
            flops=4 * rows * columns * hidden, bytes_accessed=moved, transcendentals=0
        ),
        compiler_params=vmem((16 << 20) + 2 * moved),
    )(gate_delta, up_delta, gate, up)


def share_kernel(total_ref, got_ref, shares_ref):
    devices, size, _ = shares_ref.shape
    experts, along_z, along_y, _ = sizes()
    places = experts * along_z
    y, core = my_y(), my_core()

    def step(row, carry):
        shift, half, place = row // (CORES * places), row // places % CORES, row % places
        got_row = row + (1 - 2 * half) * places
        here = pl.ds(pl.multiple_of(row * size, size), size)
        there = pl.ds(pl.multiple_of(got_row * size, size), size)
        expert, z = place_at(place)
        owner = order_of(expert, z, (y + shift) % along_y, (core + half) % CORES)
        total = total_ref[here] + got_ref[there].astype(jnp.float32)
        shares_ref[owner] = total.astype(jnp.bfloat16)
        return carry

    lax.fori_loop(0, devices, step, 0, unroll=devices <= 32)


def share(total, got, devices):
    size = total.shape[0] // devices
    return pl.pallas_call(
        share_kernel,
        out_shape=pltpu.VMEM((devices, size, LANES), jnp.bfloat16),
        in_specs=[VMEM] * 2,
        out_specs=VMEM,
        compiler_params=vmem((8 << 20) + 32 * total.size),
    )(total, got)


def sum_kernel(shares_ref, out_hbm, wide_ref, out_ref, sem):
    devices, size, _ = shares_ref.shape
    _, tok_dev, width = out_ref.shape
    groups = size // tok_dev
    for core in range(CORES):
        total = lax.fori_loop(
            0,
            devices // CORES,
            lambda i, acc: acc + shares_ref[i * CORES + core].astype(jnp.float32),
            jnp.zeros((size, LANES), jnp.float32),
            unroll=devices <= 32,
        )
        for row in range(size):
            token, lane = row // groups, (core * groups + row % groups) * LANES
            wide_ref[token : token + 1, lane : lane + LANES] = total[row : row + 1]
    out_ref[0] = wide_ref[...].astype(jnp.bfloat16)
    copy = pltpu.make_async_copy(out_ref, out_hbm, sem)
    copy.start()
    copy.wait()


def sum_shares(shares, tok_dev):
    _, size, _ = shares.shape
    width = CORES * size // tok_dev * LANES
    return pl.pallas_call(
        sum_kernel,
        out_shape=pltpu.HBM((1, tok_dev, width), jnp.bfloat16),
        in_specs=[VMEM],
        out_specs=HBM,
        scratch_shapes=[
            pltpu.VMEM((tok_dev, width), jnp.float32),
            pltpu.VMEM((1, tok_dev, width), jnp.bfloat16),
            pltpu.SemaphoreType.DMA,
        ],
        compiler_params=vmem(16 << 20),
    )(shares)


def local(tokens, out_grad, expert_ids, gate_scores, w_gate, w_up, w_down):
    experts, along_z, along_y, _ = sizes()
    places = experts * along_z
    devices = places * along_y * CORES
    groups = [
        [device_at(expert, z, y, core) for expert, z in map(place_at, range(places))]
        for y in range(along_y)
        for core in range(CORES)
    ]
    core_pairs = [(d, d ^ 1) for d in range(devices)]

    def from_y(shift):
        return [
            (device_at(e, z, (y + shift) % along_y, c), device_at(e, z, y, c))
            for e in range(experts)
            for z in range(along_z)
            for y in range(along_y)
            for c in range(CORES)
        ]

    copies = pack(tokens, out_grad, expert_ids, gate_scores, places)
    mine = lax.all_to_all(copies, BOTH, 0, 0, axis_index_groups=groups, tiled=True)
    width = mine.shape[2] // 2
    parts = (mine[:, :, :width], mine[:, :, width:])
    beside = [
        [lax.ppermute(part, BOTH, from_y(shift)) for part in parts]
        for shift in range(1, along_y)
    ]
    other = lax.ppermute(mine, BOTH, core_pairs)
    gate, up, down, my_x, my_dy = fetch(mine, w_gate, w_up, w_down)
    beside, my_x = lax.optimization_barrier((beside, my_x))
    others = [[lax.ppermute(part, BOTH, core_pairs) for part in pair] for pair in beside]
    laid_x, laid_dy = lay(other, beside)
    sent, x, dy, gate_delta, up_delta, hidden = rows_pass(
        others, my_x, my_dy, laid_x, laid_dy, gate, up, down
    )
    got = lax.ppermute(sent, BOTH, core_pairs)
    total = finish(gate_delta, up_delta, gate, up)
    shares = share(total, got, devices)
    shares, gate_delta, up_delta, hidden = lax.optimization_barrier(
        (shares, gate_delta, up_delta, hidden)
    )
    everyone = [[order_at(place) for place in range(devices)]]
    shares = lax.all_to_all(shares, BOTH, 0, 0, axis_index_groups=everyone, tiled=True)
    token_grad = sum_shares(shares, tokens.shape[1])
    grad_down = jnp.dot(hidden.T, dy, preferred_element_type=jnp.float32)
    grad_gate = jnp.dot(x.T, gate_delta, preferred_element_type=jnp.float32)
    grad_up = jnp.dot(x.T, up_delta, preferred_element_type=jnp.float32)
    weight_grads = (grad_gate, grad_up, grad_down)
    return (token_grad,) + tuple(g.astype(jnp.bfloat16)[None] for g in weight_grads)


def solution(mesh):
    return jax.shard_map(
        local,
        mesh=mesh,
        in_specs=(
            P("dp", "expert", None),
            P("dp", "expert", None),
            P("dp", None, None),
            P("dp", None, None),
            P("expert", None, "dp"),
            P("expert", None, "dp"),
            P("expert", "dp", None),
        ),
        out_specs=(
            P("dp", "expert", None),
            P("expert", None, "dp"),
            P("expert", None, "dp"),
            P("expert", "dp", None),
        ),
        check_vma=False,
    )
```

```python
import functools

import jax
import jax.numpy as jnp
from jax import lax
from jax.experimental import pallas as pl
from jax.experimental.pallas import tpu as pltpu
from jax.sharding import PartitionSpec as P

LANES = 128
CORES = 2
BOTH = ("expert", "dp")
ROWS = 64
TILE = 16
CONTRACT_LAST = (((1,), (1,)), ((), ()))
PIECES = 4
VMEM = pl.BlockSpec(memory_space=pltpu.VMEM)
HBM = pl.BlockSpec(memory_space=pltpu.HBM)


def vmem(size):
    return pltpu.CompilerParams(vmem_limit_bytes=min(size, 36 << 20))


def sizes():
    dp = lax.axis_size("dp")
    along_y = 1
    while (2 * along_y) ** 2 <= dp // CORES:
        along_y *= 2
    return lax.axis_size("expert"), dp // CORES // along_y, along_y, CORES


def device_at(expert, z, y, core):
    _, along_z, along_y, _ = sizes()
    return ((expert * along_z + z) * along_y + y) * CORES + core


def z_at(step):
    upper = 1 - step % 2
    return sizes()[1] // 2 + upper * (step // 2) - (1 - upper) * (1 + step // 2)


def place_at(place):
    experts = sizes()[0]
    pair = place // 2
    return pair % experts, z_at(place % 2 + 2 * (pair // experts))


def order_at(place):
    experts, _, along_y, _ = sizes()
    place, core = place // CORES, place % CORES
    place, turn = place // 2, place % 2
    place, expert = place // experts, place % experts
    return device_at(expert, z_at(turn + 2 * (place // along_y)), place % along_y, core)


def order_of(expert, z, y, core):
    experts, along_z, along_y, _ = sizes()
    upper = (z >= along_z // 2) * 1
    step = upper * (z - along_z // 2) + (1 - upper) * (along_z // 2 - 1 - z)
    return (((step * along_y + y) * experts + expert) * 2 + 1 - upper) * CORES + core


def my_y():
    return lax.axis_index("dp") // CORES % sizes()[2]


def pack_kernel(
    tokens_hbm, grad_hbm, ids_hbm, scores_hbm, out_ref,
    tokens_ref, grad_ref, ids_ref, scores_ref, weighted_ref, sems,
):
    copies = [
        pltpu.make_async_copy(src, dst, sems.at[i])
        for i, (src, dst) in enumerate((
            (ids_hbm, ids_ref),
            (scores_hbm, scores_ref),
            (tokens_hbm, tokens_ref),
            (grad_hbm, grad_ref),
        ))
    ]
    for copy in copies:
        copy.start()
    for copy in copies:
        copy.wait()
    places, tok_dev, _ = out_ref.shape
    width = tokens_ref.shape[2]
    experts = lax.axis_size("expert")
    first = lax.axis_index("expert") * tok_dev
    ids = ids_ref[0]
    scores = scores_ref[0].astype(jnp.float32)
    token = lax.broadcasted_iota(jnp.int32, ids.shape, 1)
    lane = lax.broadcasted_iota(jnp.int32, (ids.shape[0], LANES), 1)
    row = lax.broadcasted_iota(jnp.int32, (tok_dev, LANES), 0)
    table = jnp.zeros((tok_dev, LANES), jnp.float32)
    for i in range(tok_dev):
        mine = token == first + i
        named = jnp.sum(jnp.where(mine, ids, 0), axis=1, keepdims=True)
        score = jnp.sum(jnp.where(mine, scores, 0.0), axis=1, keepdims=True)
        weights = jnp.sum(jnp.where(lane == named, score, 0.0), axis=0, keepdims=True)
        table = jnp.where(row == i, weights, table)
    grad = grad_ref[0].astype(jnp.float32)
    for expert in range(experts):
        weighted_ref[expert] = (grad * table[:, expert : expert + 1]).astype(jnp.bfloat16)

    def write(place, carry):
        out_ref[place, :, :width] = tokens_ref[0]
        out_ref[place, :, width:] = weighted_ref[place_at(place)[0]]
        return carry

    lax.fori_loop(0, places, write, 0, unroll=places <= 16)


def pack(tokens, out_grad, expert_ids, gate_scores, places):
    _, tok_dev, width = tokens.shape
    operands = [
        pltpu.with_memory_space_constraint(a, pltpu.HBM)
        for a in (
            tokens, out_grad, jnp.swapaxes(expert_ids, 1, 2), jnp.swapaxes(gate_scores, 1, 2)
        )
    ]
    return pl.pallas_call(
        pack_kernel,
        out_shape=jax.ShapeDtypeStruct((places, tok_dev, 2 * width), jnp.bfloat16),
        in_specs=[HBM] * 4,
        out_specs=VMEM,
        scratch_shapes=[pltpu.VMEM(a.shape, a.dtype) for a in operands]
        + [
            pltpu.VMEM((lax.axis_size("expert"), tok_dev, width), jnp.bfloat16),
            pltpu.SemaphoreType.DMA((4,)),
        ],
        compiler_params=vmem(16 << 20),
    )(*operands)


def copy_pieces(src, dst, sems):
    rows = dst.shape[0] // PIECES
    parts = [pl.ds(piece * rows, rows) for piece in range(PIECES)]
    return [
        pltpu.make_async_copy(src.at[0, part], dst.at[part], sems.at[piece])
        for piece, part in enumerate(parts)
    ]


def lay_out(src_ref, x_ref, dy_ref, first):
    chips, tok_dev, _ = src_ref.shape
    width = x_ref.shape[1]
    per_tile = TILE // tok_dev

    def step(tile, carry):
        rows = pl.ds(pl.multiple_of(first + tile * TILE, TILE), TILE)
        blocks = [src_ref[tile * per_tile + j] for j in range(per_tile)]
        x_ref[rows] = jnp.concatenate([b[:, :width] for b in blocks], axis=0)
        dy_ref[rows] = jnp.concatenate([b[:, width:] for b in blocks], axis=0)
        return carry

    tiles = chips // per_tile
    lax.fori_loop(0, tiles, step, 0, unroll=tiles <= 2)


def fetch_kernel(
    mine_ref, gate_hbm, up_hbm, down_hbm, gate_ref, up_ref, down_ref, x_ref, dy_ref, sems
):
    copies = copy_pieces(gate_hbm, gate_ref, sems.at[0])
    copies += copy_pieces(up_hbm, up_ref, sems.at[1])
    copies += copy_pieces(down_hbm, down_ref, sems.at[2])
    for copy in copies:
        copy.start()
    lay_out(mine_ref, x_ref, dy_ref, 0)
    for copy in copies:
        copy.wait()


def fetch(mine, *weights):
    places, tok_dev, row = mine.shape
    rows = (places * tok_dev, row // 2)
    moved = sum(2 * w.size for w in weights)
    weights = [pltpu.with_memory_space_constraint(w, pltpu.HBM) for w in weights]
    return pl.pallas_call(
        fetch_kernel,
        out_shape=tuple(pltpu.VMEM(w.shape[1:], w.dtype) for w in weights)
        + (pltpu.VMEM(rows, jnp.bfloat16), pltpu.VMEM(rows, jnp.bfloat16)),
        in_specs=[VMEM] + [HBM] * 3,
        out_specs=(VMEM,) * 5,
        scratch_shapes=[pltpu.SemaphoreType.DMA((3, PIECES))],
        cost_estimate=pl.CostEstimate(flops=0, bytes_accessed=2 * moved, transcendentals=0),
        compiler_params=vmem((4 << 20) + 2 * moved + 8 * mine.size),
    )(mine, *weights)


def lay_kernel(*refs):
    *src_refs, x_ref, dy_ref = refs
    for i, src_ref in enumerate(src_refs):
        lay_out(src_ref, x_ref, dy_ref, i * (x_ref.shape[0] // len(src_refs)))


def lay(*blocks):
    places, tok_dev, row = blocks[0].shape
    rows = (len(blocks) * places * tok_dev, row // 2)
    return pl.pallas_call(
        lay_kernel,
        out_shape=(pltpu.VMEM(rows, jnp.bfloat16), pltpu.VMEM(rows, jnp.bfloat16)),
        in_specs=[VMEM] * len(blocks),
        out_specs=(VMEM,) * 2,
        cost_estimate=pl.CostEstimate(
            flops=0, bytes_accessed=8 * len(blocks) * blocks[0].size, transcendentals=0
        ),
        compiler_params=vmem((8 << 20) + 8 * len(blocks) * blocks[0].size),
    )(*blocks)


def my_core():
    return lax.axis_index("dp") % CORES


def row_blocks(rows, step):
    step(0, True)
    if rows > ROWS:
        pl.loop(1, rows // ROWS)(lambda block: step(block, False))


def half_total(gate_delta, up_delta, gate_ref, up_ref, core):
    columns = gate_ref.shape[0] // CORES
    part = pl.ds(pl.multiple_of(core * columns, columns), columns)
    total = lax.dot_general(
        gate_delta, gate_ref[part], CONTRACT_LAST, preferred_element_type=jnp.float32
    )
    return total + lax.dot_general(
        up_delta, up_ref[part], CONTRACT_LAST, preferred_element_type=jnp.float32
    )


def store_groups(ref, first, total):
    rows, columns = total.shape
    groups = columns // LANES
    for c in range(groups):
        ref[pl.ds(first + c, rows, stride=groups)] = total[:, c * LANES : (c + 1) * LANES]


def rows_kernel(*refs):
    along_y = sizes()[2]
    other_refs, refs = refs[: along_y - 1], refs[along_y - 1 :]
    my_x_ref, my_dy_ref, laid_x_ref, laid_dy_ref, gate_ref, up_ref, down_ref, *refs = refs
    sent_ref, x_ref, dy_ref, gate_delta_ref, up_delta_ref, hidden_ref, total_ref = refs
    size = my_x_ref.shape[0]
    x_ref[:size] = my_x_ref[...]
    dy_ref[:size] = my_dy_ref[...]
    for i in range(along_y):
        there = pl.ds(size if i == 0 else 2 * i * size, size)
        x_ref[there] = laid_x_ref[i * size : (i + 1) * size]
        dy_ref[there] = laid_dy_ref[i * size : (i + 1) * size]
    for i, other_ref in enumerate(other_refs):
        lay_out(other_ref, x_ref, dy_ref, (2 * i + 3) * size)

    def step(block, first):
        rows = pl.ds(pl.multiple_of(block * ROWS, ROWS), ROWS)
        x = x_ref[rows]
        pre_gate = jnp.dot(x, gate_ref[...], preferred_element_type=jnp.float32)
        pre_up = jnp.dot(x, up_ref[...], preferred_element_type=jnp.float32)
        sigmoid_gate = jax.nn.sigmoid(pre_gate)
        activated = pre_gate * sigmoid_gate
        slope = sigmoid_gate * (1.0 + pre_gate * (1.0 - sigmoid_gate))
        hidden_ref[rows] = (activated * pre_up).astype(jnp.bfloat16)
        grad_hidden = lax.dot_general(
            dy_ref[rows], down_ref[...], CONTRACT_LAST, preferred_element_type=jnp.float32
        )
        gate_delta = (grad_hidden * pre_up * slope).astype(jnp.bfloat16)
        up_delta = (grad_hidden * activated).astype(jnp.bfloat16)
        gate_delta_ref[rows] = gate_delta
        up_delta_ref[rows] = up_delta
        total = half_total(gate_delta, up_delta, gate_ref, up_ref, 1 - my_core())
        store_groups(total_ref, 0, total)
        size = total_ref.shape[0]
        part = pl.ds(pl.multiple_of(block * size, size), size)
        sent_ref[part] = total_ref[...].astype(jnp.bfloat16)

    row_blocks(x_ref.shape[0], step)


def rows_pass(others, my_x, my_dy, laid_x, laid_dy, gate, up, down):
    width, hidden = gate.shape
    rows = CORES * laid_x.shape[0]
    groups = width // CORES // LANES
    bf16 = functools.partial(jax.ShapeDtypeStruct, dtype=jnp.bfloat16)
    moved = rows * (6 * width + 3 * hidden) * 2
    return pl.pallas_call(
        rows_kernel,
        out_shape=(
            bf16((rows * groups, LANES)),
            bf16((rows, width)),
            bf16((rows, width)),
            bf16((rows, hidden)),
            bf16((rows, hidden)),
            bf16((rows, hidden)),
        ),
        in_specs=[VMEM] * (len(others) + 7),
        out_specs=(VMEM,) * 6,
        scratch_shapes=[pltpu.VMEM((ROWS * groups, LANES), jnp.float32)],
        cost_estimate=pl.CostEstimate(
            flops=8 * rows * width * hidden, bytes_accessed=moved, transcendentals=rows * hidden
        ),
        compiler_params=vmem((12 << 20) + 2 * moved),
    )(*others, my_x, my_dy, laid_x, laid_dy, gate, up, down)


def finish_kernel(gate_delta_ref, up_delta_ref, gate_ref, up_ref, total_ref):
    rows_all = gate_delta_ref.shape[0]
    size = total_ref.shape[0] // rows_all * ROWS

    def step(block, first):
        rows = pl.ds(pl.multiple_of(block * ROWS, ROWS), ROWS)
        total = half_total(
            gate_delta_ref[rows], up_delta_ref[rows], gate_ref, up_ref, my_core()
        )
        store_groups(total_ref, block * size, total)

    row_blocks(rows_all, step)


def finish(gate_delta, up_delta, gate, up):
    rows, hidden = gate_delta.shape
    columns = gate.shape[0] // CORES
    moved = 4 * columns * hidden + 4 * rows * (columns + hidden)
    return pl.pallas_call(
        finish_kernel,
        out_shape=jax.ShapeDtypeStruct((rows * columns // LANES, LANES), jnp.float32),
        in_specs=[VMEM] * 4,
        out_specs=VMEM,
        cost_estimate=pl.CostEstimate(
            flops=4 * rows * columns * hidden, bytes_accessed=moved, transcendentals=0
        ),
        compiler_params=vmem((16 << 20) + 2 * moved),
    )(gate_delta, up_delta, gate, up)


def share_kernel(total_ref, got_ref, shares_ref):
    devices, size, _ = shares_ref.shape
    experts, along_z, along_y, _ = sizes()
    places = experts * along_z
    y, core = my_y(), my_core()

    def step(row, carry):
        shift, half, place = row // (CORES * places), row // places % CORES, row % places
        got_row = row + (1 - 2 * half) * places
        here = pl.ds(pl.multiple_of(row * size, size), size)
        there = pl.ds(pl.multiple_of(got_row * size, size), size)
        expert, z = place_at(place)
        owner = order_of(expert, z, (y + shift) % along_y, (core + half) % CORES)
        total = total_ref[here] + got_ref[there].astype(jnp.float32)
        shares_ref[owner] = total.astype(jnp.bfloat16)
        return carry

    lax.fori_loop(0, devices, step, 0, unroll=devices <= 32)


def share(total, got, devices):
    size = total.shape[0] // devices
    return pl.pallas_call(
        share_kernel,
        out_shape=pltpu.VMEM((devices, size, LANES), jnp.bfloat16),
        in_specs=[VMEM] * 2,
        out_specs=VMEM,
        compiler_params=vmem((8 << 20) + 32 * total.size),
    )(total, got)


def sum_kernel(shares_ref, out_hbm, wide_ref, out_ref, sem):
    devices, size, _ = shares_ref.shape
    _, tok_dev, width = out_ref.shape
    groups = size // tok_dev
    for core in range(CORES):
        total = lax.fori_loop(
            0,
            devices // CORES,
            lambda i, acc: acc + shares_ref[i * CORES + core].astype(jnp.float32),
            jnp.zeros((size, LANES), jnp.float32),
            unroll=devices <= 32,
        )
        for row in range(size):
            token, lane = row // groups, (core * groups + row % groups) * LANES
            wide_ref[token : token + 1, lane : lane + LANES] = total[row : row + 1]
    out_ref[0] = wide_ref[...].astype(jnp.bfloat16)
    copy = pltpu.make_async_copy(out_ref, out_hbm, sem)
    copy.start()
    copy.wait()


def sum_shares(shares, tok_dev):
    _, size, _ = shares.shape
    width = CORES * size // tok_dev * LANES
    return pl.pallas_call(
        sum_kernel,
        out_shape=pltpu.HBM((1, tok_dev, width), jnp.bfloat16),
        in_specs=[VMEM],
        out_specs=HBM,
        scratch_shapes=[
            pltpu.VMEM((tok_dev, width), jnp.float32),
            pltpu.VMEM((1, tok_dev, width), jnp.bfloat16),
            pltpu.SemaphoreType.DMA,
        ],
        compiler_params=vmem(16 << 20),
    )(shares)


def local(tokens, out_grad, expert_ids, gate_scores, w_gate, w_up, w_down):
    experts, along_z, along_y, _ = sizes()
    places = experts * along_z
    devices = places * along_y * CORES
    groups = [
        [device_at(expert, z, y, core) for expert, z in map(place_at, range(places))]
        for y in range(along_y)
        for core in range(CORES)
    ]
    core_pairs = [(d, d ^ 1) for d in range(devices)]

    def from_y(shift):
        return [
            (device_at(e, z, (y + shift) % along_y, c), device_at(e, z, y, c))
            for e in range(experts)
            for z in range(along_z)
            for y in range(along_y)
            for c in range(CORES)
        ]

    copies = pack(tokens, out_grad, expert_ids, gate_scores, places)
    mine = lax.all_to_all(copies, BOTH, 0, 0, axis_index_groups=groups, tiled=True)
    beside = [lax.ppermute(mine, BOTH, from_y(shift)) for shift in range(1, along_y)]
    other = lax.ppermute(mine, BOTH, core_pairs)
    gate, up, down, my_x, my_dy = fetch(mine, w_gate, w_up, w_down)
    *beside, my_x = lax.optimization_barrier((*beside, my_x))
    others = [lax.ppermute(piece, BOTH, core_pairs) for piece in beside]
    laid_x, laid_dy = lay(other, *beside)
    sent, x, dy, gate_delta, up_delta, hidden = rows_pass(
        others, my_x, my_dy, laid_x, laid_dy, gate, up, down
    )
    got = lax.ppermute(sent, BOTH, core_pairs)
    total = finish(gate_delta, up_delta, gate, up)
    got, gate_delta, up_delta, hidden = lax.optimization_barrier(
        (got, gate_delta, up_delta, hidden)
    )
    shares = share(total, got, devices)
    everyone = [[order_at(place) for place in range(devices)]]
    shares = lax.all_to_all(shares, BOTH, 0, 0, axis_index_groups=everyone, tiled=True)
    token_grad = sum_shares(shares, tokens.shape[1])
    grad_down = jnp.dot(hidden.T, dy, preferred_element_type=jnp.float32)
    grad_gate = jnp.dot(x.T, gate_delta, preferred_element_type=jnp.float32)
    grad_up = jnp.dot(x.T, up_delta, preferred_element_type=jnp.float32)
    weight_grads = (grad_gate, grad_up, grad_down)
    return (token_grad,) + tuple(g.astype(jnp.bfloat16)[None] for g in weight_grads)


def solution(mesh):
    return jax.shard_map(
        local,
        mesh=mesh,
        in_specs=(
            P("dp", "expert", None),
            P("dp", "expert", None),
            P("dp", None, None),
            P("dp", None, None),
            P("expert", None, "dp"),
            P("expert", None, "dp"),
            P("expert", "dp", None),
        ),
        out_specs=(
            P("dp", "expert", None),
            P("expert", None, "dp"),
            P("expert", None, "dp"),
            P("expert", "dp", None),
        ),
        check_vma=False,
    )
```

```python
import functools

import jax
import jax.numpy as jnp
from jax import lax
from jax.experimental import pallas as pl
from jax.experimental.pallas import tpu as pltpu
from jax.sharding import PartitionSpec as P

LANES = 128
CORES = 2
BOTH = ("expert", "dp")
ROWS = 64
TILE = 16
CONTRACT_LAST = (((1,), (1,)), ((), ()))
PIECES = 4
VMEM = pl.BlockSpec(memory_space=pltpu.VMEM)
HBM = pl.BlockSpec(memory_space=pltpu.HBM)


def vmem(size):
    return pltpu.CompilerParams(vmem_limit_bytes=min(size, 36 << 20))


def sizes():
    dp = lax.axis_size("dp")
    along_y = 1
    while (2 * along_y) ** 2 <= dp // CORES:
        along_y *= 2
    return lax.axis_size("expert"), dp // CORES // along_y, along_y, CORES


def device_at(expert, z, y, core):
    _, along_z, along_y, _ = sizes()
    return ((expert * along_z + z) * along_y + y) * CORES + core


def z_at(step):
    upper = 1 - step % 2
    return sizes()[1] // 2 + upper * (step // 2) - (1 - upper) * (1 + step // 2)


def place_at(place):
    experts = sizes()[0]
    pair = place // 2
    return pair % experts, z_at(place % 2 + 2 * (pair // experts))


def order_at(place):
    experts, _, along_y, _ = sizes()
    place, core = place // CORES, place % CORES
    place, turn = place // 2, place % 2
    place, expert = place // experts, place % experts
    y = place % along_y
    y = y + turn * (along_y - 1 - 2 * y)
    return device_at(expert, z_at(turn + 2 * (place // along_y)), y, core)


def order_of(expert, z, y, core):
    experts, along_z, along_y, _ = sizes()
    upper = (z >= along_z // 2) * 1
    step = upper * (z - along_z // 2) + (1 - upper) * (along_z // 2 - 1 - z)
    y = y + (1 - upper) * (along_y - 1 - 2 * y)
    return (((step * along_y + y) * experts + expert) * 2 + 1 - upper) * CORES + core


def my_y():
    return lax.axis_index("dp") // CORES % sizes()[2]


def pack_kernel(
    tokens_hbm, grad_hbm, ids_hbm, scores_hbm, out_ref,
    tokens_ref, grad_ref, ids_ref, scores_ref, weighted_ref, sems,
):
    copies = [
        pltpu.make_async_copy(src, dst, sems.at[i])
        for i, (src, dst) in enumerate((
            (ids_hbm, ids_ref),
            (scores_hbm, scores_ref),
            (tokens_hbm, tokens_ref),
            (grad_hbm, grad_ref),
        ))
    ]
    for copy in copies:
        copy.start()
    for copy in copies:
        copy.wait()
    places, tok_dev, _ = out_ref.shape
    width = tokens_ref.shape[2]
    experts = lax.axis_size("expert")
    first = lax.axis_index("expert") * tok_dev
    ids = ids_ref[0]
    scores = scores_ref[0].astype(jnp.float32)
    token = lax.broadcasted_iota(jnp.int32, ids.shape, 1)
    lane = lax.broadcasted_iota(jnp.int32, (ids.shape[0], LANES), 1)
    row = lax.broadcasted_iota(jnp.int32, (tok_dev, LANES), 0)
    table = jnp.zeros((tok_dev, LANES), jnp.float32)
    for i in range(tok_dev):
        mine = token == first + i
        named = jnp.sum(jnp.where(mine, ids, 0), axis=1, keepdims=True)
        score = jnp.sum(jnp.where(mine, scores, 0.0), axis=1, keepdims=True)
        weights = jnp.sum(jnp.where(lane == named, score, 0.0), axis=0, keepdims=True)
        table = jnp.where(row == i, weights, table)
    grad = grad_ref[0].astype(jnp.float32)
    for expert in range(experts):
        weighted_ref[expert] = (grad * table[:, expert : expert + 1]).astype(jnp.bfloat16)

    def write(place, carry):
        out_ref[place, :, :width] = tokens_ref[0]
        out_ref[place, :, width:] = weighted_ref[place_at(place)[0]]
        return carry

    lax.fori_loop(0, places, write, 0, unroll=places <= 16)


def pack(tokens, out_grad, expert_ids, gate_scores, places):
    _, tok_dev, width = tokens.shape
    operands = [
        pltpu.with_memory_space_constraint(a, pltpu.HBM)
        for a in (
            tokens, out_grad, jnp.swapaxes(expert_ids, 1, 2), jnp.swapaxes(gate_scores, 1, 2)
        )
    ]
    return pl.pallas_call(
        pack_kernel,
        out_shape=jax.ShapeDtypeStruct((places, tok_dev, 2 * width), jnp.bfloat16),
        in_specs=[HBM] * 4,
        out_specs=VMEM,
        scratch_shapes=[pltpu.VMEM(a.shape, a.dtype) for a in operands]
        + [
            pltpu.VMEM((lax.axis_size("expert"), tok_dev, width), jnp.bfloat16),
            pltpu.SemaphoreType.DMA((4,)),
        ],
        compiler_params=vmem(16 << 20),
    )(*operands)


def copy_pieces(src, dst, sems):
    rows = dst.shape[0] // PIECES
    parts = [pl.ds(piece * rows, rows) for piece in range(PIECES)]
    return [
        pltpu.make_async_copy(src.at[0, part], dst.at[part], sems.at[piece])
        for piece, part in enumerate(parts)
    ]


def lay_out(src_ref, x_ref, dy_ref, first):
    chips, tok_dev, _ = src_ref.shape
    width = x_ref.shape[1]
    per_tile = TILE // tok_dev

    def step(tile, carry):
        rows = pl.ds(pl.multiple_of(first + tile * TILE, TILE), TILE)
        blocks = [src_ref[tile * per_tile + j] for j in range(per_tile)]
        x_ref[rows] = jnp.concatenate([b[:, :width] for b in blocks], axis=0)
        dy_ref[rows] = jnp.concatenate([b[:, width:] for b in blocks], axis=0)
        return carry

    tiles = chips // per_tile
    lax.fori_loop(0, tiles, step, 0, unroll=tiles <= 2)


def fetch_kernel(
    mine_ref, gate_hbm, up_hbm, down_hbm, gate_ref, up_ref, down_ref, x_ref, dy_ref, sems
):
    copies = copy_pieces(gate_hbm, gate_ref, sems.at[0])
    copies += copy_pieces(up_hbm, up_ref, sems.at[1])
    copies += copy_pieces(down_hbm, down_ref, sems.at[2])
    for copy in copies:
        copy.start()
    lay_out(mine_ref, x_ref, dy_ref, 0)
    for copy in copies:
        copy.wait()


def fetch(mine, *weights):
    places, tok_dev, row = mine.shape
    rows = (places * tok_dev, row // 2)
    moved = sum(2 * w.size for w in weights)
    weights = [pltpu.with_memory_space_constraint(w, pltpu.HBM) for w in weights]
    return pl.pallas_call(
        fetch_kernel,
        out_shape=tuple(pltpu.VMEM(w.shape[1:], w.dtype) for w in weights)
        + (pltpu.VMEM(rows, jnp.bfloat16), pltpu.VMEM(rows, jnp.bfloat16)),
        in_specs=[VMEM] + [HBM] * 3,
        out_specs=(VMEM,) * 5,
        scratch_shapes=[pltpu.SemaphoreType.DMA((3, PIECES))],
        cost_estimate=pl.CostEstimate(flops=0, bytes_accessed=2 * moved, transcendentals=0),
        compiler_params=vmem((4 << 20) + 2 * moved + 8 * mine.size),
    )(mine, *weights)


def lay_kernel(*refs):
    *src_refs, x_ref, dy_ref = refs
    for i, src_ref in enumerate(src_refs):
        lay_out(src_ref, x_ref, dy_ref, i * (x_ref.shape[0] // len(src_refs)))


def lay(*blocks):
    places, tok_dev, row = blocks[0].shape
    rows = (len(blocks) * places * tok_dev, row // 2)
    return pl.pallas_call(
        lay_kernel,
        out_shape=(pltpu.VMEM(rows, jnp.bfloat16), pltpu.VMEM(rows, jnp.bfloat16)),
        in_specs=[VMEM] * len(blocks),
        out_specs=(VMEM,) * 2,
        cost_estimate=pl.CostEstimate(
            flops=0, bytes_accessed=8 * len(blocks) * blocks[0].size, transcendentals=0
        ),
        compiler_params=vmem((8 << 20) + 8 * len(blocks) * blocks[0].size),
    )(*blocks)


def my_core():
    return lax.axis_index("dp") % CORES


def row_blocks(rows, step):
    step(0, True)
    if rows > ROWS:
        pl.loop(1, rows // ROWS)(lambda block: step(block, False))


def half_total(gate_delta, up_delta, gate_ref, up_ref, core):
    columns = gate_ref.shape[0] // CORES
    part = pl.ds(pl.multiple_of(core * columns, columns), columns)
    total = lax.dot_general(
        gate_delta, gate_ref[part], CONTRACT_LAST, preferred_element_type=jnp.float32
    )
    return total + lax.dot_general(
        up_delta, up_ref[part], CONTRACT_LAST, preferred_element_type=jnp.float32
    )


def store_groups(ref, first, total):
    rows, columns = total.shape
    groups = columns // LANES
    for c in range(groups):
        ref[pl.ds(first + c, rows, stride=groups)] = total[:, c * LANES : (c + 1) * LANES]


def rows_kernel(*refs):
    along_y = sizes()[2]
    other_refs, refs = refs[: along_y - 1], refs[along_y - 1 :]
    my_x_ref, my_dy_ref, laid_x_ref, laid_dy_ref, gate_ref, up_ref, down_ref, *refs = refs
    sent_ref, x_ref, dy_ref, gate_delta_ref, up_delta_ref, hidden_ref, total_ref = refs
    size = my_x_ref.shape[0]
    x_ref[:size] = my_x_ref[...]
    dy_ref[:size] = my_dy_ref[...]
    for i in range(along_y):
        there = pl.ds(size if i == 0 else 2 * i * size, size)
        x_ref[there] = laid_x_ref[i * size : (i + 1) * size]
        dy_ref[there] = laid_dy_ref[i * size : (i + 1) * size]
    for i, other_ref in enumerate(other_refs):
        lay_out(other_ref, x_ref, dy_ref, (2 * i + 3) * size)

    def step(block, first):
        rows = pl.ds(pl.multiple_of(block * ROWS, ROWS), ROWS)
        x = x_ref[rows]
        pre_gate = jnp.dot(x, gate_ref[...], preferred_element_type=jnp.float32)
        pre_up = jnp.dot(x, up_ref[...], preferred_element_type=jnp.float32)
        sigmoid_gate = jax.nn.sigmoid(pre_gate)
        activated = pre_gate * sigmoid_gate
        slope = sigmoid_gate * (1.0 + pre_gate * (1.0 - sigmoid_gate))
        hidden_ref[rows] = (activated * pre_up).astype(jnp.bfloat16)
        grad_hidden = lax.dot_general(
            dy_ref[rows], down_ref[...], CONTRACT_LAST, preferred_element_type=jnp.float32
        )
        gate_delta = (grad_hidden * pre_up * slope).astype(jnp.bfloat16)
        up_delta = (grad_hidden * activated).astype(jnp.bfloat16)
        gate_delta_ref[rows] = gate_delta
        up_delta_ref[rows] = up_delta
        total = half_total(gate_delta, up_delta, gate_ref, up_ref, 1 - my_core())
        store_groups(total_ref, 0, total)
        size = total_ref.shape[0]
        part = pl.ds(pl.multiple_of(block * size, size), size)
        sent_ref[part] = total_ref[...].astype(jnp.bfloat16)

    row_blocks(x_ref.shape[0], step)


def rows_pass(others, my_x, my_dy, laid_x, laid_dy, gate, up, down):
    width, hidden = gate.shape
    rows = CORES * laid_x.shape[0]
    groups = width // CORES // LANES
    bf16 = functools.partial(jax.ShapeDtypeStruct, dtype=jnp.bfloat16)
    moved = rows * (6 * width + 3 * hidden) * 2
    return pl.pallas_call(
        rows_kernel,
        out_shape=(
            bf16((rows * groups, LANES)),
            bf16((rows, width)),
            bf16((rows, width)),
            bf16((rows, hidden)),
            bf16((rows, hidden)),
            bf16((rows, hidden)),
        ),
        in_specs=[VMEM] * (len(others) + 7),
        out_specs=(VMEM,) * 6,
        scratch_shapes=[pltpu.VMEM((ROWS * groups, LANES), jnp.float32)],
        cost_estimate=pl.CostEstimate(
            flops=8 * rows * width * hidden, bytes_accessed=moved, transcendentals=rows * hidden
        ),
        compiler_params=vmem((12 << 20) + 2 * moved),
    )(*others, my_x, my_dy, laid_x, laid_dy, gate, up, down)


def finish_kernel(gate_delta_ref, up_delta_ref, gate_ref, up_ref, total_ref):
    rows_all = gate_delta_ref.shape[0]
    size = total_ref.shape[0] // rows_all * ROWS

    def step(block, first):
        rows = pl.ds(pl.multiple_of(block * ROWS, ROWS), ROWS)
        total = half_total(
            gate_delta_ref[rows], up_delta_ref[rows], gate_ref, up_ref, my_core()
        )
        store_groups(total_ref, block * size, total)

    row_blocks(rows_all, step)


def finish(gate_delta, up_delta, gate, up):
    rows, hidden = gate_delta.shape
    columns = gate.shape[0] // CORES
    moved = 4 * columns * hidden + 4 * rows * (columns + hidden)
    return pl.pallas_call(
        finish_kernel,
        out_shape=jax.ShapeDtypeStruct((rows * columns // LANES, LANES), jnp.float32),
        in_specs=[VMEM] * 4,
        out_specs=VMEM,
        cost_estimate=pl.CostEstimate(
            flops=4 * rows * columns * hidden, bytes_accessed=moved, transcendentals=0
        ),
        compiler_params=vmem((16 << 20) + 2 * moved),
    )(gate_delta, up_delta, gate, up)


def share_kernel(total_ref, got_ref, shares_ref):
    devices, size, _ = shares_ref.shape
    experts, along_z, along_y, _ = sizes()
    places = experts * along_z
    y, core = my_y(), my_core()

    def step(row, carry):
        shift, half, place = row // (CORES * places), row // places % CORES, row % places
        got_row = row + (1 - 2 * half) * places
        here = pl.ds(pl.multiple_of(row * size, size), size)
        there = pl.ds(pl.multiple_of(got_row * size, size), size)
        expert, z = place_at(place)
        owner = order_of(expert, z, (y + shift) % along_y, (core + half) % CORES)
        total = total_ref[here] + got_ref[there].astype(jnp.float32)
        shares_ref[owner] = total.astype(jnp.bfloat16)
        return carry

    lax.fori_loop(0, devices, step, 0, unroll=devices <= 32)


def share(total, got, devices):
    size = total.shape[0] // devices
    return pl.pallas_call(
        share_kernel,
        out_shape=pltpu.VMEM((devices, size, LANES), jnp.bfloat16),
        in_specs=[VMEM] * 2,
        out_specs=VMEM,
        compiler_params=vmem((8 << 20) + 32 * total.size),
    )(total, got)


def sum_kernel(shares_ref, out_hbm, wide_ref, out_ref, sem):
    devices, size, _ = shares_ref.shape
    _, tok_dev, width = out_ref.shape
    groups = size // tok_dev
    for core in range(CORES):
        total = lax.fori_loop(
            0,
            devices // CORES,
            lambda i, acc: acc + shares_ref[i * CORES + core].astype(jnp.float32),
            jnp.zeros((size, LANES), jnp.float32),
            unroll=devices <= 32,
        )
        for row in range(size):
            token, lane = row // groups, (core * groups + row % groups) * LANES
            wide_ref[token : token + 1, lane : lane + LANES] = total[row : row + 1]
    out_ref[0] = wide_ref[...].astype(jnp.bfloat16)
    copy = pltpu.make_async_copy(out_ref, out_hbm, sem)
    copy.start()
    copy.wait()


def sum_shares(shares, tok_dev):
    _, size, _ = shares.shape
    width = CORES * size // tok_dev * LANES
    return pl.pallas_call(
        sum_kernel,
        out_shape=pltpu.HBM((1, tok_dev, width), jnp.bfloat16),
        in_specs=[VMEM],
        out_specs=HBM,
        scratch_shapes=[
            pltpu.VMEM((tok_dev, width), jnp.float32),
            pltpu.VMEM((1, tok_dev, width), jnp.bfloat16),
            pltpu.SemaphoreType.DMA,
        ],
        compiler_params=vmem(16 << 20),
    )(shares)


def local(tokens, out_grad, expert_ids, gate_scores, w_gate, w_up, w_down):
    experts, along_z, along_y, _ = sizes()
    places = experts * along_z
    devices = places * along_y * CORES
    groups = [
        [device_at(expert, z, y, core) for expert, z in map(place_at, range(places))]
        for y in range(along_y)
        for core in range(CORES)
    ]
    core_pairs = [(d, d ^ 1) for d in range(devices)]

    def from_y(shift):
        return [
            (device_at(e, z, (y + shift) % along_y, c), device_at(e, z, y, c))
            for e in range(experts)
            for z in range(along_z)
            for y in range(along_y)
            for c in range(CORES)
        ]

    copies = pack(tokens, out_grad, expert_ids, gate_scores, places)
    mine = lax.all_to_all(copies, BOTH, 0, 0, axis_index_groups=groups, tiled=True)
    beside = [lax.ppermute(mine, BOTH, from_y(shift)) for shift in range(1, along_y)]
    other = lax.ppermute(mine, BOTH, core_pairs)
    gate, up, down, my_x, my_dy = fetch(mine, w_gate, w_up, w_down)
    *beside, my_x = lax.optimization_barrier((*beside, my_x))
    others = [lax.ppermute(piece, BOTH, core_pairs) for piece in beside]
    laid_x, laid_dy = lay(other, *beside)
    sent, x, dy, gate_delta, up_delta, hidden = rows_pass(
        others, my_x, my_dy, laid_x, laid_dy, gate, up, down
    )
    got = lax.ppermute(sent, BOTH, core_pairs)
    total = finish(gate_delta, up_delta, gate, up)
    got, gate_delta, up_delta, hidden = lax.optimization_barrier(
        (got, gate_delta, up_delta, hidden)
    )
    shares = share(total, got, devices)
    everyone = [[order_at(place) for place in range(devices)]]
    shares = lax.all_to_all(shares, BOTH, 0, 0, axis_index_groups=everyone, tiled=True)
    token_grad = sum_shares(shares, tokens.shape[1])
    grad_down = jnp.dot(hidden.T, dy, preferred_element_type=jnp.float32)
    grad_gate = jnp.dot(x.T, gate_delta, preferred_element_type=jnp.float32)
    grad_up = jnp.dot(x.T, up_delta, preferred_element_type=jnp.float32)
    weight_grads = (grad_gate, grad_up, grad_down)
    return (token_grad,) + tuple(g.astype(jnp.bfloat16)[None] for g in weight_grads)


def solution(mesh):
    return jax.shard_map(
        local,
        mesh=mesh,
        in_specs=(
            P("dp", "expert", None),
            P("dp", "expert", None),
            P("dp", None, None),
            P("dp", None, None),
            P("expert", None, "dp"),
            P("expert", None, "dp"),
            P("expert", "dp", None),
        ),
        out_specs=(
            P("dp", "expert", None),
            P("expert", None, "dp"),
            P("expert", None, "dp"),
            P("expert", "dp", None),
        ),
        check_vma=False,
    )
```

```python
import functools

import jax
import jax.numpy as jnp
from jax import lax
from jax.experimental import pallas as pl
from jax.experimental.pallas import tpu as pltpu
from jax.sharding import PartitionSpec as P

LANES = 128
CORES = 2
BOTH = ("expert", "dp")
ROWS = 64
TILE = 16
CONTRACT_LAST = (((1,), (1,)), ((), ()))
PIECES = 4
VMEM = pl.BlockSpec(memory_space=pltpu.VMEM)
HBM = pl.BlockSpec(memory_space=pltpu.HBM)


def vmem(size):
    return pltpu.CompilerParams(vmem_limit_bytes=min(size, 36 << 20))


def sizes():
    dp = lax.axis_size("dp")
    along_y = 1
    while (2 * along_y) ** 2 <= dp // CORES:
        along_y *= 2
    return lax.axis_size("expert"), dp // CORES // along_y, along_y, CORES


def device_at(expert, z, y, core):
    _, along_z, along_y, _ = sizes()
    return ((expert * along_z + z) * along_y + y) * CORES + core


def z_at(step):
    upper = 1 - step % 2
    return sizes()[1] // 2 + upper * (step // 2) - (1 - upper) * (1 + step // 2)


def place_at(place):
    experts, along_z, _, _ = sizes()
    return place % experts, (place // experts + along_z // 2) % along_z


def order_at(place):
    experts, _, along_y, _ = sizes()
    place, core = place // CORES, place % CORES
    place, turn = place // 2, place % 2
    place, expert = place // experts, place % experts
    y = place % along_y
    y = y + turn * (along_y - 1 - 2 * y)
    return device_at(expert, z_at(turn + 2 * (place // along_y)), y, core)


def order_of(expert, z, y, core):
    experts, along_z, along_y, _ = sizes()
    upper = (z >= along_z // 2) * 1
    step = upper * (z - along_z // 2) + (1 - upper) * (along_z // 2 - 1 - z)
    y = y + (1 - upper) * (along_y - 1 - 2 * y)
    return (((step * along_y + y) * experts + expert) * 2 + 1 - upper) * CORES + core


def my_y():
    return lax.axis_index("dp") // CORES % sizes()[2]


def pack_kernel(
    tokens_hbm, grad_hbm, ids_hbm, scores_hbm, out_ref,
    tokens_ref, grad_ref, ids_ref, scores_ref, weighted_ref, sems,
):
    copies = [
        pltpu.make_async_copy(src, dst, sems.at[i])
        for i, (src, dst) in enumerate((
            (ids_hbm, ids_ref),
            (scores_hbm, scores_ref),
            (tokens_hbm, tokens_ref),
            (grad_hbm, grad_ref),
        ))
    ]
    for copy in copies:
        copy.start()
    for copy in copies[:2]:
        copy.wait()
    places, tok_dev, _ = out_ref.shape
    width = tokens_ref.shape[2]
    experts = lax.axis_size("expert")
    first = lax.axis_index("expert") * tok_dev
    ids = ids_ref[0]
    scores = scores_ref[0].astype(jnp.float32)
    token = lax.broadcasted_iota(jnp.int32, ids.shape, 1)
    lane = lax.broadcasted_iota(jnp.int32, (ids.shape[0], LANES), 1)
    row = lax.broadcasted_iota(jnp.int32, (tok_dev, LANES), 0)
    table = jnp.zeros((tok_dev, LANES), jnp.float32)
    for i in range(tok_dev):
        mine = token == first + i
        named = jnp.sum(jnp.where(mine, ids, 0), axis=1, keepdims=True)
        score = jnp.sum(jnp.where(mine, scores, 0.0), axis=1, keepdims=True)
        weights = jnp.sum(jnp.where(lane == named, score, 0.0), axis=0, keepdims=True)
        table = jnp.where(row == i, weights, table)
    for copy in copies[2:]:
        copy.wait()
    grad = grad_ref[0].astype(jnp.float32)
    for expert in range(experts):
        weighted_ref[expert] = (grad * table[:, expert : expert + 1]).astype(jnp.bfloat16)

    def write(place, carry):
        out_ref[place, :, :width] = tokens_ref[0]
        out_ref[place, :, width:] = weighted_ref[place_at(place)[0]]
        return carry

    lax.fori_loop(0, places, write, 0, unroll=places <= 16)


def pack(tokens, out_grad, expert_ids, gate_scores, places):
    _, tok_dev, width = tokens.shape
    operands = [
        pltpu.with_memory_space_constraint(a, pltpu.HBM)
        for a in (
            tokens, out_grad, jnp.swapaxes(expert_ids, 1, 2), jnp.swapaxes(gate_scores, 1, 2)
        )
    ]
    return pl.pallas_call(
        pack_kernel,
        out_shape=jax.ShapeDtypeStruct((places, tok_dev, 2 * width), jnp.bfloat16),
        in_specs=[HBM] * 4,
        out_specs=VMEM,
        scratch_shapes=[pltpu.VMEM(a.shape, a.dtype) for a in operands]
        + [
            pltpu.VMEM((lax.axis_size("expert"), tok_dev, width), jnp.bfloat16),
            pltpu.SemaphoreType.DMA((4,)),
        ],
        compiler_params=vmem(16 << 20),
    )(*operands)


def copy_pieces(src, dst, sems):
    rows = dst.shape[0] // PIECES
    parts = [pl.ds(piece * rows, rows) for piece in range(PIECES)]
    return [
        pltpu.make_async_copy(src.at[0, part], dst.at[part], sems.at[piece])
        for piece, part in enumerate(parts)
    ]


def lay_out(src_ref, x_ref, dy_ref, first):
    chips, tok_dev, _ = src_ref.shape
    width = x_ref.shape[1]
    per_tile = TILE // tok_dev

    def step(tile, carry):
        rows = pl.ds(pl.multiple_of(first + tile * TILE, TILE), TILE)
        blocks = [src_ref[tile * per_tile + j] for j in range(per_tile)]
        x_ref[rows] = jnp.concatenate([b[:, :width] for b in blocks], axis=0)
        dy_ref[rows] = jnp.concatenate([b[:, width:] for b in blocks], axis=0)
        return carry

    tiles = chips // per_tile
    lax.fori_loop(0, tiles, step, 0, unroll=tiles <= 2)


def fetch_kernel(
    mine_ref, gate_hbm, up_hbm, down_hbm, gate_ref, up_ref, down_ref, x_ref, dy_ref, sems
):
    copies = copy_pieces(gate_hbm, gate_ref, sems.at[0])
    copies += copy_pieces(up_hbm, up_ref, sems.at[1])
    copies += copy_pieces(down_hbm, down_ref, sems.at[2])
    for copy in copies:
        copy.start()
    lay_out(mine_ref, x_ref, dy_ref, 0)
    for copy in copies:
        copy.wait()


def fetch(mine, *weights):
    places, tok_dev, row = mine.shape
    rows = (places * tok_dev, row // 2)
    moved = sum(2 * w.size for w in weights)
    weights = [pltpu.with_memory_space_constraint(w, pltpu.HBM) for w in weights]
    return pl.pallas_call(
        fetch_kernel,
        out_shape=tuple(pltpu.VMEM(w.shape[1:], w.dtype) for w in weights)
        + (pltpu.VMEM(rows, jnp.bfloat16), pltpu.VMEM(rows, jnp.bfloat16)),
        in_specs=[VMEM] + [HBM] * 3,
        out_specs=(VMEM,) * 5,
        scratch_shapes=[pltpu.SemaphoreType.DMA((3, PIECES))],
        cost_estimate=pl.CostEstimate(flops=0, bytes_accessed=2 * moved, transcendentals=0),
        compiler_params=vmem((4 << 20) + 2 * moved + 8 * mine.size),
    )(mine, *weights)


def lay_kernel(*refs):
    *src_refs, x_ref, dy_ref = refs
    for i, src_ref in enumerate(src_refs):
        lay_out(src_ref, x_ref, dy_ref, i * (x_ref.shape[0] // len(src_refs)))


def lay(*blocks):
    places, tok_dev, row = blocks[0].shape
    rows = (len(blocks) * places * tok_dev, row // 2)
    return pl.pallas_call(
        lay_kernel,
        out_shape=(pltpu.VMEM(rows, jnp.bfloat16), pltpu.VMEM(rows, jnp.bfloat16)),
        in_specs=[VMEM] * len(blocks),
        out_specs=(VMEM,) * 2,
        cost_estimate=pl.CostEstimate(
            flops=0, bytes_accessed=8 * len(blocks) * blocks[0].size, transcendentals=0
        ),
        compiler_params=vmem((8 << 20) + 8 * len(blocks) * blocks[0].size),
    )(*blocks)


def my_core():
    return lax.axis_index("dp") % CORES


def row_blocks(rows, step):
    step(0, True)
    if rows > ROWS:
        pl.loop(1, rows // ROWS)(lambda block: step(block, False))


def half_total(gate_delta, up_delta, gate_ref, up_ref, core):
    columns = gate_ref.shape[0] // CORES
    part = pl.ds(pl.multiple_of(core * columns, columns), columns)
    total = lax.dot_general(
        gate_delta, gate_ref[part], CONTRACT_LAST, preferred_element_type=jnp.float32
    )
    return total + lax.dot_general(
        up_delta, up_ref[part], CONTRACT_LAST, preferred_element_type=jnp.float32
    )


def store_groups(ref, first, total):
    rows, columns = total.shape
    groups = columns // LANES
    for c in range(groups):
        ref[pl.ds(first + c, rows, stride=groups)] = total[:, c * LANES : (c + 1) * LANES]


def rows_kernel(*refs):
    along_y = sizes()[2]
    other_refs, refs = refs[: along_y - 1], refs[along_y - 1 :]
    my_x_ref, my_dy_ref, laid_x_ref, laid_dy_ref, gate_ref, up_ref, down_ref, *refs = refs
    sent_ref, x_ref, dy_ref, gate_delta_ref, up_delta_ref, hidden_ref, total_ref = refs
    size = my_x_ref.shape[0]
    x_ref[:size] = my_x_ref[...]
    dy_ref[:size] = my_dy_ref[...]
    for i in range(along_y):
        there = pl.ds(size if i == 0 else 2 * i * size, size)
        x_ref[there] = laid_x_ref[i * size : (i + 1) * size]
        dy_ref[there] = laid_dy_ref[i * size : (i + 1) * size]
    for i, other_ref in enumerate(other_refs):
        lay_out(other_ref, x_ref, dy_ref, (2 * i + 3) * size)

    def step(block, first):
        rows = pl.ds(pl.multiple_of(block * ROWS, ROWS), ROWS)
        x = x_ref[rows]
        pre_gate = jnp.dot(x, gate_ref[...], preferred_element_type=jnp.float32)
        pre_up = jnp.dot(x, up_ref[...], preferred_element_type=jnp.float32)
        sigmoid_gate = jax.nn.sigmoid(pre_gate)
        activated = pre_gate * sigmoid_gate
        slope = sigmoid_gate * (1.0 + pre_gate * (1.0 - sigmoid_gate))
        hidden_ref[rows] = (activated * pre_up).astype(jnp.bfloat16)
        grad_hidden = lax.dot_general(
            dy_ref[rows], down_ref[...], CONTRACT_LAST, preferred_element_type=jnp.float32
        )
        gate_delta = (grad_hidden * pre_up * slope).astype(jnp.bfloat16)
        up_delta = (grad_hidden * activated).astype(jnp.bfloat16)
        gate_delta_ref[rows] = gate_delta
        up_delta_ref[rows] = up_delta
        total = half_total(gate_delta, up_delta, gate_ref, up_ref, 1 - my_core())
        store_groups(total_ref, 0, total)
        size = total_ref.shape[0]
        part = pl.ds(pl.multiple_of(block * size, size), size)
        sent_ref[part] = total_ref[...].astype(jnp.bfloat16)

    row_blocks(x_ref.shape[0], step)


def rows_pass(others, my_x, my_dy, laid_x, laid_dy, gate, up, down):
    width, hidden = gate.shape
    rows = CORES * laid_x.shape[0]
    groups = width // CORES // LANES
    bf16 = functools.partial(jax.ShapeDtypeStruct, dtype=jnp.bfloat16)
    moved = rows * (6 * width + 3 * hidden) * 2
    return pl.pallas_call(
        rows_kernel,
        out_shape=(
            bf16((rows * groups, LANES)),
            bf16((rows, width)),
            bf16((rows, width)),
            bf16((rows, hidden)),
            bf16((rows, hidden)),
            bf16((rows, hidden)),
        ),
        in_specs=[VMEM] * (len(others) + 7),
        out_specs=(VMEM,) * 6,
        scratch_shapes=[pltpu.VMEM((ROWS * groups, LANES), jnp.float32)],
        cost_estimate=pl.CostEstimate(
            flops=8 * rows * width * hidden, bytes_accessed=moved, transcendentals=rows * hidden
        ),
        compiler_params=vmem((12 << 20) + 2 * moved),
    )(*others, my_x, my_dy, laid_x, laid_dy, gate, up, down)


def finish_kernel(gate_delta_ref, up_delta_ref, gate_ref, up_ref, total_ref):
    rows_all = gate_delta_ref.shape[0]
    size = total_ref.shape[0] // rows_all * ROWS

    def step(block, first):
        rows = pl.ds(pl.multiple_of(block * ROWS, ROWS), ROWS)
        total = half_total(
            gate_delta_ref[rows], up_delta_ref[rows], gate_ref, up_ref, my_core()
        )
        store_groups(total_ref, block * size, total)

    row_blocks(rows_all, step)


def finish(gate_delta, up_delta, gate, up):
    rows, hidden = gate_delta.shape
    columns = gate.shape[0] // CORES
    moved = 4 * columns * hidden + 4 * rows * (columns + hidden)
    return pl.pallas_call(
        finish_kernel,
        out_shape=jax.ShapeDtypeStruct((rows * columns // LANES, LANES), jnp.float32),
        in_specs=[VMEM] * 4,
        out_specs=VMEM,
        cost_estimate=pl.CostEstimate(
            flops=4 * rows * columns * hidden, bytes_accessed=moved, transcendentals=0
        ),
        compiler_params=vmem((16 << 20) + 2 * moved),
    )(gate_delta, up_delta, gate, up)


def share_kernel(total_ref, got_ref, shares_ref):
    devices, size, _ = shares_ref.shape
    experts, along_z, along_y, _ = sizes()
    places = experts * along_z
    y, core = my_y(), my_core()

    def step(row, carry):
        shift, half, place = row // (CORES * places), row // places % CORES, row % places
        got_row = row + (1 - 2 * half) * places
        here = pl.ds(pl.multiple_of(row * size, size), size)
        there = pl.ds(pl.multiple_of(got_row * size, size), size)
        expert, z = place_at(place)
        owner = order_of(expert, z, (y + shift) % along_y, (core + half) % CORES)
        total = total_ref[here] + got_ref[there].astype(jnp.float32)
        shares_ref[owner] = total.astype(jnp.bfloat16)
        return carry

    lax.fori_loop(0, devices, step, 0, unroll=devices <= 32)


def share(total, got, devices):
    size = total.shape[0] // devices
    return pl.pallas_call(
        share_kernel,
        out_shape=pltpu.VMEM((devices, size, LANES), jnp.bfloat16),
        in_specs=[VMEM] * 2,
        out_specs=VMEM,
        compiler_params=vmem((8 << 20) + 32 * total.size),
    )(total, got)


def sum_kernel(shares_ref, out_hbm, wide_ref, out_ref, sem):
    devices, size, _ = shares_ref.shape
    _, tok_dev, width = out_ref.shape
    groups = size // tok_dev
    for core in range(CORES):
        total = lax.fori_loop(
            0,
            devices // CORES,
            lambda i, acc: acc + shares_ref[i * CORES + core].astype(jnp.float32),
            jnp.zeros((size, LANES), jnp.float32),
            unroll=devices <= 32,
        )
        for row in range(size):
            token, lane = row // groups, (core * groups + row % groups) * LANES
            wide_ref[token : token + 1, lane : lane + LANES] = total[row : row + 1]
    out_ref[0] = wide_ref[...].astype(jnp.bfloat16)
    copy = pltpu.make_async_copy(out_ref, out_hbm, sem)
    copy.start()
    copy.wait()


def sum_shares(shares, tok_dev):
    _, size, _ = shares.shape
    width = CORES * size // tok_dev * LANES
    return pl.pallas_call(
        sum_kernel,
        out_shape=pltpu.HBM((1, tok_dev, width), jnp.bfloat16),
        in_specs=[VMEM],
        out_specs=HBM,
        scratch_shapes=[
            pltpu.VMEM((tok_dev, width), jnp.float32),
            pltpu.VMEM((1, tok_dev, width), jnp.bfloat16),
            pltpu.SemaphoreType.DMA,
        ],
        compiler_params=vmem(16 << 20),
    )(shares)


def local(tokens, out_grad, expert_ids, gate_scores, w_gate, w_up, w_down):
    experts, along_z, along_y, _ = sizes()
    places = experts * along_z
    devices = places * along_y * CORES
    groups = [
        [device_at(expert, z, y, core) for expert, z in map(place_at, range(places))]
        for y in range(along_y)
        for core in range(CORES)
    ]
    core_pairs = [(d, d ^ 1) for d in range(devices)]

    def from_y(shift):
        return [
            (device_at(e, z, (y + shift) % along_y, c), device_at(e, z, y, c))
            for e in range(experts)
            for z in range(along_z)
            for y in range(along_y)
            for c in range(CORES)
        ]

    copies = pack(tokens, out_grad, expert_ids, gate_scores, places)
    mine = lax.all_to_all(copies, BOTH, 0, 0, axis_index_groups=groups, tiled=True)
    beside = [lax.ppermute(mine, BOTH, from_y(shift)) for shift in range(1, along_y)]
    other = lax.ppermute(mine, BOTH, core_pairs)
    gate, up, down, my_x, my_dy = fetch(mine, w_gate, w_up, w_down)
    *beside, my_x = lax.optimization_barrier((*beside, my_x))
    others = [lax.ppermute(piece, BOTH, core_pairs) for piece in beside]
    laid_x, laid_dy = lay(other, *beside)
    sent, x, dy, gate_delta, up_delta, hidden = rows_pass(
        others, my_x, my_dy, laid_x, laid_dy, gate, up, down
    )
    got = lax.ppermute(sent, BOTH, core_pairs)
    total = finish(gate_delta, up_delta, gate, up)
    got, gate_delta, up_delta, hidden = lax.optimization_barrier(
        (got, gate_delta, up_delta, hidden)
    )
    shares = share(total, got, devices)
    everyone = [[order_at(place) for place in range(devices)]]
    shares = lax.all_to_all(shares, BOTH, 0, 0, axis_index_groups=everyone, tiled=True)
    token_grad = sum_shares(shares, tokens.shape[1])
    grad_down = jnp.dot(hidden.T, dy, preferred_element_type=jnp.float32)
    grad_gate = jnp.dot(x.T, gate_delta, preferred_element_type=jnp.float32)
    grad_up = jnp.dot(x.T, up_delta, preferred_element_type=jnp.float32)
    weight_grads = (grad_gate, grad_up, grad_down)
    return (token_grad,) + tuple(g.astype(jnp.bfloat16)[None] for g in weight_grads)


def solution(mesh):
    return jax.shard_map(
        local,
        mesh=mesh,
        in_specs=(
            P("dp", "expert", None),
            P("dp", "expert", None),
            P("dp", None, None),
            P("dp", None, None),
            P("expert", None, "dp"),
            P("expert", None, "dp"),
            P("expert", "dp", None),
        ),
        out_specs=(
            P("dp", "expert", None),
            P("expert", None, "dp"),
            P("expert", None, "dp"),
            P("expert", "dp", None),
        ),
        check_vma=False,
    )
```

```python
import functools

import jax
import jax.numpy as jnp
from jax import lax
from jax.experimental import pallas as pl
from jax.experimental.pallas import tpu as pltpu
from jax.sharding import PartitionSpec as P

LANES = 128
CORES = 2
BOTH = ("expert", "dp")
ROWS = 64
TILE = 16
CONTRACT_LAST = (((1,), (1,)), ((), ()))
PIECES = 4
VMEM = pl.BlockSpec(memory_space=pltpu.VMEM)
HBM = pl.BlockSpec(memory_space=pltpu.HBM)


def vmem(size):
    return pltpu.CompilerParams(vmem_limit_bytes=min(size, 36 << 20))


def sizes():
    dp = lax.axis_size("dp")
    along_y = 1
    while (2 * along_y) ** 2 <= dp // CORES:
        along_y *= 2
    return lax.axis_size("expert"), dp // CORES // along_y, along_y, CORES


def device_at(expert, z, y, core):
    _, along_z, along_y, _ = sizes()
    return ((expert * along_z + z) * along_y + y) * CORES + core


def z_at(step):
    upper = 1 - step % 2
    return sizes()[1] // 2 + upper * (step // 2) - (1 - upper) * (1 + step // 2)


def place_at(place):
    experts = sizes()[0]
    pair = place // 2
    return pair % experts, z_at(place % 2 + 2 * (pair // experts))


def order_at(place):
    experts, _, along_y, _ = sizes()
    place, core = place // CORES, place % CORES
    place, turn = place // 2, place % 2
    place, expert = place // experts, place % experts
    y = place % along_y
    y = y + turn * (along_y - 1 - 2 * y)
    return device_at(expert, z_at(turn + 2 * (place // along_y)), y, core)


def order_of(expert, z, y, core):
    experts, along_z, along_y, _ = sizes()
    upper = (z >= along_z // 2) * 1
    step = upper * (z - along_z // 2) + (1 - upper) * (along_z // 2 - 1 - z)
    y = y + (1 - upper) * (along_y - 1 - 2 * y)
    return (((step * along_y + y) * experts + expert) * 2 + 1 - upper) * CORES + core


def my_y():
    return lax.axis_index("dp") // CORES % sizes()[2]


def pack_kernel(
    tokens_hbm, grad_hbm, ids_hbm, scores_hbm, out_ref,
    tokens_ref, grad_ref, ids_ref, scores_ref, weighted_ref, sems,
):
    copies = [
        pltpu.make_async_copy(src, dst, sems.at[i])
        for i, (src, dst) in enumerate((
            (ids_hbm, ids_ref),
            (scores_hbm, scores_ref),
            (tokens_hbm, tokens_ref),
            (grad_hbm, grad_ref),
        ))
    ]
    for copy in copies:
        copy.start()
    for copy in copies[:2]:
        copy.wait()
    places, tok_dev, _ = out_ref.shape
    width = tokens_ref.shape[2]
    experts = lax.axis_size("expert")
    first = lax.axis_index("expert") * tok_dev
    ids = ids_ref[0]
    scores = scores_ref[0].astype(jnp.float32)
    token = lax.broadcasted_iota(jnp.int32, ids.shape, 1)
    lane = lax.broadcasted_iota(jnp.int32, (ids.shape[0], LANES), 1)
    row = lax.broadcasted_iota(jnp.int32, (tok_dev, LANES), 0)
    table = jnp.zeros((tok_dev, LANES), jnp.float32)
    for i in range(tok_dev):
        mine = token == first + i
        named = jnp.sum(jnp.where(mine, ids, 0), axis=1, keepdims=True)
        score = jnp.sum(jnp.where(mine, scores, 0.0), axis=1, keepdims=True)
        weights = jnp.sum(jnp.where(lane == named, score, 0.0), axis=0, keepdims=True)
        table = jnp.where(row == i, weights, table)
    for copy in copies[2:]:
        copy.wait()
    grad = grad_ref[0].astype(jnp.float32)
    for expert in range(experts):
        weighted_ref[expert] = (grad * table[:, expert : expert + 1]).astype(jnp.bfloat16)

    def write(place, carry):
        out_ref[place, :, :width] = tokens_ref[0]
        out_ref[place, :, width:] = weighted_ref[place_at(place)[0]]
        return carry

    lax.fori_loop(0, places, write, 0, unroll=places <= 16)


def pack(tokens, out_grad, expert_ids, gate_scores, places):
    _, tok_dev, width = tokens.shape
    operands = [
        pltpu.with_memory_space_constraint(a, pltpu.HBM)
        for a in (
            tokens, out_grad, jnp.swapaxes(expert_ids, 1, 2), jnp.swapaxes(gate_scores, 1, 2)
        )
    ]
    return pl.pallas_call(
        pack_kernel,
        out_shape=jax.ShapeDtypeStruct((places, tok_dev, 2 * width), jnp.bfloat16),
        in_specs=[HBM] * 4,
        out_specs=VMEM,
        scratch_shapes=[pltpu.VMEM(a.shape, a.dtype) for a in operands]
        + [
            pltpu.VMEM((lax.axis_size("expert"), tok_dev, width), jnp.bfloat16),
            pltpu.SemaphoreType.DMA((4,)),
        ],
        compiler_params=vmem(16 << 20),
    )(*operands)


def copy_pieces(src, dst, sems):
    rows = dst.shape[0] // PIECES
    parts = [pl.ds(piece * rows, rows) for piece in range(PIECES)]
    return [
        pltpu.make_async_copy(src.at[0, part], dst.at[part], sems.at[piece])
        for piece, part in enumerate(parts)
    ]


def lay_out(src_ref, x_ref, dy_ref, first):
    chips, tok_dev, _ = src_ref.shape
    width = x_ref.shape[1]
    per_tile = TILE // tok_dev

    def step(tile, carry):
        rows = pl.ds(pl.multiple_of(first + tile * TILE, TILE), TILE)
        blocks = [src_ref[tile * per_tile + j] for j in range(per_tile)]
        x_ref[rows] = jnp.concatenate([b[:, :width] for b in blocks], axis=0)
        dy_ref[rows] = jnp.concatenate([b[:, width:] for b in blocks], axis=0)
        return carry

    tiles = chips // per_tile
    lax.fori_loop(0, tiles, step, 0, unroll=tiles <= 2)


def fetch_kernel(
    mine_ref, gate_hbm, up_hbm, down_hbm, gate_ref, up_ref, down_ref, x_ref, dy_ref, sems
):
    copies = copy_pieces(gate_hbm, gate_ref, sems.at[0])
    copies += copy_pieces(up_hbm, up_ref, sems.at[1])
    copies += copy_pieces(down_hbm, down_ref, sems.at[2])
    for copy in copies:
        copy.start()
    lay_out(mine_ref, x_ref, dy_ref, 0)
    for copy in copies:
        copy.wait()


def fetch(mine, *weights):
    places, tok_dev, row = mine.shape
    rows = (places * tok_dev, row // 2)
    moved = sum(2 * w.size for w in weights)
    weights = [pltpu.with_memory_space_constraint(w, pltpu.HBM) for w in weights]
    return pl.pallas_call(
        fetch_kernel,
        out_shape=tuple(pltpu.VMEM(w.shape[1:], w.dtype) for w in weights)
        + (pltpu.VMEM(rows, jnp.bfloat16), pltpu.VMEM(rows, jnp.bfloat16)),
        in_specs=[VMEM] + [HBM] * 3,
        out_specs=(VMEM,) * 5,
        scratch_shapes=[pltpu.SemaphoreType.DMA((3, PIECES))],
        cost_estimate=pl.CostEstimate(flops=0, bytes_accessed=2 * moved, transcendentals=0),
        compiler_params=vmem((4 << 20) + 2 * moved + 8 * mine.size),
    )(mine, *weights)


def lay_kernel(*refs):
    *src_refs, x_ref, dy_ref = refs
    for i, src_ref in enumerate(src_refs):
        lay_out(src_ref, x_ref, dy_ref, i * (x_ref.shape[0] // len(src_refs)))


def lay(*blocks):
    places, tok_dev, row = blocks[0].shape
    rows = (len(blocks) * places * tok_dev, row // 2)
    return pl.pallas_call(
        lay_kernel,
        out_shape=(pltpu.VMEM(rows, jnp.bfloat16), pltpu.VMEM(rows, jnp.bfloat16)),
        in_specs=[VMEM] * len(blocks),
        out_specs=(VMEM,) * 2,
        cost_estimate=pl.CostEstimate(
            flops=0, bytes_accessed=8 * len(blocks) * blocks[0].size, transcendentals=0
        ),
        compiler_params=vmem((8 << 20) + 8 * len(blocks) * blocks[0].size),
    )(*blocks)


def my_core():
    return lax.axis_index("dp") % CORES


def row_blocks(rows, step):
    step(0, True)
    if rows > ROWS:
        pl.loop(1, rows // ROWS)(lambda block: step(block, False))


def half_total(gate_delta, up_delta, gate_ref, up_ref, core):
    columns = gate_ref.shape[0] // CORES
    part = pl.ds(pl.multiple_of(core * columns, columns), columns)
    total = lax.dot_general(
        gate_delta, gate_ref[part], CONTRACT_LAST, preferred_element_type=jnp.float32
    )
    return total + lax.dot_general(
        up_delta, up_ref[part], CONTRACT_LAST, preferred_element_type=jnp.float32
    )


def store_groups(ref, first, total):
    rows, columns = total.shape
    groups = columns // LANES
    for c in range(groups):
        ref[pl.ds(first + c, rows, stride=groups)] = total[:, c * LANES : (c + 1) * LANES]


def rows_kernel(*refs):
    along_y = sizes()[2]
    other_refs, refs = refs[: along_y - 1], refs[along_y - 1 :]
    my_x_ref, my_dy_ref, laid_x_ref, laid_dy_ref, gate_ref, up_ref, down_ref, *refs = refs
    sent_ref, x_ref, dy_ref, gate_delta_ref, up_delta_ref, hidden_ref, total_ref = refs
    size = my_x_ref.shape[0]
    x_ref[:size] = my_x_ref[...]
    dy_ref[:size] = my_dy_ref[...]
    for i in range(along_y):
        there = pl.ds(size if i == 0 else 2 * i * size, size)
        x_ref[there] = laid_x_ref[i * size : (i + 1) * size]
        dy_ref[there] = laid_dy_ref[i * size : (i + 1) * size]
    for i, other_ref in enumerate(other_refs):
        lay_out(other_ref, x_ref, dy_ref, (2 * i + 3) * size)

    def step(block, first):
        rows = pl.ds(pl.multiple_of(block * ROWS, ROWS), ROWS)
        x = x_ref[rows]
        pre_gate = jnp.dot(x, gate_ref[...], preferred_element_type=jnp.float32)
        pre_up = jnp.dot(x, up_ref[...], preferred_element_type=jnp.float32)
        sigmoid_gate = jax.nn.sigmoid(pre_gate)
        activated = pre_gate * sigmoid_gate
        slope = sigmoid_gate * (1.0 + pre_gate * (1.0 - sigmoid_gate))
        hidden_ref[rows] = (activated * pre_up).astype(jnp.bfloat16)
        grad_hidden = lax.dot_general(
            dy_ref[rows], down_ref[...], CONTRACT_LAST, preferred_element_type=jnp.float32
        )
        gate_delta = (grad_hidden * pre_up * slope).astype(jnp.bfloat16)
        up_delta = (grad_hidden * activated).astype(jnp.bfloat16)
        gate_delta_ref[rows] = gate_delta
        up_delta_ref[rows] = up_delta
        total = half_total(gate_delta, up_delta, gate_ref, up_ref, 1 - my_core())
        store_groups(total_ref, 0, total)
        size = total_ref.shape[0]
        part = pl.ds(pl.multiple_of(block * size, size), size)
        sent_ref[part] = total_ref[...].astype(jnp.bfloat16)

    row_blocks(x_ref.shape[0], step)


def rows_pass(others, my_x, my_dy, laid_x, laid_dy, gate, up, down):
    width, hidden = gate.shape
    rows = CORES * laid_x.shape[0]
    groups = width // CORES // LANES
    bf16 = functools.partial(jax.ShapeDtypeStruct, dtype=jnp.bfloat16)
    moved = rows * (6 * width + 3 * hidden) * 2
    return pl.pallas_call(
        rows_kernel,
        out_shape=(
            bf16((rows * groups, LANES)),
            bf16((rows, width)),
            bf16((rows, width)),
            bf16((rows, hidden)),
            bf16((rows, hidden)),
            bf16((rows, hidden)),
        ),
        in_specs=[VMEM] * (len(others) + 7),
        out_specs=(VMEM,) * 6,
        scratch_shapes=[pltpu.VMEM((ROWS * groups, LANES), jnp.float32)],
        cost_estimate=pl.CostEstimate(
            flops=8 * rows * width * hidden, bytes_accessed=moved, transcendentals=rows * hidden
        ),
        compiler_params=vmem((12 << 20) + 2 * moved),
    )(*others, my_x, my_dy, laid_x, laid_dy, gate, up, down)


def finish_kernel(gate_delta_ref, up_delta_ref, gate_ref, up_ref, total_ref):
    rows_all = gate_delta_ref.shape[0]
    size = total_ref.shape[0] // rows_all * ROWS

    def step(block, first):
        rows = pl.ds(pl.multiple_of(block * ROWS, ROWS), ROWS)
        total = half_total(
            gate_delta_ref[rows], up_delta_ref[rows], gate_ref, up_ref, my_core()
        )
        store_groups(total_ref, block * size, total)

    row_blocks(rows_all, step)


def finish(gate_delta, up_delta, gate, up):
    rows, hidden = gate_delta.shape
    columns = gate.shape[0] // CORES
    moved = 4 * columns * hidden + 4 * rows * (columns + hidden)
    return pl.pallas_call(
        finish_kernel,
        out_shape=jax.ShapeDtypeStruct((rows * columns // LANES, LANES), jnp.float32),
        in_specs=[VMEM] * 4,
        out_specs=VMEM,
        cost_estimate=pl.CostEstimate(
            flops=4 * rows * columns * hidden, bytes_accessed=moved, transcendentals=0
        ),
        compiler_params=vmem((16 << 20) + 2 * moved),
    )(gate_delta, up_delta, gate, up)


def share_kernel(total_ref, got_ref, shares_ref):
    devices, size, _ = shares_ref.shape
    experts, along_z, along_y, _ = sizes()
    places = experts * along_z
    y, core = my_y(), my_core()

    def step(row, carry):
        shift, half, place = row // (CORES * places), row // places % CORES, row % places
        got_row = row + (1 - 2 * half) * places
        here = pl.ds(pl.multiple_of(row * size, size), size)
        there = pl.ds(pl.multiple_of(got_row * size, size), size)
        expert, z = place_at(place)
        owner = order_of(expert, z, (y + shift) % along_y, (core + half) % CORES)
        total = total_ref[here] + got_ref[there].astype(jnp.float32)
        shares_ref[owner] = total.astype(jnp.bfloat16)
        return carry

    lax.fori_loop(0, devices, step, 0, unroll=devices <= 32)


def share(total, got, devices):
    size = total.shape[0] // devices
    return pl.pallas_call(
        share_kernel,
        out_shape=pltpu.VMEM((devices, size, LANES), jnp.bfloat16),
        in_specs=[VMEM] * 2,
        out_specs=VMEM,
        compiler_params=vmem((8 << 20) + 32 * total.size),
    )(total, got)


def sum_kernel(shares_ref, out_hbm, wide_ref, out_ref, sem):
    devices, size, _ = shares_ref.shape
    _, tok_dev, width = out_ref.shape
    groups = size // tok_dev
    for core in range(CORES):
        total = lax.fori_loop(
            0,
            devices // CORES,
            lambda i, acc: acc + shares_ref[i * CORES + core].astype(jnp.float32),
            jnp.zeros((size, LANES), jnp.float32),
            unroll=devices <= 32,
        )
        for row in range(size):
            token, lane = row // groups, (core * groups + row % groups) * LANES
            wide_ref[token : token + 1, lane : lane + LANES] = total[row : row + 1]
    out_ref[0] = wide_ref[...].astype(jnp.bfloat16)
    copy = pltpu.make_async_copy(out_ref, out_hbm, sem)
    copy.start()
    copy.wait()


def sum_shares(shares, tok_dev):
    _, size, _ = shares.shape
    width = CORES * size // tok_dev * LANES
    return pl.pallas_call(
        sum_kernel,
        out_shape=pltpu.HBM((1, tok_dev, width), jnp.bfloat16),
        in_specs=[VMEM],
        out_specs=HBM,
        scratch_shapes=[
            pltpu.VMEM((tok_dev, width), jnp.float32),
            pltpu.VMEM((1, tok_dev, width), jnp.bfloat16),
            pltpu.SemaphoreType.DMA,
        ],
        compiler_params=vmem(16 << 20),
    )(shares)


def local(tokens, out_grad, expert_ids, gate_scores, w_gate, w_up, w_down):
    experts, along_z, along_y, _ = sizes()
    places = experts * along_z
    devices = places * along_y * CORES
    groups = [
        [device_at(expert, z, y, core) for expert, z in map(place_at, range(places))]
        for y in range(along_y)
        for core in range(CORES)
    ]
    core_pairs = [(d, d ^ 1) for d in range(devices)]

    def from_y(shift):
        return [
            (device_at(e, z, (y + shift) % along_y, c), device_at(e, z, y, c))
            for e in range(experts)
            for z in range(along_z)
            for y in range(along_y)
            for c in range(CORES)
        ]

    copies = pack(tokens, out_grad, expert_ids, gate_scores, places)
    mine = lax.all_to_all(copies, BOTH, 0, 0, axis_index_groups=groups, tiled=True)
    beside = [lax.ppermute(mine, BOTH, from_y(shift)) for shift in range(1, along_y)]
    other = lax.ppermute(mine, BOTH, core_pairs)
    gate, up, down, my_x, my_dy = fetch(mine, w_gate, w_up, w_down)
    *beside, my_x = lax.optimization_barrier((*beside, my_x))
    others = [lax.ppermute(piece, BOTH, core_pairs) for piece in beside]
    laid_x, laid_dy = lay(other, *beside)
    sent, x, dy, gate_delta, up_delta, hidden = rows_pass(
        others, my_x, my_dy, laid_x, laid_dy, gate, up, down
    )
    got = lax.ppermute(sent, BOTH, core_pairs)
    total = finish(gate_delta, up_delta, gate, up)
    got, gate_delta, up_delta, hidden = lax.optimization_barrier(
        (got, gate_delta, up_delta, hidden)
    )
    shares = share(total, got, devices)
    everyone = [[order_at(place) for place in range(devices)]]
    shares = lax.all_to_all(shares, BOTH, 0, 0, axis_index_groups=everyone, tiled=True)
    token_grad = sum_shares(shares, tokens.shape[1])
    grad_down = jnp.dot(hidden.T, dy, preferred_element_type=jnp.float32)
    grad_gate = jnp.dot(x.T, gate_delta, preferred_element_type=jnp.float32)
    grad_up = jnp.dot(x.T, up_delta, preferred_element_type=jnp.float32)
    weight_grads = (grad_gate, grad_up, grad_down)
    return (token_grad,) + tuple(g.astype(jnp.bfloat16)[None] for g in weight_grads)


def solution(mesh):
    return jax.shard_map(
        local,
        mesh=mesh,
        in_specs=(
            P("dp", "expert", None),
            P("dp", "expert", None),
            P("dp", None, None),
            P("dp", None, None),
            P("expert", None, "dp"),
            P("expert", None, "dp"),
            P("expert", "dp", None),
        ),
        out_specs=(
            P("dp", "expert", None),
            P("expert", None, "dp"),
            P("expert", None, "dp"),
            P("expert", "dp", None),
        ),
        check_vma=False,
    )
```

```python
import functools

import jax
import jax.numpy as jnp
from jax import lax
from jax.experimental import pallas as pl
from jax.experimental.pallas import tpu as pltpu
from jax.sharding import PartitionSpec as P

LANES = 128
CORES = 2
BOTH = ("expert", "dp")
ROWS = 64
TILE = 16
CONTRACT_LAST = (((1,), (1,)), ((), ()))
PIECES = 4
VMEM = pl.BlockSpec(memory_space=pltpu.VMEM)
HBM = pl.BlockSpec(memory_space=pltpu.HBM)


def vmem(size):
    return pltpu.CompilerParams(vmem_limit_bytes=min(size, 36 << 20))


def sizes():
    dp = lax.axis_size("dp")
    along_y = 1
    while (2 * along_y) ** 2 <= dp // CORES:
        along_y *= 2
    return lax.axis_size("expert"), dp // CORES // along_y, along_y, CORES


def device_at(expert, z, y, core):
    _, along_z, along_y, _ = sizes()
    return ((expert * along_z + z) * along_y + y) * CORES + core


def z_at(step):
    upper = 1 - step % 2
    return sizes()[1] // 2 + upper * (step // 2) - (1 - upper) * (1 + step // 2)


def place_at(place):
    experts = sizes()[0]
    pair = place // 2
    return pair % experts, z_at(place % 2 + 2 * (pair // experts))


def order_at(place):
    experts, _, along_y, _ = sizes()
    place, core = place // CORES, place % CORES
    place, turn = place // 2, place % 2
    place, expert = place // experts, place % experts
    y = place % along_y
    y = y + turn * (along_y - 1 - 2 * y)
    return device_at(expert, z_at(turn + 2 * (place // along_y)), y, core)


def order_of(expert, z, y, core):
    experts, along_z, along_y, _ = sizes()
    upper = (z >= along_z // 2) * 1
    step = upper * (z - along_z // 2) + (1 - upper) * (along_z // 2 - 1 - z)
    y = y + (1 - upper) * (along_y - 1 - 2 * y)
    return (((step * along_y + y) * experts + expert) * 2 + 1 - upper) * CORES + core


def my_y():
    return lax.axis_index("dp") // CORES % sizes()[2]


def pack_kernel(
    tokens_hbm, grad_hbm, ids_hbm, scores_hbm, out_ref,
    tokens_ref, grad_ref, ids_ref, scores_ref, weighted_ref, sems,
):
    copies = [
        pltpu.make_async_copy(src, dst, sems.at[i])
        for i, (src, dst) in enumerate((
            (ids_hbm, ids_ref),
            (scores_hbm, scores_ref),
            (tokens_hbm, tokens_ref),
            (grad_hbm, grad_ref),
        ))
    ]
    for copy in copies:
        copy.start()
    for copy in copies[:2]:
        copy.wait()
    places, tok_dev, _ = out_ref.shape
    width = tokens_ref.shape[2]
    experts = lax.axis_size("expert")
    first = lax.axis_index("expert") * tok_dev
    ids = ids_ref[0]
    scores = scores_ref[0].astype(jnp.float32)
    token = lax.broadcasted_iota(jnp.int32, ids.shape, 1)
    lane = lax.broadcasted_iota(jnp.int32, (ids.shape[0], LANES), 1)
    row = lax.broadcasted_iota(jnp.int32, (tok_dev, LANES), 0)
    table = jnp.zeros((tok_dev, LANES), jnp.float32)
    for i in range(tok_dev):
        mine = token == first + i
        named = jnp.sum(jnp.where(mine, ids, 0), axis=1, keepdims=True)
        score = jnp.sum(jnp.where(mine, scores, 0.0), axis=1, keepdims=True)
        weights = jnp.sum(jnp.where(lane == named, score, 0.0), axis=0, keepdims=True)
        table = jnp.where(row == i, weights, table)
    for copy in copies[2:]:
        copy.wait()
    grad = grad_ref[0].astype(jnp.float32)
    for expert in range(experts):
        weighted_ref[expert] = (grad * table[:, expert : expert + 1]).astype(jnp.bfloat16)

    def write(place, carry):
        out_ref[place, :, :width] = tokens_ref[0]
        out_ref[place, :, width:] = weighted_ref[place_at(place)[0]]
        return carry

    lax.fori_loop(0, places, write, 0, unroll=places <= 16)


def pack(tokens, out_grad, expert_ids, gate_scores, places):
    _, tok_dev, width = tokens.shape
    operands = [
        pltpu.with_memory_space_constraint(a, pltpu.HBM)
        for a in (
            tokens, out_grad, jnp.swapaxes(expert_ids, 1, 2), jnp.swapaxes(gate_scores, 1, 2)
        )
    ]
    return pl.pallas_call(
        pack_kernel,
        out_shape=jax.ShapeDtypeStruct((places, tok_dev, 2 * width), jnp.bfloat16),
        in_specs=[HBM] * 4,
        out_specs=VMEM,
        scratch_shapes=[pltpu.VMEM(a.shape, a.dtype) for a in operands]
        + [
            pltpu.VMEM((lax.axis_size("expert"), tok_dev, width), jnp.bfloat16),
            pltpu.SemaphoreType.DMA((4,)),
        ],
        compiler_params=vmem(16 << 20),
    )(*operands)


def copy_pieces(src, dst, sems):
    rows = dst.shape[0] // PIECES
    parts = [pl.ds(piece * rows, rows) for piece in range(PIECES)]
    return [
        pltpu.make_async_copy(src.at[0, part], dst.at[part], sems.at[piece])
        for piece, part in enumerate(parts)
    ]


def lay_out(src_ref, x_ref, dy_ref, first):
    chips, tok_dev, _ = src_ref.shape
    width = x_ref.shape[1]
    per_tile = TILE // tok_dev

    def step(tile, carry):
        rows = pl.ds(pl.multiple_of(first + tile * TILE, TILE), TILE)
        blocks = [src_ref[tile * per_tile + j] for j in range(per_tile)]
        x_ref[rows] = jnp.concatenate([b[:, :width] for b in blocks], axis=0)
        dy_ref[rows] = jnp.concatenate([b[:, width:] for b in blocks], axis=0)
        return carry

    tiles = chips // per_tile
    lax.fori_loop(0, tiles, step, 0, unroll=tiles <= 2)


def fetch_kernel(
    mine_ref, gate_hbm, up_hbm, down_hbm, gate_ref, up_ref, down_ref, x_ref, dy_ref, sems
):
    copies = copy_pieces(gate_hbm, gate_ref, sems.at[0])
    copies += copy_pieces(up_hbm, up_ref, sems.at[1])
    copies += copy_pieces(down_hbm, down_ref, sems.at[2])
    for copy in copies:
        copy.start()
    lay_out(mine_ref, x_ref, dy_ref, 0)
    for copy in copies:
        copy.wait()


def fetch(mine, *weights):
    places, tok_dev, row = mine.shape
    rows = (places * tok_dev, row // 2)
    moved = sum(2 * w.size for w in weights)
    weights = [pltpu.with_memory_space_constraint(w, pltpu.HBM) for w in weights]
    return pl.pallas_call(
        fetch_kernel,
        out_shape=tuple(pltpu.VMEM(w.shape[1:], w.dtype) for w in weights)
        + (pltpu.VMEM(rows, jnp.bfloat16), pltpu.VMEM(rows, jnp.bfloat16)),
        in_specs=[VMEM] + [HBM] * 3,
        out_specs=(VMEM,) * 5,
        scratch_shapes=[pltpu.SemaphoreType.DMA((3, PIECES))],
        cost_estimate=pl.CostEstimate(flops=0, bytes_accessed=2 * moved, transcendentals=0),
        compiler_params=vmem((4 << 20) + 2 * moved + 8 * mine.size),
    )(mine, *weights)


def lay_kernel(*refs):
    *src_refs, x_ref, dy_ref = refs
    for i, src_ref in enumerate(src_refs):
        lay_out(src_ref, x_ref, dy_ref, i * (x_ref.shape[0] // len(src_refs)))


def lay(*blocks):
    places, tok_dev, row = blocks[0].shape
    rows = (len(blocks) * places * tok_dev, row // 2)
    return pl.pallas_call(
        lay_kernel,
        out_shape=(pltpu.VMEM(rows, jnp.bfloat16), pltpu.VMEM(rows, jnp.bfloat16)),
        in_specs=[VMEM] * len(blocks),
        out_specs=(VMEM,) * 2,
        cost_estimate=pl.CostEstimate(
            flops=0, bytes_accessed=8 * len(blocks) * blocks[0].size, transcendentals=0
        ),
        compiler_params=vmem((8 << 20) + 8 * len(blocks) * blocks[0].size),
    )(*blocks)


def my_core():
    return lax.axis_index("dp") % CORES


def row_blocks(rows, step):
    step(0, True)
    if rows > ROWS:
        pl.loop(1, rows // ROWS)(lambda block: step(block, False))


def half_total(gate_delta, up_delta, gate_ref, up_ref, core):
    columns = gate_ref.shape[0] // CORES
    part = pl.ds(pl.multiple_of(core * columns, columns), columns)
    total = lax.dot_general(
        gate_delta, gate_ref[part], CONTRACT_LAST, preferred_element_type=jnp.float32
    )
    return total + lax.dot_general(
        up_delta, up_ref[part], CONTRACT_LAST, preferred_element_type=jnp.float32
    )


def store_groups(ref, first, total):
    rows, columns = total.shape
    groups = columns // LANES
    for c in range(groups):
        ref[pl.ds(first + c, rows, stride=groups)] = total[:, c * LANES : (c + 1) * LANES]


def rows_kernel(*refs):
    along_y = sizes()[2]
    other_refs, refs = refs[: along_y - 1], refs[along_y - 1 :]
    my_x_ref, my_dy_ref, laid_x_ref, laid_dy_ref, gate_ref, up_ref, down_ref, *refs = refs
    sent_ref, x_ref, dy_ref, gate_delta_ref, up_delta_ref, hidden_ref, total_ref = refs
    size = my_x_ref.shape[0]
    one_block = x_ref.shape[0] == ROWS and along_y == CORES and size == TILE
    if one_block:
        width = x_ref.shape[1]
        last = jnp.concatenate([other_refs[0][j] for j in range(other_refs[0].shape[0])], axis=0)
        all_x = jnp.concatenate([my_x_ref[...], laid_x_ref[...], last[:, :width]], axis=0)
        all_dy = jnp.concatenate([my_dy_ref[...], laid_dy_ref[...], last[:, width:]], axis=0)
        x_ref[...] = all_x
        dy_ref[...] = all_dy
    else:
        x_ref[:size] = my_x_ref[...]
        dy_ref[:size] = my_dy_ref[...]
    for i in range(0 if one_block else along_y):
        there = pl.ds(size if i == 0 else 2 * i * size, size)
        x_ref[there] = laid_x_ref[i * size : (i + 1) * size]
        dy_ref[there] = laid_dy_ref[i * size : (i + 1) * size]
    for i, other_ref in enumerate(() if one_block else other_refs):
        lay_out(other_ref, x_ref, dy_ref, (2 * i + 3) * size)

    def step(block, first):
        rows = pl.ds(pl.multiple_of(block * ROWS, ROWS), ROWS)
        x, dy = (all_x, all_dy) if one_block else (x_ref[rows], dy_ref[rows])
        pre_gate = jnp.dot(x, gate_ref[...], preferred_element_type=jnp.float32)
        pre_up = jnp.dot(x, up_ref[...], preferred_element_type=jnp.float32)
        sigmoid_gate = jax.nn.sigmoid(pre_gate)
        activated = pre_gate * sigmoid_gate
        slope = sigmoid_gate * (1.0 + pre_gate * (1.0 - sigmoid_gate))
        hidden_ref[rows] = (activated * pre_up).astype(jnp.bfloat16)
        grad_hidden = lax.dot_general(
            dy, down_ref[...], CONTRACT_LAST, preferred_element_type=jnp.float32
        )
        gate_delta = (grad_hidden * pre_up * slope).astype(jnp.bfloat16)
        up_delta = (grad_hidden * activated).astype(jnp.bfloat16)
        gate_delta_ref[rows] = gate_delta
        up_delta_ref[rows] = up_delta
        total = half_total(gate_delta, up_delta, gate_ref, up_ref, 1 - my_core())
        store_groups(total_ref, 0, total)
        size = total_ref.shape[0]
        part = pl.ds(pl.multiple_of(block * size, size), size)
        sent_ref[part] = total_ref[...].astype(jnp.bfloat16)

    row_blocks(x_ref.shape[0], step)


def rows_pass(others, my_x, my_dy, laid_x, laid_dy, gate, up, down):
    width, hidden = gate.shape
    rows = CORES * laid_x.shape[0]
    groups = width // CORES // LANES
    bf16 = functools.partial(jax.ShapeDtypeStruct, dtype=jnp.bfloat16)
    moved = rows * (6 * width + 3 * hidden) * 2
    return pl.pallas_call(
        rows_kernel,
        out_shape=(
            bf16((rows * groups, LANES)),
            bf16((rows, width)),
            bf16((rows, width)),
            bf16((rows, hidden)),
            bf16((rows, hidden)),
            bf16((rows, hidden)),
        ),
        in_specs=[VMEM] * (len(others) + 7),
        out_specs=(VMEM,) * 6,
        scratch_shapes=[pltpu.VMEM((ROWS * groups, LANES), jnp.float32)],
        cost_estimate=pl.CostEstimate(
            flops=8 * rows * width * hidden, bytes_accessed=moved, transcendentals=rows * hidden
        ),
        compiler_params=vmem((12 << 20) + 2 * moved),
    )(*others, my_x, my_dy, laid_x, laid_dy, gate, up, down)


def finish_kernel(gate_delta_ref, up_delta_ref, gate_ref, up_ref, total_ref):
    rows_all = gate_delta_ref.shape[0]
    size = total_ref.shape[0] // rows_all * ROWS

    def step(block, first):
        rows = pl.ds(pl.multiple_of(block * ROWS, ROWS), ROWS)
        total = half_total(
            gate_delta_ref[rows], up_delta_ref[rows], gate_ref, up_ref, my_core()
        )
        store_groups(total_ref, block * size, total)

    row_blocks(rows_all, step)


def finish(gate_delta, up_delta, gate, up):
    rows, hidden = gate_delta.shape
    columns = gate.shape[0] // CORES
    moved = 4 * columns * hidden + 4 * rows * (columns + hidden)
    return pl.pallas_call(
        finish_kernel,
        out_shape=jax.ShapeDtypeStruct((rows * columns // LANES, LANES), jnp.float32),
        in_specs=[VMEM] * 4,
        out_specs=VMEM,
        cost_estimate=pl.CostEstimate(
            flops=4 * rows * columns * hidden, bytes_accessed=moved, transcendentals=0
        ),
        compiler_params=vmem((16 << 20) + 2 * moved),
    )(gate_delta, up_delta, gate, up)


def share_kernel(total_ref, got_ref, shares_ref):
    devices, size, _ = shares_ref.shape
    experts, along_z, along_y, _ = sizes()
    places = experts * along_z
    y, core = my_y(), my_core()

    def step(row, carry):
        shift, half, place = row // (CORES * places), row // places % CORES, row % places
        got_row = row + (1 - 2 * half) * places
        here = pl.ds(pl.multiple_of(row * size, size), size)
        there = pl.ds(pl.multiple_of(got_row * size, size), size)
        expert, z = place_at(place)
        owner = order_of(expert, z, (y + shift) % along_y, (core + half) % CORES)
        total = total_ref[here] + got_ref[there].astype(jnp.float32)
        shares_ref[owner] = total.astype(jnp.bfloat16)
        return carry

    lax.fori_loop(0, devices, step, 0, unroll=devices <= 32)


def share(total, got, devices):
    size = total.shape[0] // devices
    return pl.pallas_call(
        share_kernel,
        out_shape=pltpu.VMEM((devices, size, LANES), jnp.bfloat16),
        in_specs=[VMEM] * 2,
        out_specs=VMEM,
        compiler_params=vmem((8 << 20) + 32 * total.size),
    )(total, got)


def sum_kernel(shares_ref, out_hbm, wide_ref, out_ref, sems):
    devices, size, _ = shares_ref.shape
    _, tok_dev, width = out_ref.shape
    groups = size // tok_dev
    copies = []
    for core in range(CORES):
        total = lax.fori_loop(
            0,
            devices // CORES,
            lambda i, acc: acc + shares_ref[i * CORES + core].astype(jnp.float32),
            jnp.zeros((size, LANES), jnp.float32),
            unroll=devices <= 32,
        )
        for row in range(size):
            token, lane = row // groups, (core * groups + row % groups) * LANES
            wide_ref[token : token + 1, lane : lane + LANES] = total[row : row + 1]
        half = pl.ds(core * groups * LANES, groups * LANES)
        out_ref[0, :, half] = wide_ref[:, half].astype(jnp.bfloat16)
        copies.append(
            pltpu.make_async_copy(out_ref.at[:, :, half], out_hbm.at[:, :, half], sems.at[core])
        )
        copies[-1].start()
    for copy in copies:
        copy.wait()


def sum_shares(shares, tok_dev):
    _, size, _ = shares.shape
    width = CORES * size // tok_dev * LANES
    return pl.pallas_call(
        sum_kernel,
        out_shape=pltpu.HBM((1, tok_dev, width), jnp.bfloat16),
        in_specs=[VMEM],
        out_specs=HBM,
        scratch_shapes=[
            pltpu.VMEM((tok_dev, width), jnp.float32),
            pltpu.VMEM((1, tok_dev, width), jnp.bfloat16),
            pltpu.SemaphoreType.DMA((CORES,)),
        ],
        compiler_params=vmem(16 << 20),
    )(shares)


def local(tokens, out_grad, expert_ids, gate_scores, w_gate, w_up, w_down):
    experts, along_z, along_y, _ = sizes()
    places = experts * along_z
    devices = places * along_y * CORES
    groups = [
        [device_at(expert, z, y, core) for expert, z in map(place_at, range(places))]
        for y in range(along_y)
        for core in range(CORES)
    ]
    core_pairs = [(d, d ^ 1) for d in range(devices)]

    def from_y(shift):
        return [
            (device_at(e, z, (y + shift) % along_y, c), device_at(e, z, y, c))
            for e in range(experts)
            for z in range(along_z)
            for y in range(along_y)
            for c in range(CORES)
        ]

    copies = pack(tokens, out_grad, expert_ids, gate_scores, places)
    mine = lax.all_to_all(copies, BOTH, 0, 0, axis_index_groups=groups, tiled=True)
    beside = [lax.ppermute(mine, BOTH, from_y(shift)) for shift in range(1, along_y)]
    other = lax.ppermute(mine, BOTH, core_pairs)
    gate, up, down, my_x, my_dy = fetch(mine, w_gate, w_up, w_down)
    *beside, my_x = lax.optimization_barrier((*beside, my_x))
    others = [lax.ppermute(piece, BOTH, core_pairs) for piece in beside]
    laid_x, laid_dy = lay(other, *beside)
    sent, x, dy, gate_delta, up_delta, hidden = rows_pass(
        others, my_x, my_dy, laid_x, laid_dy, gate, up, down
    )
    got = lax.ppermute(sent, BOTH, core_pairs)
    total = finish(gate_delta, up_delta, gate, up)
    got, gate_delta, up_delta, hidden = lax.optimization_barrier(
        (got, gate_delta, up_delta, hidden)
    )
    shares = share(total, got, devices)
    everyone = [[order_at(place) for place in range(devices)]]
    shares = lax.all_to_all(shares, BOTH, 0, 0, axis_index_groups=everyone, tiled=True)
    token_grad = sum_shares(shares, tokens.shape[1])
    grad_down = jnp.dot(hidden.T, dy, preferred_element_type=jnp.float32)
    grad_gate = jnp.dot(x.T, gate_delta, preferred_element_type=jnp.float32)
    grad_up = jnp.dot(x.T, up_delta, preferred_element_type=jnp.float32)
    weight_grads = (grad_gate, grad_up, grad_down)
    return (token_grad,) + tuple(g.astype(jnp.bfloat16)[None] for g in weight_grads)


def solution(mesh):
    return jax.shard_map(
        local,
        mesh=mesh,
        in_specs=(
            P("dp", "expert", None),
            P("dp", "expert", None),
            P("dp", None, None),
            P("dp", None, None),
            P("expert", None, "dp"),
            P("expert", None, "dp"),
            P("expert", "dp", None),
        ),
        out_specs=(
            P("dp", "expert", None),
            P("expert", None, "dp"),
            P("expert", None, "dp"),
            P("expert", "dp", None),
        ),
        check_vma=False,
    )
```

```python
import functools

import jax
import jax.numpy as jnp
from jax import lax
from jax.experimental import pallas as pl
from jax.experimental.pallas import tpu as pltpu
from jax.sharding import PartitionSpec as P

LANES = 128
CORES = 2
BOTH = ("expert", "dp")
ROWS = 64
TILE = 16
CONTRACT_LAST = (((1,), (1,)), ((), ()))
PIECES = 4
VMEM = pl.BlockSpec(memory_space=pltpu.VMEM)
HBM = pl.BlockSpec(memory_space=pltpu.HBM)


def vmem(size):
    return pltpu.CompilerParams(vmem_limit_bytes=min(size, 36 << 20))


def sizes():
    dp = lax.axis_size("dp")
    along_y = 1
    while (2 * along_y) ** 2 <= dp // CORES:
        along_y *= 2
    return lax.axis_size("expert"), dp // CORES // along_y, along_y, CORES


def device_at(expert, z, y, core):
    _, along_z, along_y, _ = sizes()
    return ((expert * along_z + z) * along_y + y) * CORES + core


def z_at(step):
    upper = 1 - step % 2
    return sizes()[1] // 2 + upper * (step // 2) - (1 - upper) * (1 + step // 2)


def place_at(place):
    experts = sizes()[0]
    pair = place // 2
    return pair % experts, z_at(place % 2 + 2 * (pair // experts))


def order_at(place):
    experts, _, along_y, _ = sizes()
    place, core = place // CORES, place % CORES
    place, turn = place // 2, place % 2
    place, expert = place // experts, place % experts
    y = place % along_y
    y = y + turn * (along_y - 1 - 2 * y)
    return device_at(expert, z_at(turn + 2 * (place // along_y)), y, core)


def order_of(expert, z, y, core):
    experts, along_z, along_y, _ = sizes()
    upper = (z >= along_z // 2) * 1
    step = upper * (z - along_z // 2) + (1 - upper) * (along_z // 2 - 1 - z)
    y = y + (1 - upper) * (along_y - 1 - 2 * y)
    return (((step * along_y + y) * experts + expert) * 2 + 1 - upper) * CORES + core


def my_y():
    return lax.axis_index("dp") // CORES % sizes()[2]


def pack_kernel(
    tokens_hbm, grad_hbm, ids_hbm, scores_hbm, out_ref,
    tokens_ref, grad_ref, ids_ref, scores_ref, weighted_ref, sems,
):
    copies = [
        pltpu.make_async_copy(src, dst, sems.at[i])
        for i, (src, dst) in enumerate((
            (ids_hbm, ids_ref),
            (scores_hbm, scores_ref),
            (tokens_hbm, tokens_ref),
            (grad_hbm, grad_ref),
        ))
    ]
    for copy in copies:
        copy.start()
    for copy in copies[:2]:
        copy.wait()
    places, tok_dev, _ = out_ref.shape
    width = tokens_ref.shape[2]
    experts = lax.axis_size("expert")
    first = lax.axis_index("expert") * tok_dev
    ids = ids_ref[0]
    scores = scores_ref[0].astype(jnp.float32)
    token = lax.broadcasted_iota(jnp.int32, ids.shape, 1)
    lane = lax.broadcasted_iota(jnp.int32, (ids.shape[0], LANES), 1)
    row = lax.broadcasted_iota(jnp.int32, (tok_dev, LANES), 0)
    table = jnp.zeros((tok_dev, LANES), jnp.float32)
    for i in range(tok_dev):
        mine = token == first + i
        named = jnp.sum(jnp.where(mine, ids, 0), axis=1, keepdims=True)
        score = jnp.sum(jnp.where(mine, scores, 0.0), axis=1, keepdims=True)
        weights = jnp.sum(jnp.where(lane == named, score, 0.0), axis=0, keepdims=True)
        table = jnp.where(row == i, weights, table)
    copies[2].wait()

    def write_tokens(place, carry):
        out_ref[place, :, :width] = tokens_ref[0]
        return carry

    def write_grads(place, carry):
        out_ref[place, :, width:] = weighted_ref[place_at(place)[0]]
        return carry

    lax.fori_loop(0, places, write_tokens, 0, unroll=places <= 16)
    copies[3].wait()
    grad = grad_ref[0].astype(jnp.float32)
    for expert in range(experts):
        weighted_ref[expert] = (grad * table[:, expert : expert + 1]).astype(jnp.bfloat16)
    lax.fori_loop(0, places, write_grads, 0, unroll=places <= 16)


def pack(tokens, out_grad, expert_ids, gate_scores, places):
    _, tok_dev, width = tokens.shape
    operands = [
        pltpu.with_memory_space_constraint(a, pltpu.HBM)
        for a in (
            tokens, out_grad, jnp.swapaxes(expert_ids, 1, 2), jnp.swapaxes(gate_scores, 1, 2)
        )
    ]
    return pl.pallas_call(
        pack_kernel,
        out_shape=jax.ShapeDtypeStruct((places, tok_dev, 2 * width), jnp.bfloat16),
        in_specs=[HBM] * 4,
        out_specs=VMEM,
        scratch_shapes=[pltpu.VMEM(a.shape, a.dtype) for a in operands]
        + [
            pltpu.VMEM((lax.axis_size("expert"), tok_dev, width), jnp.bfloat16),
            pltpu.SemaphoreType.DMA((4,)),
        ],
        compiler_params=vmem(16 << 20),
    )(*operands)


def copy_pieces(src, dst, sems):
    rows = dst.shape[0] // PIECES
    parts = [pl.ds(piece * rows, rows) for piece in range(PIECES)]
    return [
        pltpu.make_async_copy(src.at[0, part], dst.at[part], sems.at[piece])
        for piece, part in enumerate(parts)
    ]


def lay_out(src_ref, x_ref, dy_ref, first):
    chips, tok_dev, _ = src_ref.shape
    width = x_ref.shape[1]
    per_tile = TILE // tok_dev

    def step(tile, carry):
        rows = pl.ds(pl.multiple_of(first + tile * TILE, TILE), TILE)
        blocks = [src_ref[tile * per_tile + j] for j in range(per_tile)]
        x_ref[rows] = jnp.concatenate([b[:, :width] for b in blocks], axis=0)
        dy_ref[rows] = jnp.concatenate([b[:, width:] for b in blocks], axis=0)
        return carry

    tiles = chips // per_tile
    lax.fori_loop(0, tiles, step, 0, unroll=tiles <= 2)


def fetch_kernel(
    mine_ref, gate_hbm, up_hbm, down_hbm, gate_ref, up_ref, down_ref, x_ref, dy_ref, sems
):
    copies = copy_pieces(gate_hbm, gate_ref, sems.at[0])
    copies += copy_pieces(up_hbm, up_ref, sems.at[1])
    copies += copy_pieces(down_hbm, down_ref, sems.at[2])
    for copy in copies:
        copy.start()
    lay_out(mine_ref, x_ref, dy_ref, 0)
    for copy in copies:
        copy.wait()


def fetch(mine, *weights):
    places, tok_dev, row = mine.shape
    rows = (places * tok_dev, row // 2)
    moved = sum(2 * w.size for w in weights)
    weights = [pltpu.with_memory_space_constraint(w, pltpu.HBM) for w in weights]
    return pl.pallas_call(
        fetch_kernel,
        out_shape=tuple(pltpu.VMEM(w.shape[1:], w.dtype) for w in weights)
        + (pltpu.VMEM(rows, jnp.bfloat16), pltpu.VMEM(rows, jnp.bfloat16)),
        in_specs=[VMEM] + [HBM] * 3,
        out_specs=(VMEM,) * 5,
        scratch_shapes=[pltpu.SemaphoreType.DMA((3, PIECES))],
        cost_estimate=pl.CostEstimate(flops=0, bytes_accessed=2 * moved, transcendentals=0),
        compiler_params=vmem((4 << 20) + 2 * moved + 8 * mine.size),
    )(mine, *weights)


def lay_kernel(*refs):
    *src_refs, x_ref, dy_ref = refs
    for i, src_ref in enumerate(src_refs):
        lay_out(src_ref, x_ref, dy_ref, i * (x_ref.shape[0] // len(src_refs)))


def lay(*blocks):
    places, tok_dev, row = blocks[0].shape
    rows = (len(blocks) * places * tok_dev, row // 2)
    return pl.pallas_call(
        lay_kernel,
        out_shape=(pltpu.VMEM(rows, jnp.bfloat16), pltpu.VMEM(rows, jnp.bfloat16)),
        in_specs=[VMEM] * len(blocks),
        out_specs=(VMEM,) * 2,
        cost_estimate=pl.CostEstimate(
            flops=0, bytes_accessed=8 * len(blocks) * blocks[0].size, transcendentals=0
        ),
        compiler_params=vmem((8 << 20) + 8 * len(blocks) * blocks[0].size),
    )(*blocks)


def my_core():
    return lax.axis_index("dp") % CORES


def row_blocks(rows, step):
    step(0, True)
    if rows > ROWS:
        pl.loop(1, rows // ROWS)(lambda block: step(block, False))


def half_total(gate_delta, up_delta, gate_ref, up_ref, core):
    columns = gate_ref.shape[0] // CORES
    part = pl.ds(pl.multiple_of(core * columns, columns), columns)
    total = lax.dot_general(
        gate_delta, gate_ref[part], CONTRACT_LAST, preferred_element_type=jnp.float32
    )
    return total + lax.dot_general(
        up_delta, up_ref[part], CONTRACT_LAST, preferred_element_type=jnp.float32
    )


def store_groups(ref, first, total):
    rows, columns = total.shape
    groups = columns // LANES
    for c in range(groups):
        ref[pl.ds(first + c, rows, stride=groups)] = total[:, c * LANES : (c + 1) * LANES]


def rows_kernel(*refs):
    along_y = sizes()[2]
    other_refs, refs = refs[: along_y - 1], refs[along_y - 1 :]
    my_x_ref, my_dy_ref, laid_x_ref, laid_dy_ref, gate_ref, up_ref, down_ref, *refs = refs
    sent_ref, x_ref, dy_ref, gate_delta_ref, up_delta_ref, hidden_ref, total_ref = refs
    size = my_x_ref.shape[0]
    x_ref[:size] = my_x_ref[...]
    dy_ref[:size] = my_dy_ref[...]
    for i in range(along_y):
        there = pl.ds(size if i == 0 else 2 * i * size, size)
        x_ref[there] = laid_x_ref[i * size : (i + 1) * size]
        dy_ref[there] = laid_dy_ref[i * size : (i + 1) * size]
    for i, other_ref in enumerate(other_refs):
        lay_out(other_ref, x_ref, dy_ref, (2 * i + 3) * size)

    def step(block, first):
        rows = pl.ds(pl.multiple_of(block * ROWS, ROWS), ROWS)
        x = x_ref[rows]
        pre_gate = jnp.dot(x, gate_ref[...], preferred_element_type=jnp.float32)
        pre_up = jnp.dot(x, up_ref[...], preferred_element_type=jnp.float32)
        sigmoid_gate = jax.nn.sigmoid(pre_gate)
        activated = pre_gate * sigmoid_gate
        slope = sigmoid_gate * (1.0 + pre_gate * (1.0 - sigmoid_gate))
        hidden_ref[rows] = (activated * pre_up).astype(jnp.bfloat16)
        grad_hidden = lax.dot_general(
            dy_ref[rows], down_ref[...], CONTRACT_LAST, preferred_element_type=jnp.float32
        )
        gate_delta = (grad_hidden * pre_up * slope).astype(jnp.bfloat16)
        up_delta = (grad_hidden * activated).astype(jnp.bfloat16)
        gate_delta_ref[rows] = gate_delta
        up_delta_ref[rows] = up_delta
        total = half_total(gate_delta, up_delta, gate_ref, up_ref, 1 - my_core())
        store_groups(total_ref, 0, total)
        size = total_ref.shape[0]
        part = pl.ds(pl.multiple_of(block * size, size), size)
        sent_ref[part] = total_ref[...].astype(jnp.bfloat16)

    row_blocks(x_ref.shape[0], step)


def rows_pass(others, my_x, my_dy, laid_x, laid_dy, gate, up, down):
    width, hidden = gate.shape
    rows = CORES * laid_x.shape[0]
    groups = width // CORES // LANES
    bf16 = functools.partial(jax.ShapeDtypeStruct, dtype=jnp.bfloat16)
    moved = rows * (6 * width + 3 * hidden) * 2
    return pl.pallas_call(
        rows_kernel,
        out_shape=(
            bf16((rows * groups, LANES)),
            bf16((rows, width)),
            bf16((rows, width)),
            bf16((rows, hidden)),
            bf16((rows, hidden)),
            bf16((rows, hidden)),
        ),
        in_specs=[VMEM] * (len(others) + 7),
        out_specs=(VMEM,) * 6,
        scratch_shapes=[pltpu.VMEM((ROWS * groups, LANES), jnp.float32)],
        cost_estimate=pl.CostEstimate(
            flops=8 * rows * width * hidden, bytes_accessed=moved, transcendentals=rows * hidden
        ),
        compiler_params=vmem((12 << 20) + 2 * moved),
    )(*others, my_x, my_dy, laid_x, laid_dy, gate, up, down)


def finish_kernel(gate_delta_ref, up_delta_ref, gate_ref, up_ref, total_ref):
    rows_all = gate_delta_ref.shape[0]
    size = total_ref.shape[0] // rows_all * ROWS

    def step(block, first):
        rows = pl.ds(pl.multiple_of(block * ROWS, ROWS), ROWS)
        total = half_total(
            gate_delta_ref[rows], up_delta_ref[rows], gate_ref, up_ref, my_core()
        )
        store_groups(total_ref, block * size, total)

    row_blocks(rows_all, step)


def finish(gate_delta, up_delta, gate, up):
    rows, hidden = gate_delta.shape
    columns = gate.shape[0] // CORES
    moved = 4 * columns * hidden + 4 * rows * (columns + hidden)
    return pl.pallas_call(
        finish_kernel,
        out_shape=jax.ShapeDtypeStruct((rows * columns // LANES, LANES), jnp.float32),
        in_specs=[VMEM] * 4,
        out_specs=VMEM,
        cost_estimate=pl.CostEstimate(
            flops=4 * rows * columns * hidden, bytes_accessed=moved, transcendentals=0
        ),
        compiler_params=vmem((16 << 20) + 2 * moved),
    )(gate_delta, up_delta, gate, up)


def share_kernel(total_ref, got_ref, shares_ref):
    devices, size, _ = shares_ref.shape
    experts, along_z, along_y, _ = sizes()
    places = experts * along_z
    y, core = my_y(), my_core()

    def step(row, carry):
        shift, half, place = row // (CORES * places), row // places % CORES, row % places
        got_row = row + (1 - 2 * half) * places
        here = pl.ds(pl.multiple_of(row * size, size), size)
        there = pl.ds(pl.multiple_of(got_row * size, size), size)
        expert, z = place_at(place)
        owner = order_of(expert, z, (y + shift) % along_y, (core + half) % CORES)
        total = total_ref[here] + got_ref[there].astype(jnp.float32)
        shares_ref[owner] = total.astype(jnp.bfloat16)
        return carry

    lax.fori_loop(0, devices, step, 0, unroll=devices <= 32)


def share(total, got, devices):
    size = total.shape[0] // devices
    return pl.pallas_call(
        share_kernel,
        out_shape=pltpu.VMEM((devices, size, LANES), jnp.bfloat16),
        in_specs=[VMEM] * 2,
        out_specs=VMEM,
        compiler_params=vmem((8 << 20) + 32 * total.size),
    )(total, got)


def sum_kernel(shares_ref, out_hbm, wide_ref, out_ref, sem):
    devices, size, _ = shares_ref.shape
    _, tok_dev, width = out_ref.shape
    groups = size // tok_dev
    for core in range(CORES):
        total = lax.fori_loop(
            0,
            devices // CORES,
            lambda i, acc: acc + shares_ref[i * CORES + core].astype(jnp.float32),
            jnp.zeros((size, LANES), jnp.float32),
            unroll=devices <= 32,
        )
        for row in range(size):
            token, lane = row // groups, (core * groups + row % groups) * LANES
            wide_ref[token : token + 1, lane : lane + LANES] = total[row : row + 1]
    out_ref[0] = wide_ref[...].astype(jnp.bfloat16)
    copy = pltpu.make_async_copy(out_ref, out_hbm, sem)
    copy.start()
    copy.wait()


def sum_shares(shares, tok_dev):
    _, size, _ = shares.shape
    width = CORES * size // tok_dev * LANES
    return pl.pallas_call(
        sum_kernel,
        out_shape=pltpu.HBM((1, tok_dev, width), jnp.bfloat16),
        in_specs=[VMEM],
        out_specs=HBM,
        scratch_shapes=[
            pltpu.VMEM((tok_dev, width), jnp.float32),
            pltpu.VMEM((1, tok_dev, width), jnp.bfloat16),
            pltpu.SemaphoreType.DMA,
        ],
        compiler_params=vmem(16 << 20),
    )(shares)


def local(tokens, out_grad, expert_ids, gate_scores, w_gate, w_up, w_down):
    experts, along_z, along_y, _ = sizes()
    places = experts * along_z
    devices = places * along_y * CORES
    groups = [
        [device_at(expert, z, y, core) for expert, z in map(place_at, range(places))]
        for y in range(along_y)
        for core in range(CORES)
    ]
    core_pairs = [(d, d ^ 1) for d in range(devices)]

    def from_y(shift):
        return [
            (device_at(e, z, (y + shift) % along_y, c), device_at(e, z, y, c))
            for e in range(experts)
            for z in range(along_z)
            for y in range(along_y)
            for c in range(CORES)
        ]

    copies = pack(tokens, out_grad, expert_ids, gate_scores, places)
    mine = lax.all_to_all(copies, BOTH, 0, 0, axis_index_groups=groups, tiled=True)
    beside = [lax.ppermute(mine, BOTH, from_y(shift)) for shift in range(1, along_y)]
    other = lax.ppermute(mine, BOTH, core_pairs)
    gate, up, down, my_x, my_dy = fetch(mine, w_gate, w_up, w_down)
    *beside, my_x = lax.optimization_barrier((*beside, my_x))
    others = [lax.ppermute(piece, BOTH, core_pairs) for piece in beside]
    laid_x, laid_dy = lay(other, *beside)
    sent, x, dy, gate_delta, up_delta, hidden = rows_pass(
        others, my_x, my_dy, laid_x, laid_dy, gate, up, down
    )
    got = lax.ppermute(sent, BOTH, core_pairs)
    total = finish(gate_delta, up_delta, gate, up)
    got, gate_delta, up_delta, hidden = lax.optimization_barrier(
        (got, gate_delta, up_delta, hidden)
    )
    shares = share(total, got, devices)
    everyone = [[order_at(place) for place in range(devices)]]
    shares = lax.all_to_all(shares, BOTH, 0, 0, axis_index_groups=everyone, tiled=True)
    token_grad = sum_shares(shares, tokens.shape[1])
    grad_down = jnp.dot(hidden.T, dy, preferred_element_type=jnp.float32)
    grad_gate = jnp.dot(x.T, gate_delta, preferred_element_type=jnp.float32)
    grad_up = jnp.dot(x.T, up_delta, preferred_element_type=jnp.float32)
    weight_grads = (grad_gate, grad_up, grad_down)
    return (token_grad,) + tuple(g.astype(jnp.bfloat16)[None] for g in weight_grads)


def solution(mesh):
    return jax.shard_map(
        local,
        mesh=mesh,
        in_specs=(
            P("dp", "expert", None),
            P("dp", "expert", None),
            P("dp", None, None),
            P("dp", None, None),
            P("expert", None, "dp"),
            P("expert", None, "dp"),
            P("expert", "dp", None),
        ),
        out_specs=(
            P("dp", "expert", None),
            P("expert", None, "dp"),
            P("expert", None, "dp"),
            P("expert", "dp", None),
        ),
        check_vma=False,
    )
```
